32 devices in a mesh: dp: 4 (over y, x), ctx: 2 (over core), tp: 4 (over z).
Axes of the slice: x: 2, y: 2, z: 4, core: 2. Of those that a mesh axis runs over, the one named last changes fastest.
Arguments:
- inputs: bfloat16 [4, 16, 256, 1152], P('dp', 'ctx', 'tp'), may hold values from -7 to 7
- conditioning: float32 [4, 1152], P('dp'), may hold values from -7 to 7
- qkv_weight: float32 [2, 1152, 3, 1152], P(None, 'dp', None, 'tp'), may hold values from -2 to 2
- out_weight: float32 [2, 1152, 1152], P(None, 'tp', 'dp'), may hold values from -5 to 5
- up_weight: float32 [2, 1152, 4608], P(None, 'dp', 'tp'), may hold values from -2 to 2
- down_weight: float32 [2, 4608, 1152], P(None, 'tp', 'dp'), may hold values from -2 to 2
- mod_weight: float32 [2, 1152, 6, 1152], P(None, 'dp', None, 'tp'), may hold values from -0.1875 to 0.1875
- qkv_first: float32 [2, 1152, 3, 1152], P(None, 'dp', None, 'tp'), may hold values from -1 to 1
- out_first: float32 [2, 1152, 1152], P(None, 'tp', 'dp'), may hold values from -1 to 1
- up_first: float32 [2, 1152, 4608], P(None, 'dp', 'tp'), may hold values from -1 to 1
- down_first: float32 [2, 4608, 1152], P(None, 'tp', 'dp'), may hold values from -1 to 1
- mod_first: float32 [2, 1152, 6, 1152], P(None, 'dp', None, 'tp'), may hold values from -1 to 1
- qkv_second: float32 [2, 1152, 3, 1152], P(None, 'dp', None, 'tp'), may hold values from 0 to 1
- out_second: float32 [2, 1152, 1152], P(None, 'tp', 'dp'), may hold values from 0 to 1
- up_second: float32 [2, 1152, 4608], P(None, 'dp', 'tp'), may hold values from 0 to 1
- down_second: float32 [2, 4608, 1152], P(None, 'tp', 'dp'), may hold values from 0 to 1
- mod_second: float32 [2, 1152, 6, 1152], P(None, 'dp', None, 'tp'), may hold values from 0 to 1
- cotangent: bfloat16 [4, 16, 256, 1152], P('dp', 'ctx', 'tp'), may hold values from -7 to 7
Outputs:
- output: bfloat16 [4, 16, 256, 1152], P('dp', 'ctx', 'tp')
- input_grad: float32 [4, 16, 256, 1152], P('dp', 'ctx', 'tp')
- cond_grad: float32 [4, 1152], P('dp')
- grad_norm: float32 [], replicated
- qkv_new: float32 [2, 1152, 3, 1152], P(None, 'dp', None, 'tp')
- out_new: float32 [2, 1152, 1152], P(None, 'tp', 'dp')
- up_new: float32 [2, 1152, 4608], P(None, 'dp', 'tp')
- down_new: float32 [2, 4608, 1152], P(None, 'tp', 'dp')
- mod_new: float32 [2, 1152, 6, 1152], P(None, 'dp', None, 'tp')
- qkv_copy: bfloat16 [2, 1152, 3, 1152], P(None, 'dp', None, 'tp')
- out_copy: bfloat16 [2, 1152, 1152], P(None, 'tp', 'dp')
- up_copy: bfloat16 [2, 1152, 4608], P(None, 'dp', 'tp')
- down_copy: bfloat16 [2, 4608, 1152], P(None, 'tp', 'dp')
- mod_copy: bfloat16 [2, 1152, 6, 1152], P(None, 'dp', None, 'tp')
- qkv_moment: float32 [2, 1152, 3, 1152], P(None, 'dp', None, 'tp')
- out_moment: float32 [2, 1152, 1152], P(None, 'tp', 'dp')
- up_moment: float32 [2, 1152, 4608], P(None, 'dp', 'tp')
- down_moment: float32 [2, 4608, 1152], P(None, 'tp', 'dp')
- mod_moment: float32 [2, 1152, 6, 1152], P(None, 'dp', None, 'tp')
- qkv_square: float32 [2, 1152, 3, 1152], P(None, 'dp', None, 'tp')
- out_square: float32 [2, 1152, 1152], P(None, 'tp', 'dp')
- up_square: float32 [2, 1152, 4608], P(None, 'dp', 'tp')
- down_square: float32 [2, 4608, 1152], P(None, 'tp', 'dp')
- mod_square: float32 [2, 1152, 6, 1152], P(None, 'dp', None, 'tp')
The draws below stay inside these ranges and needn't reach their ends.
All inputs are finite; a program needn't handle non-finite values.
Results may differ from the reference program's by a relative error of at most 0.02125.
Values may be sent and summed in bfloat16 or wider, within the bound.
A program may use at most 384 MiB of HBM per device.

```python
import math
import jax
import jax.numpy as jnp
from jax import lax

D = 1152
HEADS = 16
HD = 72
FF = 4608
FRAMES = 16
PATCHES = 256
LAYERS = 2
STEP = 5
CLIPS = 4


def ramp(count, ratio):
    place = jnp.arange(count, dtype=jnp.float32) / (count - 1) - 0.5
    return jnp.exp(math.log(ratio) * place)


def unit_size():
    return (LAYERS * (10.0 * D * D + 2.0 * D * FF)) ** (-0.5)


def first_moment(key, shape):
    return jax.random.truncated_normal(key, -3.0, 3.0, shape, jnp.float32) * unit_size()


def second_moment(key, shape):
    unit = unit_size()
    return jnp.exp(jax.random.uniform(key, shape, jnp.float32, 0.0, math.log(4.0))) * unit * unit


def draw_inputs(key, part):
    key = jax.random.fold_in(key, 1)
    shape = (CLIPS, FRAMES, PATCHES, D)
    base = jax.random.truncated_normal(key, -4.0, 4.0, shape, jnp.float32)
    ratio = 3.0
    return (base * ramp(D, ratio)).astype(jnp.bfloat16)


def draw_cotangent(key, part):
    key = jax.random.fold_in(key, 2)
    shape = (CLIPS, FRAMES, PATCHES, D)
    base = jax.random.truncated_normal(key, -4.0, 4.0, shape, jnp.float32)
    ratio = 3.0
    return (base * ramp(D, ratio)).astype(jnp.bfloat16)


def draw_conditioning(key, part):
    key = jax.random.fold_in(key, 3)
    shape = (CLIPS, D)
    base = jax.random.truncated_normal(key, -4.0, 4.0, shape, jnp.float32)
    ratio = 3.0
    return base * ramp(D, ratio)


def draw_qkv_weight(key, part):
    key = jax.random.fold_in(key, 4)
    shape = (LAYERS, D, 3, D)
    base = jax.random.truncated_normal(key, -4.0, 4.0, shape, jnp.float32)
    ratio = 3.0
    ones = jnp.ones((D,), jnp.float32)
    factor = jnp.stack([ones, ones, ramp(D, ratio)])
    return base * factor * D ** (-0.5)


def draw_out_weight(key, part):
    key = jax.random.fold_in(key, 5)
    shape = (LAYERS, D, D)
    base = jax.random.truncated_normal(key, -4.0, 4.0, shape, jnp.float32)
    ratio = 3.0
    level_scale = jnp.where(jnp.arange(LAYERS) % 2 == 0, 4.0, 2.0)
    return base * level_scale[:, None, None] * ramp(D, ratio)[None, :, None] * D ** (-0.5)


def draw_up_weight(key, part):
    key = jax.random.fold_in(key, 6)
    shape = (LAYERS, D, FF)
    base = jax.random.truncated_normal(key, -4.0, 4.0, shape, jnp.float32)
    ratio = 3.0
    return base * ramp(FF, ratio) * D ** (-0.5)


def draw_down_weight(key, part):
    key = jax.random.fold_in(key, 7)
    shape = (LAYERS, FF, D)
    base = jax.random.truncated_normal(key, -4.0, 4.0, shape, jnp.float32)
    ratio = 3.0
    return base * ramp(FF, ratio)[None, :, None] * FF ** (-0.5)


def draw_qkv_first(key, part):
    key = jax.random.fold_in(key, 11)
    return first_moment(key, (LAYERS, D, 3, D))


def draw_out_first(key, part):
    key = jax.random.fold_in(key, 12)
    return first_moment(key, (LAYERS, D, D))


def draw_up_first(key, part):
    key = jax.random.fold_in(key, 13)
    return first_moment(key, (LAYERS, D, FF))


def draw_down_first(key, part):
    key = jax.random.fold_in(key, 14)
    return first_moment(key, (LAYERS, FF, D))


def draw_mod_first(key, part):
    key = jax.random.fold_in(key, 15)
    return first_moment(key, (LAYERS, D, 6, D))


def draw_qkv_second(key, part):
    key = jax.random.fold_in(key, 21)
    return second_moment(key, (LAYERS, D, 3, D))


def draw_out_second(key, part):
    key = jax.random.fold_in(key, 22)
    return second_moment(key, (LAYERS, D, D))


def draw_up_second(key, part):
    key = jax.random.fold_in(key, 23)
    return second_moment(key, (LAYERS, D, FF))


def draw_down_second(key, part):
    key = jax.random.fold_in(key, 24)
    return second_moment(key, (LAYERS, FF, D))


def draw_mod_second(key, part):
    key = jax.random.fold_in(key, 25)
    return second_moment(key, (LAYERS, D, 6, D))


def block_scale(own_key, shape, pieces, smallest, largest):
    gain, own = 1.0, jax.random.fold_in(own_key, 6)
    for position, blocks in pieces:
        draws = jnp.exp(jax.random.uniform(jax.random.fold_in(own, position), (blocks,), jnp.float32, smallest / len(pieces), largest / len(pieces)))
        gain = gain * jnp.repeat(draws, shape[position] // blocks).reshape([-1 if axis == position else 1 for axis in range(len(shape))])
    return gain


def gaussian(own_key, dims, scale, reach, pieces=(), kind=jnp.bfloat16):
    array = scale * jax.random.normal(own_key, dims, jnp.float32)
    if pieces:
        array = array * block_scale(own_key, dims, pieces, -0.22, 0.18)
    return jnp.clip(array, -reach, reach).astype(kind)


def setup_inputs(seed: int = 0) -> dict:
    key_of = jax.random.split(jax.random.key(seed), 19)
    inputs = draw_inputs(jax.random.fold_in(key_of[18], 71), 0)
    conditioning = draw_conditioning(jax.random.fold_in(key_of[18], 71), 0)
    qkv_weight = draw_qkv_weight(jax.random.fold_in(key_of[18], 71), 0)
    out_weight = draw_out_weight(jax.random.fold_in(key_of[18], 71), 0)
    up_weight = draw_up_weight(jax.random.fold_in(key_of[18], 71), 0)
    down_weight = draw_down_weight(jax.random.fold_in(key_of[18], 71), 0)
    mod_weight = gaussian(key_of[6], (LAYERS, D, 6, D), D ** -0.5, 0.1875, ((1, 4), (3, 4)), jnp.float32)
    qkv_first = draw_qkv_first(jax.random.fold_in(key_of[18], 71), 0)
    out_first = draw_out_first(jax.random.fold_in(key_of[18], 71), 0)
    up_first = draw_up_first(jax.random.fold_in(key_of[18], 71), 0)
    down_first = draw_down_first(jax.random.fold_in(key_of[18], 71), 0)
    mod_first = draw_mod_first(jax.random.fold_in(key_of[18], 71), 0)
    qkv_second = draw_qkv_second(jax.random.fold_in(key_of[18], 71), 0)
    out_second = draw_out_second(jax.random.fold_in(key_of[18], 71), 0)
    up_second = draw_up_second(jax.random.fold_in(key_of[18], 71), 0)
    down_second = draw_down_second(jax.random.fold_in(key_of[18], 71), 0)
    mod_second = draw_mod_second(jax.random.fold_in(key_of[18], 71), 0)
    cotangent = draw_cotangent(jax.random.fold_in(key_of[18], 71), 0)
    return dict(inputs=inputs, conditioning=conditioning, qkv_weight=qkv_weight, out_weight=out_weight, up_weight=up_weight, down_weight=down_weight, mod_weight=mod_weight, qkv_first=qkv_first, out_first=out_first, up_first=up_first, down_first=down_first, mod_first=mod_first, qkv_second=qkv_second, out_second=out_second, up_second=up_second, down_second=down_second, mod_second=mod_second, cotangent=cotangent)


EPS_NORM = 1e-06
LEARN_RATE = 0.03
DECAY_RATE = 0.1
BETA_ONE = 0.5
BETA_TWO = 0.5
ADAM_EPS = 1e-08
CLIP_MAX = 1.0

@jax.custom_vjp
def low(v):
    return lax.optimization_barrier(v.astype(jnp.bfloat16)).astype(jnp.float32)

@jax.custom_vjp
def low_back(v):
    return v

def low_keep(v):
    return (low(v), None)

def low_pass(kept, grad):
    return (grad,)

def back_keep(v):
    return (v, None)

def back_low(kept, grad):
    return (low(grad),)
low.defvjp(low_keep, low_pass)
low_back.defvjp(back_keep, back_low)

def normalize(rows):
    centred = rows - lax.optimization_barrier(jnp.mean(rows, axis=-1, keepdims=True))
    return centred * lax.rsqrt(lax.optimization_barrier(jnp.mean(centred * centred, axis=-1, keepdims=True)) + EPS_NORM)

def run_clip(weights, clip_rows, clip_cond):
    qkv_w, out_w, up_w, down_w, mod_w = weights
    highest = lax.Precision.HIGHEST
    scale = HD ** (-0.5)
    hidden = clip_rows
    cond_low = low(jax.nn.silu(clip_cond))
    for level in range(LAYERS):
        modulation = jnp.einsum('d,dke->ke', cond_low, mod_w[level], precision=highest)
        attn_in = low(normalize(hidden) * (1.0 + modulation[1]) + modulation[0])
        projected = low_back(low(jnp.einsum('fpd,dke->fpke', attn_in, qkv_w[level], precision=highest)))
        frames = projected.shape[0]
        patches = projected.shape[1]
        query = projected[:, :, 0].reshape(frames, patches, HEADS, HD)
        key_rows = projected[:, :, 1].reshape(frames, patches, HEADS, HD)
        value_rows = projected[:, :, 2].reshape(frames, patches, HEADS, HD)
        if level % 2 == 0:
            scores = low_back(jnp.einsum('fqhe,fkhe->fhqk', query, key_rows, precision=highest) * scale)
            probs = low(jax.nn.softmax(scores, axis=-1))
            mixed = jnp.einsum('fhqk,fkhe->fqhe', probs, value_rows, precision=highest)
        else:
            scores = low_back(jnp.einsum('qphe,kphe->phqk', query, key_rows, precision=highest) * scale)
            probs = low(jax.nn.softmax(scores, axis=-1))
            mixed = jnp.einsum('phqk,kphe->qphe', probs, value_rows, precision=highest)
        mixed = low_back(low(mixed.reshape(frames, patches, HEADS * HD)))
        branch_a = low_back(jnp.einsum('fpe,ed->fpd', mixed, out_w[level], precision=highest))
        hidden = hidden + modulation[2] * branch_a
        mlp_in = low(normalize(hidden) * (1.0 + modulation[4]) + modulation[3])
        hidden_pre = low_back(jnp.einsum('fpd,dh->fph', mlp_in, up_w[level], precision=highest))
        hidden_act = low(jax.nn.gelu(hidden_pre, approximate=True))
        branch_m = low_back(jnp.einsum('fph,hd->fpd', hidden_act, down_w[level], precision=highest))
        hidden = hidden + modulation[5] * branch_m
    return hidden

def forward(rows, cond, masters):
    lowered = tuple((low(weight) for weight in masters))

    def clip_step(item):
        return jax.checkpoint(run_clip)(lowered, item[0], item[1])
    return lax.map(clip_step, (rows, cond))

def adam_update(master, first, second, grad, coef):
    clipped = coef * grad
    first_new = BETA_ONE * first + (1.0 - BETA_ONE) * clipped
    second_new = BETA_TWO * second + (1.0 - BETA_TWO) * clipped * clipped
    first_hat = first_new / (1.0 - BETA_ONE ** STEP)
    second_hat = second_new / (1.0 - BETA_TWO ** STEP)
    master_new = master - LEARN_RATE * (first_hat / (jnp.sqrt(second_hat) + ADAM_EPS) + DECAY_RATE * master)
    return (master_new, master_new.astype(jnp.bfloat16), first_new, second_new)

def reference(inputs, conditioning, qkv_weight, out_weight, up_weight, down_weight, mod_weight, qkv_first, out_first, up_first, down_first, mod_first, qkv_second, out_second, up_second, down_second, mod_second, cotangent):
    masters = (qkv_weight, out_weight, up_weight, down_weight, mod_weight)
    firsts = (qkv_first, out_first, up_first, down_first, mod_first)
    seconds = (qkv_second, out_second, up_second, down_second, mod_second)
    result, pull = jax.vjp(forward, inputs.astype(jnp.float32), conditioning, masters)
    input_grad, cond_grad, grads = pull(cotangent.astype(jnp.float32))
    squares = jnp.zeros((), jnp.float32)
    for grad in grads:
        squares = squares + jnp.sum(grad * grad)
    grad_norm = jnp.sqrt(squares)
    coef = CLIP_MAX / jnp.maximum(grad_norm, CLIP_MAX)
    updates = [adam_update(masters[kind], firsts[kind], seconds[kind], grads[kind], coef) for kind in range(5)]
    return (result.astype(jnp.bfloat16), input_grad, cond_grad, grad_norm, updates[0][0], updates[1][0], updates[2][0], updates[3][0], updates[4][0], updates[0][1], updates[1][1], updates[2][1], updates[3][1], updates[4][1], updates[0][2], updates[1][2], updates[2][2], updates[3][2], updates[4][2], updates[0][3], updates[1][3], updates[2][3], updates[3][3], updates[4][3])
```

```python
from functools import partial

import jax
import jax.numpy as jnp
from jax import lax
from jax.experimental import pallas as pl
from jax.experimental.pallas import tpu as pltpu
from jax.sharding import PartitionSpec as P

HD = 72
STEP = 5
EPS_NORM = 1e-06
LEARN_RATE = 0.03
DECAY_RATE = 0.1
BETA_ONE = 0.5
BETA_TWO = 0.5
ADAM_EPS = 1e-08
CLIP_MAX = 1.0
MESH = pl.DeviceIdType.MESH
MATS = 3
DEPTH = 4
VMEM_LIMIT = 60 * 1024 * 1024
SPATIAL_FORMS = ("fqjhe,fkjhe->fjhqk", "fjhqk,fkjhe->fqjhe", "fjhqk,fqjhe->fkjhe")
TEMPORAL_FORMS = ("qpjhe,kpjhe->pjhqk", "pjhqk,kpjhe->qpjhe", "pjhqk,qpjhe->kpjhe")


def normalize(rows):
    centred = rows - jnp.mean(rows, axis=-1, keepdims=True)
    rstd = lax.rsqrt(jnp.mean(centred * centred, axis=-1, keepdims=True) + EPS_NORM)
    return (centred * rstd, rstd)


def normalize_back(grad, normed, rstd):
    return rstd * (
        grad
        - jnp.mean(grad, axis=-1, keepdims=True)
        - normed * jnp.mean(grad * normed, axis=-1, keepdims=True)
    )


def attend(query, key, value, forms, scale):
    scores = jnp.einsum(forms[0], query, key, preferred_element_type=jnp.float32) * scale
    top = jnp.max(scores, axis=-1, keepdims=True)
    expo = jnp.exp(scores - top)
    total = jnp.sum(expo, axis=-1, keepdims=True)
    probs = (expo / total).astype(jnp.bfloat16)
    mixed = jnp.einsum(forms[1], probs, value, preferred_element_type=jnp.float32)
    return (mixed.astype(jnp.bfloat16), top + jnp.log(total))


def attend_back(query, key, value, d_mixed, log_total, forms, scale):
    scores = jnp.einsum(forms[0], query, key, preferred_element_type=jnp.float32) * scale
    probs = jnp.exp(scores - log_total)
    d_probs = jnp.einsum(forms[0], d_mixed, value, preferred_element_type=jnp.float32)
    d_scores = (probs * (d_probs - jnp.sum(probs * d_probs, axis=-1, keepdims=True))).astype(
        jnp.bfloat16
    )
    d_value = jnp.einsum(
        forms[2], probs.astype(jnp.bfloat16), d_mixed, preferred_element_type=jnp.float32
    )
    d_query = jnp.einsum(forms[1], d_scores, key, preferred_element_type=jnp.float32) * scale
    d_key = jnp.einsum(forms[2], d_scores, query, preferred_element_type=jnp.float32) * scale
    return (d_query, d_key, d_value)


def adam_update(master, first, second, grad, coef):
    clipped = coef * grad
    first_new = BETA_ONE * first + (1.0 - BETA_ONE) * clipped
    second_new = BETA_TWO * second + (1.0 - BETA_TWO) * clipped * clipped
    first_hat = first_new / (1.0 - BETA_ONE**STEP)
    second_hat = second_new / (1.0 - BETA_TWO**STEP)
    master_new = master - LEARN_RATE * (
        first_hat / (jnp.sqrt(second_hat) + ADAM_EPS) + DECAY_RATE * master
    )
    return (master_new, master_new.astype(jnp.bfloat16), first_new, second_new)


def place():
    return lax.axis_index("dp"), lax.axis_index("ctx"), lax.axis_index("tp")


def greet(peers):
    barrier = pltpu.get_barrier_semaphore()
    for peer in peers:
        pl.semaphore_signal(barrier, inc=1, device_id=peer, device_id_type=MESH)
    pl.semaphore_wait(barrier, len(peers))


def gather_kernel(tps, shard_ref, full_ref, send_sem, recv_sem, local_sem):
    p, c, t = place()
    mats, rows = shard_ref.shape[0], shard_ref.shape[1]
    half = rows // 2
    mine = pl.ds(pl.multiple_of(c * half, half), half)
    beside, above, twin = (p ^ 1, c, t), (p ^ 2, c, t), (p, 1 - c, t)
    chain = [(p, c, lax.rem(t + k, tps)) for k in range(1, tps)]
    greet(chain + [beside, above, twin])
    split = tps // 2
    base_z, base_x, base_y, base_d, base_s = 0, tps, 2 * tps, 3 * tps, 4 * tps

    def copy(m, slot, src, dst, peer):
        return pltpu.make_async_remote_copy(
            src_ref=src, dst_ref=dst, send_sem=send_sem.at[m, slot], recv_sem=recv_sem.at[m, slot],
            device_id=peer, device_id_type=MESH,
        )

    def block(m, k, owner):
        return full_ref.at[m, lax.rem(t + tps - k, tps), owner, mine]

    def column(m, owner):
        return full_ref.at[m, :, owner, mine]

    def own(m):
        return shard_ref.at[m, mine]

    def keep(m):
        return pltpu.make_async_copy(own(m), block(m, 0, p), local_sem.at[m])

    def along(m, k):
        return copy(m, base_z + k, own(m), block(m, 0, p), chain[k - 1])

    def to_x(m, k):
        return copy(m, base_x + k, own(m) if k == 0 else block(m, k, p), block(m, k, p), beside)

    def to_y(m, k):
        return copy(m, base_y + k, own(m) if k == 0 else block(m, k, p), block(m, k, p), above)

    def corner(m, k):
        if k < split:
            return copy(m, base_d + k, block(m, k, p ^ 1), block(m, k, p ^ 1), above)
        return copy(m, base_d + k, block(m, k, p ^ 2), block(m, k, p ^ 2), beside)

    def to_twin(m, which):
        owner = (p, p ^ 1, p ^ 2, p ^ 3)[which]
        return copy(m, base_s + which, column(m, owner), column(m, owner), twin)

    def open_up(m):
        keep(m).start()
        for k in range(1, tps):
            along(m, k).start()
        to_x(m, 0).start()
        to_y(m, 0).start()

    def spread(m):
        for k in range(1, tps):
            along(m, k).wait_recv()
            to_x(m, k).start()
            to_y(m, k).start()
        keep(m).wait()
        to_twin(m, 0).start()

    def turn(m):
        for k in range(tps):
            to_x(m, k).wait_recv()
            if k < split:
                corner(m, k).start()
            to_y(m, k).wait_recv()
            if k >= split:
                corner(m, k).start()
        to_twin(m, 1).start()
        to_twin(m, 2).start()

    def close(m):
        for k in range(tps):
            corner(m, k).wait_recv()
        to_twin(m, 3).start()

    for step in range(mats + 3):
        if step < mats:
            open_up(step)
        if 0 <= step - 1 < mats:
            spread(step - 1)
        if 0 <= step - 2 < mats:
            turn(step - 2)
        if 0 <= step - 3 < mats:
            close(step - 3)
    for m in range(mats):
        for which in range(4):
            to_twin(m, which).wait()
        for k in range(tps):
            if k:
                along(m, k).wait_send()
            to_x(m, k).wait_send()
            to_y(m, k).wait_send()
            corner(m, k).wait_send()


def by_hand(mesh_shape, rows):
    return mesh_shape["dp"] == 4 and mesh_shape["ctx"] == 2 and rows % 32 == 0


def gather_weights(shards, mesh_shape):
    tps = mesh_shape["tp"]
    mats, rows, width = shards.shape
    if not by_hand(mesh_shape, rows):
        full = lax.all_gather(shards, "dp", axis=1, tiled=True)
        return lax.all_gather(full, "tp", axis=1, tiled=False)
    dps = mesh_shape["dp"]
    full = pl.pallas_call(
        partial(gather_kernel, tps),
        out_shape=jax.ShapeDtypeStruct((mats, tps, dps, rows, width), shards.dtype),
        in_specs=[pl.BlockSpec(memory_space=pl.ANY)],
        out_specs=pl.BlockSpec(memory_space=pl.ANY),
        scratch_shapes=[
            pltpu.SemaphoreType.DMA((mats, 4 * tps + 4)),
            pltpu.SemaphoreType.DMA((mats, 4 * tps + 4)),
            pltpu.SemaphoreType.DMA((mats,)),
        ],
        compiler_params=pltpu.CompilerParams(collective_id=0, has_side_effects=True),
        name="gather_weights",
    )(shards)
    return full.reshape(mats, tps, dps * rows, width)


def add_into(acc, other):
    def one(i, carry):
        acc[i] = (acc[i].astype(jnp.float32) + other[i].astype(jnp.float32)).astype(acc.dtype)
        return carry

    lax.fori_loop(0, acc.shape[0], one, 0)


def reduce_kernel(tps, mats, *refs):
    grads = refs[:mats]
    out_ref = refs[mats]
    (tot, twin_in, beside_in, above_in, corner_x, corner_y, chain_in, last,
     send_sem, recv_sem, local_sem, free_sem) = refs[mats + 1:]
    p, c, t = place()
    rows = grads[0].shape[2]
    half = rows // 2
    mine = pl.ds(pl.multiple_of(c * half, half), half)
    theirs = pl.ds(pl.multiple_of((1 - c) * half, half), half)
    beside, above, twin = (p ^ 1, c, t), (p ^ 2, c, t), (p, 1 - c, t)
    chain = [(p, c, lax.rem(t + k, tps)) for k in range(1, tps)]
    greet(chain + [beside, above, twin])
    split = tps // 2
    TWIN, CX, CY, BX, BY, ZZ = 0, 1, 2, 3, 4, 5
    END = ZZ + tps - 1

    def copy(m, slot, src, dst, peer):
        return pltpu.make_async_remote_copy(
            src_ref=src, dst_ref=dst, send_sem=send_sem.at[m, slot], recv_sem=recv_sem.at[m, slot],
            device_id=peer, device_id_type=MESH,
        )

    def to_twin(m):
        return copy(m, TWIN, grads[m].at[:, :, theirs], twin_in.at[m % 2], twin)

    def load(m):
        return pltpu.make_async_copy(grads[m].at[:, :, mine], tot.at[m % DEPTH], local_sem.at[m, 0])

    def tot_at(m, owner):
        return tot.at[m % DEPTH, :, owner]

    def corner_to_x(m):
        return copy(m, CX, tot.at[m % DEPTH, pl.ds(0, split), p ^ 3], corner_x.at[m % 2], beside)

    def corner_to_y(m):
        return copy(m, CY, tot.at[m % DEPTH, pl.ds(split, tps - split), p ^ 3], corner_y.at[m % 2], above)

    def to_x(m):
        return copy(m, BX, tot_at(m, p ^ 1), beside_in.at[m % 2], beside)

    def to_y(m):
        return copy(m, BY, tot_at(m, p ^ 2), above_in.at[m % 2], above)

    def along(m, k):
        peer = chain[k - 1]
        return copy(m, ZZ + k - 1, tot.at[m % DEPTH, peer[2], p], chain_in.at[m % 2, k - 1], peer)

    def finish(m):
        return copy(m, END, last.at[m % 2], out_ref.at[m, mine], twin)

    def keep(m):
        return pltpu.make_async_copy(last.at[m % 2], out_ref.at[m, mine], local_sem.at[m, 1])

    def credit(slot, peer, m):
        if m + 2 < mats:
            pl.semaphore_signal(free_sem.at[slot], inc=1, device_id=peer, device_id_type=MESH)

    def spend(slot, m):
        if m >= 2:
            pl.semaphore_wait(free_sem.at[slot], 1)

    def sent(m):
        corner_to_x(m).wait_send()
        corner_to_y(m).wait_send()
        to_x(m).wait_send()
        to_y(m).wait_send()
        for k in range(1, tps):
            along(m, k).wait_send()

    def stage_a(m):
        if m >= DEPTH:
            sent(m - DEPTH)
        spend(TWIN, m)
        to_twin(m).start()
        load(m).start()

    def stage_b(m):
        load(m).wait()
        to_twin(m).wait_recv()
        for i in range(tps):
            add_into(tot.at[m % DEPTH, i], twin_in.at[m % 2, i])
        credit(TWIN, twin, m)
        spend(CX, m)
        corner_to_x(m).start()
        spend(CY, m)
        corner_to_y(m).start()

    def stage_c(m):
        corner_to_x(m).wait_recv()
        for i in range(split):
            add_into(tot.at[m % DEPTH, pl.ds(i, 1), p ^ 2], corner_x.at[m % 2, pl.ds(i, 1)])
        credit(CX, beside, m)
        spend(BY, m)
        to_y(m).start()
        corner_to_y(m).wait_recv()
        for i in range(tps - split):
            add_into(tot.at[m % DEPTH, pl.ds(split + i, 1), p ^ 1], corner_y.at[m % 2, pl.ds(i, 1)])
        credit(CY, above, m)
        spend(BX, m)
        to_x(m).start()

    def stage_d(m):
        to_x(m).wait_recv()
        add_into(tot.at[m % DEPTH, :, p], beside_in.at[m % 2])
        credit(BX, beside, m)
        to_y(m).wait_recv()
        add_into(tot.at[m % DEPTH, :, p], above_in.at[m % 2])
        credit(BY, above, m)
        for k in range(1, tps):
            spend(ZZ + k - 1, m)
            along(m, k).start()

    def stage_e(m):
        if m >= 2:
            finish(m - 2).wait_send()
            keep(m - 2).wait()
        for k in range(1, tps):
            along(m, k).wait_recv()
        total = tot[m % DEPTH, t, p].astype(jnp.float32)
        for k in range(1, tps):
            total = total + chain_in[m % 2, k - 1].astype(jnp.float32)
        last[m % 2] = total.astype(last.dtype)
        for k in range(1, tps):
            credit(ZZ + k - 1, (p, c, lax.rem(t + tps - k, tps)), m)
        finish(m).start()
        keep(m).start()

    stages = [stage_a, stage_b, stage_c, stage_d, stage_e]
    for step in range(mats + len(stages) - 1):
        for lag in reversed(range(len(stages))):
            if 0 <= step - lag < mats:
                stages[lag](step - lag)
    for m in range(mats):
        to_twin(m).wait_send()
        finish(m).wait_recv()
        if m >= mats - DEPTH:
            sent(m)
        if m >= mats - 2:
            finish(m).wait_send()
            keep(m).wait()


def reduce_grads(grads, mesh_shape):
    tps, dps = mesh_shape["tp"], mesh_shape["dp"]
    mats = len(grads)
    depth, width = grads[0].shape[1:]
    rows = depth // dps
    if not by_hand(mesh_shape, rows):
        parts = []
        for grad in grads:
            part = lax.psum_scatter(grad, "tp", scatter_dimension=0, tiled=True)[0]
            part = lax.psum_scatter(part, "dp", scatter_dimension=0, tiled=True)
            parts.append(lax.psum(part, "ctx"))
        return jnp.stack(parts)
    half = rows // 2
    low = grads[0].dtype
    split = tps // 2
    slots = 5 + tps
    return pl.pallas_call(
        partial(reduce_kernel, tps, mats),
        out_shape=jax.ShapeDtypeStruct((mats, rows, width), low),
        in_specs=[pl.BlockSpec(memory_space=pl.ANY)] * mats,
        out_specs=pl.BlockSpec(memory_space=pl.ANY),
        scratch_shapes=[
            pltpu.VMEM((DEPTH, tps, dps, half, width), low),
            pltpu.VMEM((2, tps, dps, half, width), low),
            pltpu.VMEM((2, tps, half, width), low),
            pltpu.VMEM((2, tps, half, width), low),
            pltpu.VMEM((2, split, half, width), low),
            pltpu.VMEM((2, tps - split, half, width), low),
            pltpu.VMEM((2, tps - 1, half, width), low),
            pltpu.VMEM((2, half, width), low),
            pltpu.SemaphoreType.DMA((mats, slots)),
            pltpu.SemaphoreType.DMA((mats, slots)),
            pltpu.SemaphoreType.DMA((mats, 2)),
            pltpu.SemaphoreType.REGULAR((slots,)),
        ],
        compiler_params=pltpu.CompilerParams(
            collective_id=1, has_side_effects=True, vmem_limit_bytes=VMEM_LIMIT
        ),
        name="reduce_grads",
    )(*[grad.reshape(tps, dps, rows, width) for grad in grads])


def pack(qkv, out, up, down):
    rows = qkv.shape[0]
    low = jnp.bfloat16
    first = jnp.concatenate([qkv.astype(low).reshape(rows, -1), out.astype(low).T], axis=1)
    return jnp.stack([first, up.astype(low), down.astype(low).T])


def unpack(first, second, third, like):
    rows, _, wide = like.shape
    cut = 3 * wide
    return (first[:, :cut].reshape(rows, 3, wide), first[:, cut:].T, second, third.T)


def frames_whole(rows):
    return lax.all_to_all(rows, "tp", 0, 1, tiled=True)


def frames_back(rows):
    return lax.all_to_all(rows, "tp", 1, 0, tiled=True)


def patches_whole(rows):
    return lax.all_to_all(rows, ("tp", "ctx"), 1, 0, tiled=True)


def patches_back(rows):
    return lax.all_to_all(rows, ("tp", "ctx"), 0, 1, tiled=True)


def columns_home(rows, mesh_shape):
    frames, patches, width = rows.shape
    tps, cs = mesh_shape["tp"], mesh_shape["ctx"]
    split = rows.reshape(tps, cs, frames // (tps * cs), patches, width)
    split = split.transpose(1, 0, 2, 3, 4).reshape(cs, frames // cs, patches, width)
    return lax.all_to_all(split, "ctx", 0, 2, tiled=True)[0]


def columns_away(rows, mesh_shape):
    tps, cs = mesh_shape["tp"], mesh_shape["ctx"]
    frames, patches, width = rows.shape
    split = lax.all_to_all(rows[None], "ctx", 2, 0, tiled=True)
    split = split.reshape(cs, tps, frames // tps, patches // cs, width).transpose(1, 0, 2, 3, 4)
    return split.reshape(frames * cs, patches // cs, width)


def per_device(mesh_shape, inputs, conditioning, *states):
    masters, firsts, seconds, cotangent = states[:5], states[5:10], states[10:15], states[15]
    qkv_weight, out_weight, up_weight, down_weight, mod_weight = masters
    low = jnp.bfloat16
    highest = lax.Precision.HIGHEST
    layers = qkv_weight.shape[0]
    scale = HD ** (-0.5)
    dp_at, _, tp_at = place()
    tps, dps = mesh_shape["tp"], mesh_shape["dp"]
    rows = qkv_weight.shape[1]
    wide = qkv_weight.shape[3]
    heads = wide // HD
    width = inputs.shape[-1]

    shards = jnp.concatenate(
        [pack(qkv_weight[l], out_weight[l], up_weight[l], down_weight[l]) for l in range(layers)]
    )
    full = gather_weights(shards, mesh_shape)

    cond_low = jax.nn.silu(conditioning).astype(low)
    cond_all = lax.all_gather(cond_low, "dp", axis=0, tiled=True)
    cond_mine = lax.dynamic_slice_in_dim(cond_all, dp_at * rows, rows, 1)
    mod_low = mod_weight.astype(low)
    mod_part = jnp.einsum("cd,ldke->clke", cond_mine, mod_low, preferred_element_type=jnp.float32)
    mod_part = lax.psum_scatter(mod_part, "dp", scatter_dimension=0, tiled=True)
    modulation = lax.all_gather(mod_part, "tp", axis=3, tiled=True)[0]

    hidden = frames_whole(inputs[0]).astype(jnp.float32)
    saved = []
    for level in range(layers):
        if level:
            if level % 2 == 1:
                hidden = patches_whole(hidden.astype(low)).astype(jnp.float32)
            else:
                hidden = patches_back(hidden.astype(low)).astype(jnp.float32)
        forms = SPATIAL_FORMS if level % 2 == 0 else TEMPORAL_FORMS
        first_w, up_w, down_w = full[MATS * level], full[MATS * level + 1], full[MATS * level + 2]
        factors = modulation[level]
        frames, patches = hidden.shape[:2]
        normed_a, rstd_a = normalize(hidden)
        attn_in = (normed_a * (1.0 + factors[1]) + factors[0]).astype(low)
        projected = jnp.einsum(
            "fpd,jde->fpje", attn_in, first_w[:, :, : 3 * wide], preferred_element_type=jnp.float32
        ).astype(low)
        projected = projected.reshape(frames, patches, tps, 3, heads, HD)
        query, key, value = (projected[:, :, :, s] for s in range(3))
        mixed, log_total = attend(query, key, value, forms, scale)
        mixed = mixed.reshape(frames, patches, tps, wide)
        branch_a = jnp.einsum(
            "fpje,jde->fpd", mixed, first_w[:, :, 3 * wide :], preferred_element_type=jnp.float32
        )
        middle = hidden + factors[2] * branch_a
        normed_m, rstd_m = normalize(middle)
        mlp_in = (normed_m * (1.0 + factors[4]) + factors[3]).astype(low)
        hidden_pre = jnp.einsum("fpd,jdh->fpjh", mlp_in, up_w, preferred_element_type=jnp.float32)
        hidden_act = jax.nn.gelu(hidden_pre, approximate=True).astype(low)
        branch_m = jnp.einsum("fpjh,jdh->fpd", hidden_act, down_w, preferred_element_type=jnp.float32)
        saved.append(
            (forms, first_w, up_w, down_w, factors, normed_a, rstd_a, attn_in, query, key, value,
             mixed, log_total, branch_a, normed_m, rstd_m, mlp_in, hidden_pre, hidden_act, branch_m)
        )
        hidden = middle + factors[5] * branch_m
    temporal_end = layers % 2 == 0
    output = hidden.astype(low)
    output = columns_home(output, mesh_shape) if temporal_end else frames_back(output)
    upstream = columns_away(cotangent[0], mesh_shape) if temporal_end else frames_whole(cotangent[0])
    upstream = upstream.astype(jnp.float32)

    grads = [None] * (MATS * layers)
    d_mods = [None] * layers
    for level in reversed(range(layers)):
        (forms, first_w, up_w, down_w, factors, normed_a, rstd_a, attn_in, query, key, value,
         mixed, log_total, branch_a, normed_m, rstd_m, mlp_in, hidden_pre, hidden_act, branch_m) = saved[level]
        frames, patches = upstream.shape[:2]
        d_gate_m = jnp.sum(upstream * branch_m, axis=(0, 1))
        d_branch_m = (factors[5] * upstream).astype(low)
        grads[MATS * level + 2] = jnp.einsum(
            "fpd,fpjh->jdh", d_branch_m, hidden_act, preferred_element_type=jnp.float32
        ).astype(low)
        d_act = jnp.einsum("fpd,jdh->fpjh", d_branch_m, down_w, preferred_element_type=jnp.float32)
        slope_pull = jax.vjp(partial(jax.nn.gelu, approximate=True), hidden_pre)[1]
        d_pre = slope_pull(d_act)[0].astype(low)
        grads[MATS * level + 1] = jnp.einsum(
            "fpd,fpjh->jdh", mlp_in, d_pre, preferred_element_type=jnp.float32
        ).astype(low)
        d_mlp_in = jnp.einsum("fpjh,jdh->fpd", d_pre, up_w, preferred_element_type=jnp.float32)
        d_shift_m = jnp.sum(d_mlp_in, axis=(0, 1))
        d_scale_m = jnp.sum(d_mlp_in * normed_m, axis=(0, 1))
        upstream = upstream + normalize_back(d_mlp_in * (1.0 + factors[4]), normed_m, rstd_m)
        d_gate_a = jnp.sum(upstream * branch_a, axis=(0, 1))
        d_branch_a = (factors[2] * upstream).astype(low)
        grad_out = jnp.einsum("fpd,fpje->jde", d_branch_a, mixed, preferred_element_type=jnp.float32)
        d_mixed = jnp.einsum(
            "fpd,jde->fpje", d_branch_a, first_w[:, :, 3 * wide :], preferred_element_type=jnp.float32
        ).astype(low)
        d_mixed = d_mixed.reshape(frames, patches, tps, heads, HD)
        d_parts = attend_back(query, key, value, d_mixed, log_total, forms, scale)
        d_projected = jnp.stack(d_parts, axis=3).astype(low).reshape(frames, patches, tps, 3 * wide)
        grad_qkv = jnp.einsum("fpd,fpje->jde", attn_in, d_projected, preferred_element_type=jnp.float32)
        grads[MATS * level] = jnp.concatenate([grad_qkv, grad_out], axis=2).astype(low)
        d_attn_in = jnp.einsum(
            "fpje,jde->fpd", d_projected, first_w[:, :, : 3 * wide], preferred_element_type=jnp.float32
        )
        d_shift_a = jnp.sum(d_attn_in, axis=(0, 1))
        d_scale_a = jnp.sum(d_attn_in * normed_a, axis=(0, 1))
        upstream = upstream + normalize_back(d_attn_in * (1.0 + factors[1]), normed_a, rstd_a)
        d_mods[level] = jnp.stack([d_shift_a, d_scale_a, d_gate_a, d_shift_m, d_scale_m, d_gate_m])
        if level:
            if level % 2 == 1:
                upstream = patches_back(upstream.astype(low)).astype(jnp.float32)
            else:
                upstream = patches_whole(upstream.astype(low)).astype(jnp.float32)
    input_grad = frames_back(upstream.astype(low)).astype(jnp.float32)

    reduced = reduce_grads([grads[m] for m in reversed(range(MATS * layers))], mesh_shape)
    reduced = reduced.astype(jnp.float32)

    d_mod = lax.psum(jnp.stack(d_mods)[None], ("ctx", "tp"))
    d_mod_all = lax.all_gather(d_mod, "dp", axis=0, tiled=True)
    d_mod_mine = lax.dynamic_slice_in_dim(d_mod_all, tp_at * wide, wide, 3)
    grad_mod = jnp.einsum("cd,clke->ldke", cond_mine.astype(jnp.float32), d_mod_mine, precision=highest)
    cond_part = jnp.einsum("clke,ldke->cd", d_mod_mine, mod_low.astype(jnp.float32), precision=highest)
    cond_part = lax.all_gather(lax.psum(cond_part, "tp"), "dp", axis=1, tiled=True)
    cond_total = lax.dynamic_slice_in_dim(cond_part, dp_at * conditioning.shape[0], conditioning.shape[0], 0)
    cond_grad = jax.vjp(jax.nn.silu, conditioning)[1](cond_total)[0]

    order = list(reversed(range(MATS * layers)))
    per_level = [
        unpack(*[reduced[order.index(MATS * level + kind)] for kind in range(MATS)], qkv_weight[level])
        for level in range(layers)
    ]
    stacked = [jnp.stack([per_level[level][kind] for level in range(layers)]) for kind in range(4)]
    stacked.append(grad_mod)
    squares = jnp.zeros((), jnp.float32)
    for grad in stacked:
        squares = squares + jnp.sum(grad * grad)
    grad_norm = jnp.sqrt(lax.psum(squares, ("dp", "tp")))
    coef = CLIP_MAX / jnp.maximum(grad_norm, CLIP_MAX)
    updates = [
        adam_update(masters[kind], firsts[kind], seconds[kind], stacked[kind], coef) for kind in range(5)
    ]
    return (output[None], input_grad[None], cond_grad, grad_norm) + tuple(
        updates[kind][part] for part in range(4) for kind in range(5)
    )


def solution(mesh):
    weights = (
        P(None, "dp", None, "tp"),
        P(None, "tp", "dp"),
        P(None, "dp", "tp"),
        P(None, "tp", "dp"),
        P(None, "dp", None, "tp"),
    )
    rows = P("dp", "ctx", "tp", None)
    return jax.shard_map(
        partial(per_device, dict(mesh.shape)),
        mesh=mesh,
        in_specs=(rows, P("dp", None)) + weights * 3 + (rows,),
        out_specs=(rows, rows, P("dp", None), P()) + weights * 4,
        check_vma=False,
    )
```

```python
from functools import partial

import jax
import jax.numpy as jnp
from jax import lax
from jax.experimental import pallas as pl
from jax.experimental.pallas import tpu as pltpu
from jax.sharding import PartitionSpec as P

HD = 72
STEP = 5
EPS_NORM = 1e-06
LEARN_RATE = 0.03
DECAY_RATE = 0.1
BETA_ONE = 0.5
BETA_TWO = 0.5
ADAM_EPS = 1e-08
CLIP_MAX = 1.0
MESH = pl.DeviceIdType.MESH
MATS = 3
DEPTH = 4
VMEM_LIMIT = 60 * 1024 * 1024
LANES = 384
SLOTS = 4
GROUP = 256
SPATIAL_FORMS = ("fqjhe,fkjhe->fjhqk", "fjhqk,fkjhe->fqjhe", "fjhqk,fqjhe->fkjhe")
TEMPORAL_FORMS = ("qpjhe,kpjhe->pjhqk", "pjhqk,kpjhe->qpjhe", "pjhqk,qpjhe->kpjhe")


def normalize(rows):
    centred = rows - jnp.mean(rows, axis=-1, keepdims=True)
    rstd = lax.rsqrt(jnp.mean(centred * centred, axis=-1, keepdims=True) + EPS_NORM)
    return (centred * rstd, rstd)


def normalize_back(grad, normed, rstd):
    return rstd * (
        grad
        - jnp.mean(grad, axis=-1, keepdims=True)
        - normed * jnp.mean(grad * normed, axis=-1, keepdims=True)
    )


def attend(query, key, value, forms, scale):
    scores = jnp.einsum(forms[0], query, key, preferred_element_type=jnp.float32) * scale
    top = jnp.max(scores, axis=-1, keepdims=True)
    expo = jnp.exp(scores - top)
    total = jnp.sum(expo, axis=-1, keepdims=True)
    probs = (expo / total).astype(jnp.bfloat16)
    mixed = jnp.einsum(forms[1], probs, value, preferred_element_type=jnp.float32)
    return (mixed.astype(jnp.bfloat16), top + jnp.log(total))


def attend_back(query, key, value, d_mixed, log_total, forms, scale):
    scores = jnp.einsum(forms[0], query, key, preferred_element_type=jnp.float32) * scale
    probs = jnp.exp(scores - log_total)
    d_probs = jnp.einsum(forms[0], d_mixed, value, preferred_element_type=jnp.float32)
    d_scores = (probs * (d_probs - jnp.sum(probs * d_probs, axis=-1, keepdims=True))).astype(
        jnp.bfloat16
    )
    d_value = jnp.einsum(
        forms[2], probs.astype(jnp.bfloat16), d_mixed, preferred_element_type=jnp.float32
    )
    d_query = jnp.einsum(forms[1], d_scores, key, preferred_element_type=jnp.float32) * scale
    d_key = jnp.einsum(forms[2], d_scores, query, preferred_element_type=jnp.float32) * scale
    return (d_query, d_key, d_value)


def adam_update(master, first, second, grad, coef):
    clipped = coef * grad
    first_new = BETA_ONE * first + (1.0 - BETA_ONE) * clipped
    second_new = BETA_TWO * second + (1.0 - BETA_TWO) * clipped * clipped
    first_hat = first_new / (1.0 - BETA_ONE**STEP)
    second_hat = second_new / (1.0 - BETA_TWO**STEP)
    master_new = master - LEARN_RATE * (
        first_hat / (jnp.sqrt(second_hat) + ADAM_EPS) + DECAY_RATE * master
    )
    return (master_new, master_new.astype(jnp.bfloat16), first_new, second_new)


def place():
    return lax.axis_index("dp"), lax.axis_index("ctx"), lax.axis_index("tp")


def greet(peers):
    barrier = pltpu.get_barrier_semaphore()
    for peer in peers:
        pl.semaphore_signal(barrier, inc=1, device_id=peer, device_id_type=MESH)
    pl.semaphore_wait(barrier, len(peers))


def by_hand(mesh_shape, inputs, qkv_weight):
    tps, cs = mesh_shape["tp"], mesh_shape["ctx"]
    layers, rows, _, wide = qkv_weight.shape
    clips, frames, strip, width = inputs.shape
    return (
        mesh_shape["dp"] == 4 and cs == 2 and tps == 4 and clips == 1 and layers == 2 and rows % 32 == 0
        and wide == 4 * HD and 4 * wide == width and width % LANES == 0 and frames == 2 * tps
        and strip * tps == GROUP and frames * cs == 16 and strip == 64
    )


def gather_weights(shards):
    full = lax.all_gather(shards, "dp", axis=1, tiled=True)
    return lax.all_gather(full, "tp", axis=1, tiled=False)


class Links:
    def __init__(self, send_sem, recv_sem, local_sem):
        self.send_sem, self.recv_sem, self.local_sem = send_sem, recv_sem, local_sem
        self.used, self.used_local = 0, 0

    def remote(self, make):
        at = self.used
        self.used += 1

        def build(*args):
            src, dst, peer = make(*args)
            return pltpu.make_async_remote_copy(
                src_ref=src, dst_ref=dst, send_sem=self.send_sem.at[at], recv_sem=self.recv_sem.at[at],
                device_id=peer, device_id_type=MESH,
            )

        return build

    def local(self, src, dst):
        at = self.used_local
        self.used_local += 1
        return pltpu.make_async_copy(src, dst, self.local_sem.at[at])


def lane_mask(shape, low, high):
    lane = lax.broadcasted_iota(jnp.int32, shape, 1)
    return jnp.logical_and(lane >= low, lane < high)


def dot_nn(a, b):
    return lax.dot_general(a, b, (((1,), (0,)), ((), ())), preferred_element_type=jnp.float32)


def dot_nt(a, b):
    return lax.dot_general(a, b, (((1,), (1,)), ((), ())), preferred_element_type=jnp.float32)


def dot_tn(a, b):
    return lax.dot_general(a, b, (((0,), (0,)), ((), ())), preferred_element_type=jnp.float32)


def softmax_rows(scores, columns):
    if columns:
        rows = lax.broadcasted_iota(jnp.int32, scores.shape, 0)
        cols = lax.broadcasted_iota(jnp.int32, scores.shape, 1)
        scores = jnp.where((rows & (columns - 1)) == (cols & (columns - 1)), scores, -1e30)
    top = jnp.max(scores, axis=-1, keepdims=True)
    expo = jnp.exp(scores - top)
    return expo * (1.0 / jnp.sum(expo, axis=-1, keepdims=True))


def head_stack(rows, first, heads):
    return jnp.concatenate(
        [jnp.where(lane_mask(rows.shape, first + h * HD, first + (h + 1) * HD), rows, jnp.zeros_like(rows)) for h in range(heads)],
        axis=0,
    )


def head_merge(stacked, first, heads):
    size = stacked.shape[0] // heads
    total = jnp.zeros((size, stacked.shape[1]), stacked.dtype)
    for h in range(heads):
        part = stacked[h * size : (h + 1) * size]
        total = jnp.where(lane_mask(part.shape, first + h * HD, first + (h + 1) * HD), part, total)
    return total


def forward_kernel(tps, geometry, *refs):
    layers, frames, wide, heads = geometry
    (shard_ref, rows_ref, cot_ref, mod_ref,
     full_ref, out_ref, cot_out, hid_out, mid_out, bra_out, brm_out, xa_out, xm_out, qkv_out, mix_out, pre_out, act_out,
     hid, mid, acc_a, acc_m, x_a, x_m, wbuf, act, pre, qkv, mix, rows_in, moved, turned,
     send_sem, recv_sem, local_sem) = refs
    p, c, t = place()
    mats, rows, width = shard_ref.shape
    tokens = hid.shape[1]
    half = rows // 2
    own_half = pl.multiple_of(c * half, 16)
    beside, above, twin = (p ^ 1, c, t), (p ^ 2, c, t), (p, 1 - c, t)
    chain = [(p, c, lax.rem(t + k, tps)) for k in range(1, tps)]
    crossed = [(p, 1 - c, lax.rem(t + k, tps)) for k in range(1, tps)]
    greet(chain + crossed + [beside, above, twin])
    links = Links(send_sem, recv_sem, local_sem)
    split = tps // 2
    low = jnp.bfloat16

    def rows_of(owner):
        return pl.ds(pl.multiple_of(owner * rows + own_half, 16), half)

    def block(m, k, owner):
        return full_ref.at[m, lax.rem(t + tps - k, tps), rows_of(owner)]

    def column(m, owner):
        return full_ref.at[m, :, rows_of(owner)]

    def own(m):
        return shard_ref.at[m, pl.ds(own_half, half)]

    keep, along, to_x, to_y, corner, to_twin = {}, {}, {}, {}, {}, {}
    for m in range(mats):
        keep[m] = links.local(own(m), block(m, 0, p))
        for k in range(tps):
            if k:
                along[m, k] = links.remote(lambda m=m, k=k: (own(m), block(m, 0, p), chain[k - 1]))()
            source = own(m) if k == 0 else block(m, k, p)
            to_x[m, k] = links.remote(lambda m=m, k=k, s=source: (s, block(m, k, p), beside))()
            to_y[m, k] = links.remote(lambda m=m, k=k, s=source: (s, block(m, k, p), above))()
            if k < split:
                corner[m, k] = links.remote(lambda m=m, k=k: (block(m, k, p ^ 1), block(m, k, p ^ 1), above))()
            else:
                corner[m, k] = links.remote(lambda m=m, k=k: (block(m, k, p ^ 2), block(m, k, p ^ 2), beside))()
        for which in range(4):
            owner = (p, p ^ 1, p ^ 2, p ^ 3)[which]
            to_twin[m, which] = links.remote(lambda m=m, o=owner: (column(m, o), column(m, o), twin))()

    def unit(step):
        ahead, lead = divmod(step + 3, tps)
        if (lead == 0 or step == 0) and ahead < mats:
            for m in ([0, ahead] if step == 0 and lead == 0 and ahead else [ahead]):
                for j in range(1, tps):
                    along[m, j].start()
        if step < mats * tps:
            m, k = divmod(step, tps)
            if k == 0:
                keep[m].start()
                to_x[m, 0].start()
                to_y[m, 0].start()
            else:
                along[m, k].wait_recv()
                to_x[m, k].start()
                to_y[m, k].start()
            if k == tps - 1:
                keep[m].wait()
                to_twin[m, 0].start()
        if 0 <= step - 3 < mats * tps:
            m, k = divmod(step - 3, tps)
            to_x[m, k].wait_recv()
            if k < split:
                corner[m, k].start()
            to_y[m, k].wait_recv()
            if k >= split:
                corner[m, k].start()
            if k == tps - 1:
                to_twin[m, 1].start()
                to_twin[m, 2].start()
        if 0 <= step - 6 < mats * tps:
            m, k = divmod(step - 6, tps)
            corner[m, k].wait_recv()
            if k == tps - 1:
                to_twin[m, 3].start()

    progress = [0]

    def tick():
        if progress[0] < mats * tps + 6:
            unit(progress[0])
            progress[0] += 1

    def arrive(m):
        while progress[0] < tps * m + tps + 6:
            tick()
        for which in range(4):
            to_twin[m, which].wait_recv()

    loads = {}

    def fetch(m, j):
        if (m, j) not in loads and m < mats:
            loads[m, j] = links.local(full_ref.at[m, j], wbuf.at[(m * tps + j) % SLOTS])
            loads[m, j].start()

    flock = frames // tps
    patches = rows_in.shape[1]
    strip = patches // tps

    def strip_of(owner):
        return pl.ds(pl.multiple_of(owner * strip, 16), strip)

    spread_rows = [
        links.remote(lambda k=k: (rows_ref.at[chain[k - 1][2]], rows_in.at[:, strip_of(t)], chain[k - 1]))() for k in range(1, tps)
    ]
    keep_rows = links.local(rows_ref.at[t], rows_in.at[:, strip_of(t)])
    for copy in spread_rows:
        copy.start()
    keep_rows.start()

    part = strip // 2
    chunk = turned.shape[2]
    cot_copies = []
    for g in range(part // chunk):
        there = pl.ds(pl.multiple_of((1 - c) * part + g * chunk, 16), chunk)
        here = pl.ds(pl.multiple_of(c * part + g * chunk, 16), chunk)
        cot_copies.append(links.remote(lambda g=g, s=there: (cot_ref.at[:, :, s], cot_out.at[g, :, c], twin))())
        cot_copies.append(links.local(cot_ref.at[:, :, here], cot_out.at[g, :, c]))
    for copy in cot_copies:
        copy.start()

    saves = []

    def save(src, dst):
        copy = links.local(src, dst)
        copy.start()
        return copy

    def by_rows(body, size=64):
        def one(i, carry):
            body(pl.ds(pl.multiple_of(i * size, size), size))
            return carry

        lax.fori_loop(0, tokens // size, one, 0)

    def loop(count, body):
        def one(i, carry):
            body(i)
            return carry

        lax.fori_loop(0, count, one, 0)

    pending = {}

    def settle(name):
        if name in pending:
            for copy in pending.pop(name):
                copy.wait()

    for level in range(layers):
        factor = [mod_ref[level, k : k + 1, :] for k in range(6)]
        hidden = hid.at[level]
        middle = mid.at[level]
        temporal = level % 2 == 1
        first, second, third = MATS * level, MATS * level + 1, MATS * level + 2
        if level == 0:
            tick()
            tick()
            for copy in spread_rows:
                copy.wait_recv()
            keep_rows.wait()
            for f in range(flock):
                loop(patches // 64, lambda i, f=f: hidden.__setitem__(
                    pl.ds(pl.multiple_of(f * patches + i * 64, 64), 64),
                    rows_in[f, pl.ds(pl.multiple_of(i * 64, 64), 64), :].astype(jnp.float32)))
        settle("x_a")

        def enter(span, source=hidden, to=x_a, s=factor[0], r=factor[1]):
            normed, _ = normalize(source[span, :])
            to[span, :] = (normed * (1.0 + r) + s).astype(low)

        by_rows(enter)
        pending["x_a"] = [save(x_a, xa_out.at[level])]
        saves.append(save(hidden, hid_out.at[level]))
        settle("acc_a")
        acc_a[...] = jnp.zeros_like(acc_a)
        arrive(first)
        fetch(first, 0)
        for j in range(tps):
            tick()
            fetch(first, j + 1) if j + 1 < tps else None
            loads[first, j].wait()
            w = wbuf.at[(first * tps + j) % SLOTS]
            settle(("qkv", j % 2))
            settle(("mix", j % 2))
            qkv_j, mix_j = qkv.at[j % 2], mix.at[j % 2]

            def attention(g):
                span = pl.ds(pl.multiple_of(g * GROUP, GROUP), GROUP)
                x = x_a[span, :]
                q = dot_nn(x, w[:, 0:LANES])
                q = jnp.where(lane_mask(q.shape, 0, wide), q, 0.0).astype(low)
                k = pltpu.roll(dot_nn(x, w[:, 256 : 256 + LANES]), LANES - 32, 1)
                k = jnp.where(lane_mask(k.shape, 0, wide), k, 0.0).astype(low)
                v = pltpu.roll(dot_nn(x, w[:, 512 : 512 + LANES]), 32, 1)
                v = jnp.where(lane_mask(v.shape, LANES - wide, LANES), v, 0.0).astype(low)
                qkv_j[span, 0:LANES] = q
                qkv_j[span, LANES : 2 * LANES] = k
                qkv_j[span, 2 * LANES : 3 * LANES] = v
                scores = dot_nt(head_stack(q, 0, heads), k) * (HD ** (-0.5))
                probs = softmax_rows(scores, chunk if temporal else 0).astype(low)
                mixed = head_merge(dot_nn(probs, v), LANES - wide, heads).astype(low)
                mix_j[span, :] = mixed
                for i in range(width // LANES):
                    at = slice(i * LANES, (i + 1) * LANES)
                    acc_a[span, at] += dot_nt(mixed, w[at, 768 : 768 + LANES])

            loop(tokens // GROUP, attention)
            pending["qkv", j % 2] = [save(qkv_j, qkv_out.at[level, j])]
            pending["mix", j % 2] = [save(mix_j, mix_out.at[level, j])]
        settle("x_m")

        def between(span, hidden=hidden, middle=middle, gate=factor[2], s=factor[3], r=factor[4]):
            rows_mid = hidden[span, :] + gate * acc_a[span, :]
            middle[span, :] = rows_mid
            normed, _ = normalize(rows_mid)
            x_m[span, :] = (normed * (1.0 + r) + s).astype(low)

        by_rows(between)
        pending["acc_a"] = [save(acc_a, bra_out.at[level])]
        pending["x_m"] = [save(x_m, xm_out.at[level])]
        saves.append(save(middle, mid_out.at[level]))
        arrive(second)
        fetch(second, 0)
        for j in range(tps):
            tick()
            fetch(second, j + 1) if j + 1 < tps else None
            loads[second, j].wait()
            w = wbuf.at[(second * tps + j) % SLOTS]
            settle(("pre", j % 2))
            settle(("act", j))
            pre_j, act_j = pre.at[j % 2], act.at[j]

            def raise_up(i):
                at = pl.ds(pl.multiple_of(i * LANES, LANES), LANES)
                value = dot_nn(x_m[...], w[:, at])
                pre_j[:, at] = value
                act_j[:, at] = jax.nn.gelu(value, approximate=True).astype(low)

            loop(width // LANES, raise_up)
            pending["pre", j % 2] = [save(pre_j, pre_out.at[level, j])]
            pending["act", j] = [save(act_j, act_out.at[level, j])]
        settle("acc_m")
        acc_m[...] = jnp.zeros_like(acc_m)
        arrive(third)
        fetch(third, 0)
        for j in range(tps):
            tick()
            fetch(third, j + 1) if j + 1 < tps else None
            loads[third, j].wait()
            w = wbuf.at[(third * tps + j) % SLOTS]
            act_j = act.at[j]

            def lower(i):
                at = pl.ds(pl.multiple_of(i * LANES, LANES), LANES)
                acc_m[:, at] += dot_nt(act_j[...], w[at, :])

            loop(width // LANES, lower)
        if level + 1 < layers:
            def leave(span, middle=middle, gate=factor[5]):
                moved[span, :] = (middle[span, :] + gate * acc_m[span, :]).astype(low)

            by_rows(leave)
            pending["acc_m"] = [save(acc_m, brm_out.at[level])]
            away, stay = [], []
            here = (t * 2 + c) * flock
            for g in range(part // chunk):
                for f in range(flock):
                    goal = turned.at[g, here + f]
                    for peer in [None, twin] + chain + crossed:
                        _, pc, pt = peer or (p, c, t)
                        first_row = f * patches + pt * strip + pc * part + g * chunk
                        piece = moved.at[pl.ds(pl.multiple_of(first_row, 16), chunk)]
                        if peer is None:
                            stay.append(links.local(piece, goal))
                        else:
                            away.append(links.remote(lambda s=piece, d=goal, q=peer: (s, d, q))())
            for copy in away + stay:
                copy.start()
            tick()
            for copy in away:
                copy.wait()
            for copy in stay:
                copy.wait()
            nxt = hid.at[level + 1]
            for g in range(part // chunk):
                for f in range(turned.shape[1]):
                    base = (g * turned.shape[1] + f) * chunk
                    nxt[base : base + chunk, :] = turned[g, f].astype(jnp.float32)
        else:
            for g in range(part // chunk):
                for f in range(turned.shape[1]):
                    base = (g * turned.shape[1] + f) * chunk
                    span = slice(base, base + chunk)
                    turned[g, f] = (middle[span, :] + factor[5] * acc_m[span, :]).astype(low)
            pending["acc_m"] = [save(acc_m, brm_out.at[level])]
            home_copies = []
            for g in range(part // chunk):
                for ts in range(tps):
                    for f in range(flock):
                        to = pl.ds(pl.multiple_of(c * part + g * chunk, 16), chunk)
                        theirs = turned.at[g, (ts * 2 + 1 - c) * flock + f]
                        ours = turned.at[g, (ts * 2 + c) * flock + f]
                        home_copies.append(links.remote(lambda s=theirs, d=out_ref.at[ts, f, to]: (s, d, twin))())
                        home_copies.append(links.local(ours, out_ref.at[ts, f, to]))
            for copy in home_copies:
                copy.start()
    while progress[0] < mats * tps + 6:
        tick()
    for copy in saves + cot_copies + home_copies:
        copy.wait()
    for name in list(pending):
        settle(name)
    for copy in spread_rows:
        copy.wait_send()
    for m in range(mats):
        for which in range(4):
            to_twin[m, which].wait_send()
        for k in range(tps):
            if k:
                along[m, k].wait_send()
            to_x[m, k].wait_send()
            to_y[m, k].wait_send()
            corner[m, k].wait_send()


def forward_pass(shards, rows, cot, modulation, mesh_shape, heads):
    tps, dps, cs = mesh_shape["tp"], mesh_shape["dp"], mesh_shape["ctx"]
    mats, depth, width = shards.shape
    layers = mats // MATS
    frames, strip = rows.shape[:2]
    flock, wide = frames // tps, heads * HD
    tokens = frames * strip
    patches = strip * tps
    chunk = GROUP // (frames * cs)
    groups = strip // cs // chunk
    low, wider = jnp.bfloat16, jnp.float32
    sds = jax.ShapeDtypeStruct
    whole = pl.BlockSpec(memory_space=pl.ANY)
    return pl.pallas_call(
        partial(forward_kernel, tps, (layers, frames, wide, heads)),
        out_shape=[
            sds((mats, tps, dps * depth, width), low),
            sds((tps, flock, strip, width), low),
            sds((groups, tps, cs, flock, chunk, width), low),
            sds((layers, tokens, width), wider),
            sds((layers, tokens, width), wider),
            sds((layers, tokens, width), wider),
            sds((layers, tokens, width), wider),
            sds((layers, tokens, width), low),
            sds((layers, tokens, width), low),
            sds((layers, tps, tokens, 3 * LANES), low),
            sds((layers, tps, tokens, LANES), low),
            sds((layers, tps, tokens, width), wider),
            sds((layers, tps, tokens, width), low),
        ],
        in_specs=[whole, whole, whole, pl.BlockSpec(memory_space=pltpu.VMEM)],
        out_specs=[whole] * 13,
        scratch_shapes=[
            pltpu.VMEM((layers, tokens, width), wider),
            pltpu.VMEM((layers, tokens, width), wider),
            pltpu.VMEM((tokens, width), wider),
            pltpu.VMEM((tokens, width), wider),
            pltpu.VMEM((tokens, width), low),
            pltpu.VMEM((tokens, width), low),
            pltpu.VMEM((SLOTS, dps * depth, width), low),
            pltpu.VMEM((tps, tokens, width), low),
            pltpu.VMEM((2, tokens, width), wider),
            pltpu.VMEM((2, tokens, 3 * LANES), low),
            pltpu.VMEM((2, tokens, LANES), low),
            pltpu.VMEM((flock, patches, width), low),
            pltpu.VMEM((tokens, width), low),
            pltpu.VMEM((groups, frames * cs, chunk, width), low),
            pltpu.SemaphoreType.DMA((200,)),
            pltpu.SemaphoreType.DMA((200,)),
            pltpu.SemaphoreType.DMA((120,)),
        ],
        compiler_params=pltpu.CompilerParams(
            collective_id=0, has_side_effects=True, vmem_limit_bytes=VMEM_LIMIT
        ),
        name="forward_pass",
    )(shards, rows.reshape(tps, flock, strip, width), cot.reshape(tps, flock, strip, width), modulation)


def add_into(acc, other):
    def one(i, carry):
        acc[i] = (acc[i].astype(jnp.float32) + other[i].astype(jnp.float32)).astype(acc.dtype)
        return carry

    lax.fori_loop(0, acc.shape[0], one, 0)


def reduce_kernel(tps, mats, *refs):
    grads = refs[:mats]
    out_ref = refs[mats]
    (tot, twin_in, beside_in, above_in, corner_x, corner_y, chain_in, last,
     send_sem, recv_sem, local_sem, free_sem) = refs[mats + 1:]
    p, c, t = place()
    rows = grads[0].shape[2]
    half = rows // 2
    mine = pl.ds(pl.multiple_of(c * half, half), half)
    theirs = pl.ds(pl.multiple_of((1 - c) * half, half), half)
    beside, above, twin = (p ^ 1, c, t), (p ^ 2, c, t), (p, 1 - c, t)
    chain = [(p, c, lax.rem(t + k, tps)) for k in range(1, tps)]
    greet(chain + [beside, above, twin])
    split = tps // 2
    TWIN, CX, CY, BX, BY, ZZ = 0, 1, 2, 3, 4, 5
    END = ZZ + tps - 1

    def copy(m, slot, src, dst, peer):
        return pltpu.make_async_remote_copy(
            src_ref=src, dst_ref=dst, send_sem=send_sem.at[m, slot], recv_sem=recv_sem.at[m, slot],
            device_id=peer, device_id_type=MESH,
        )

    def to_twin(m):
        return copy(m, TWIN, grads[m].at[:, :, theirs], twin_in.at[m % 2], twin)

    def load(m):
        return pltpu.make_async_copy(grads[m].at[:, :, mine], tot.at[m % DEPTH], local_sem.at[m, 0])

    def tot_at(m, owner):
        return tot.at[m % DEPTH, :, owner]

    def corner_to_x(m):
        return copy(m, CX, tot.at[m % DEPTH, pl.ds(0, split), p ^ 3], corner_x.at[m % 2], beside)

    def corner_to_y(m):
        return copy(m, CY, tot.at[m % DEPTH, pl.ds(split, tps - split), p ^ 3], corner_y.at[m % 2], above)

    def to_x(m):
        return copy(m, BX, tot_at(m, p ^ 1), beside_in.at[m % 2], beside)

    def to_y(m):
        return copy(m, BY, tot_at(m, p ^ 2), above_in.at[m % 2], above)

    def along(m, k):
        peer = chain[k - 1]
        return copy(m, ZZ + k - 1, tot.at[m % DEPTH, peer[2], p], chain_in.at[m % 2, k - 1], peer)

    def finish(m):
        return copy(m, END, last.at[m % 2], out_ref.at[m, mine], twin)

    def keep(m):
        return pltpu.make_async_copy(last.at[m % 2], out_ref.at[m, mine], local_sem.at[m, 1])

    def credit(slot, peer, m):
        if m + 2 < mats:
            pl.semaphore_signal(free_sem.at[slot], inc=1, device_id=peer, device_id_type=MESH)

    def spend(slot, m):
        if m >= 2:
            pl.semaphore_wait(free_sem.at[slot], 1)

    def sent(m):
        corner_to_x(m).wait_send()
        corner_to_y(m).wait_send()
        to_x(m).wait_send()
        to_y(m).wait_send()
        for k in range(1, tps):
            along(m, k).wait_send()

    def stage_a(m):
        if m >= DEPTH:
            sent(m - DEPTH)
        spend(TWIN, m)
        to_twin(m).start()
        load(m).start()

    def stage_b(m):
        load(m).wait()
        to_twin(m).wait_recv()
        for i in range(tps):
            add_into(tot.at[m % DEPTH, i], twin_in.at[m % 2, i])
        credit(TWIN, twin, m)
        spend(CX, m)
        corner_to_x(m).start()
        spend(CY, m)
        corner_to_y(m).start()

    def stage_c(m):
        corner_to_x(m).wait_recv()
        for i in range(split):
            add_into(tot.at[m % DEPTH, pl.ds(i, 1), p ^ 2], corner_x.at[m % 2, pl.ds(i, 1)])
        credit(CX, beside, m)
        spend(BY, m)
        to_y(m).start()
        corner_to_y(m).wait_recv()
        for i in range(tps - split):
            add_into(tot.at[m % DEPTH, pl.ds(split + i, 1), p ^ 1], corner_y.at[m % 2, pl.ds(i, 1)])
        credit(CY, above, m)
        spend(BX, m)
        to_x(m).start()

    def stage_d(m):
        to_x(m).wait_recv()
        add_into(tot.at[m % DEPTH, :, p], beside_in.at[m % 2])
        credit(BX, beside, m)
        to_y(m).wait_recv()
        add_into(tot.at[m % DEPTH, :, p], above_in.at[m % 2])
        credit(BY, above, m)
        for k in range(1, tps):
            spend(ZZ + k - 1, m)
            along(m, k).start()

    def stage_e(m):
        if m >= 2:
            finish(m - 2).wait_send()
            keep(m - 2).wait()
        for k in range(1, tps):
            along(m, k).wait_recv()
        total = tot[m % DEPTH, t, p].astype(jnp.float32)
        for k in range(1, tps):
            total = total + chain_in[m % 2, k - 1].astype(jnp.float32)
        last[m % 2] = total.astype(last.dtype)
        for k in range(1, tps):
            credit(ZZ + k - 1, (p, c, lax.rem(t + tps - k, tps)), m)
        finish(m).start()
        keep(m).start()

    stages = [stage_a, stage_b, stage_c, stage_d, stage_e]
    for step in range(mats + len(stages) - 1):
        for lag in reversed(range(len(stages))):
            if 0 <= step - lag < mats:
                stages[lag](step - lag)
    for m in range(mats):
        to_twin(m).wait_send()
        finish(m).wait_recv()
        if m >= mats - DEPTH:
            sent(m)
        if m >= mats - 2:
            finish(m).wait_send()
            keep(m).wait()


def sum_grads(grads):
    parts = []
    for grad in grads:
        part = lax.psum_scatter(grad, "tp", scatter_dimension=0, tiled=True)[0]
        part = lax.psum_scatter(part, "dp", scatter_dimension=0, tiled=True)
        parts.append(lax.psum(part, "ctx"))
    return jnp.stack(parts)


def reduce_grads(grads, mesh_shape):
    tps, dps = mesh_shape["tp"], mesh_shape["dp"]
    mats = len(grads)
    depth, width = grads[0].shape[1:]
    rows = depth // dps
    half = rows // 2
    low = grads[0].dtype
    split = tps // 2
    slots = 5 + tps
    return pl.pallas_call(
        partial(reduce_kernel, tps, mats),
        out_shape=jax.ShapeDtypeStruct((mats, rows, width), low),
        in_specs=[pl.BlockSpec(memory_space=pl.ANY)] * mats,
        out_specs=pl.BlockSpec(memory_space=pl.ANY),
        scratch_shapes=[
            pltpu.VMEM((DEPTH, tps, dps, half, width), low),
            pltpu.VMEM((2, tps, dps, half, width), low),
            pltpu.VMEM((2, tps, half, width), low),
            pltpu.VMEM((2, tps, half, width), low),
            pltpu.VMEM((2, split, half, width), low),
            pltpu.VMEM((2, tps - split, half, width), low),
            pltpu.VMEM((2, tps - 1, half, width), low),
            pltpu.VMEM((2, half, width), low),
            pltpu.SemaphoreType.DMA((mats, slots)),
            pltpu.SemaphoreType.DMA((mats, slots)),
            pltpu.SemaphoreType.DMA((mats, 2)),
            pltpu.SemaphoreType.REGULAR((slots,)),
        ],
        compiler_params=pltpu.CompilerParams(
            collective_id=1, has_side_effects=True, vmem_limit_bytes=VMEM_LIMIT
        ),
        name="reduce_grads",
    )(*[grad.reshape(tps, dps, rows, width) for grad in grads])


def pack(qkv, out, up, down):
    rows = qkv.shape[0]
    low = jnp.bfloat16
    first = jnp.concatenate([qkv.astype(low).reshape(rows, -1), out.astype(low).T], axis=1)
    return jnp.stack([first, up.astype(low), down.astype(low).T])


def unpack(first, second, third, like):
    rows, _, wide = like.shape
    cut = 3 * wide
    return (first[:, :cut].reshape(rows, 3, wide), first[:, cut:].T, second, third.T)


def frames_whole(rows):
    return lax.all_to_all(rows, "tp", 0, 1, tiled=True)


def frames_back(rows):
    return lax.all_to_all(rows, "tp", 1, 0, tiled=True)


def patches_whole(rows):
    return lax.all_to_all(rows, ("tp", "ctx"), 1, 0, tiled=True)


def patches_back(rows):
    return lax.all_to_all(rows, ("tp", "ctx"), 0, 1, tiled=True)


def columns_home(rows, mesh_shape):
    frames, patches, width = rows.shape
    tps, cs = mesh_shape["tp"], mesh_shape["ctx"]
    split = rows.reshape(tps, cs, frames // (tps * cs), patches, width)
    split = split.transpose(1, 0, 2, 3, 4).reshape(cs, frames // cs, patches, width)
    return lax.all_to_all(split, "ctx", 0, 2, tiled=True)[0]


def columns_away(rows, mesh_shape):
    tps, cs = mesh_shape["tp"], mesh_shape["ctx"]
    frames, patches, width = rows.shape
    split = lax.all_to_all(rows[None], "ctx", 2, 0, tiled=True)
    split = split.reshape(cs, tps, frames // tps, patches // cs, width).transpose(1, 0, 2, 3, 4)
    return split.reshape(frames * cs, patches // cs, width)


def per_device_plain(mesh_shape, inputs, conditioning, *states):
    masters, firsts, seconds, cotangent = states[:5], states[5:10], states[10:15], states[15]
    qkv_weight, out_weight, up_weight, down_weight, mod_weight = masters
    low = jnp.bfloat16
    highest = lax.Precision.HIGHEST
    layers = qkv_weight.shape[0]
    scale = HD ** (-0.5)
    dp_at, _, tp_at = place()
    tps, dps = mesh_shape["tp"], mesh_shape["dp"]
    rows = qkv_weight.shape[1]
    wide = qkv_weight.shape[3]
    heads = wide // HD
    width = inputs.shape[-1]

    shards = jnp.concatenate(
        [pack(qkv_weight[l], out_weight[l], up_weight[l], down_weight[l]) for l in range(layers)]
    )
    full = gather_weights(shards)

    cond_low = jax.nn.silu(conditioning).astype(low)
    cond_all = lax.all_gather(cond_low, "dp", axis=0, tiled=True)
    cond_mine = lax.dynamic_slice_in_dim(cond_all, dp_at * rows, rows, 1)
    mod_low = mod_weight.astype(low)
    mod_part = jnp.einsum("cd,ldke->clke", cond_mine, mod_low, preferred_element_type=jnp.float32)
    mod_part = lax.psum_scatter(mod_part, "dp", scatter_dimension=0, tiled=True)
    modulation = lax.all_gather(mod_part, "tp", axis=3, tiled=True)[0]

    hidden = frames_whole(inputs[0]).astype(jnp.float32)
    saved = []
    for level in range(layers):
        if level:
            if level % 2 == 1:
                hidden = patches_whole(hidden.astype(low)).astype(jnp.float32)
            else:
                hidden = patches_back(hidden.astype(low)).astype(jnp.float32)
        forms = SPATIAL_FORMS if level % 2 == 0 else TEMPORAL_FORMS
        first_w, up_w, down_w = full[MATS * level], full[MATS * level + 1], full[MATS * level + 2]
        factors = modulation[level]
        frames, patches = hidden.shape[:2]
        normed_a, rstd_a = normalize(hidden)
        attn_in = (normed_a * (1.0 + factors[1]) + factors[0]).astype(low)
        projected = jnp.einsum(
            "fpd,jde->fpje", attn_in, first_w[:, :, : 3 * wide], preferred_element_type=jnp.float32
        ).astype(low)
        projected = projected.reshape(frames, patches, tps, 3, heads, HD)
        query, key, value = (projected[:, :, :, s] for s in range(3))
        mixed, log_total = attend(query, key, value, forms, scale)
        mixed = mixed.reshape(frames, patches, tps, wide)
        branch_a = jnp.einsum(
            "fpje,jde->fpd", mixed, first_w[:, :, 3 * wide :], preferred_element_type=jnp.float32
        )
        middle = hidden + factors[2] * branch_a
        normed_m, rstd_m = normalize(middle)
        mlp_in = (normed_m * (1.0 + factors[4]) + factors[3]).astype(low)
        hidden_pre = jnp.einsum("fpd,jdh->fpjh", mlp_in, up_w, preferred_element_type=jnp.float32)
        hidden_act = jax.nn.gelu(hidden_pre, approximate=True).astype(low)
        branch_m = jnp.einsum("fpjh,jdh->fpd", hidden_act, down_w, preferred_element_type=jnp.float32)
        saved.append(
            (forms, first_w, up_w, down_w, factors, normed_a, rstd_a, attn_in, query, key, value,
             mixed, log_total, branch_a, normed_m, rstd_m, mlp_in, hidden_pre, hidden_act, branch_m)
        )
        hidden = middle + factors[5] * branch_m
    temporal_end = layers % 2 == 0
    output = hidden.astype(low)
    output = columns_home(output, mesh_shape) if temporal_end else frames_back(output)
    upstream = columns_away(cotangent[0], mesh_shape) if temporal_end else frames_whole(cotangent[0])
    upstream = upstream.astype(jnp.float32)

    grads = [None] * (MATS * layers)
    d_mods = [None] * layers
    for level in reversed(range(layers)):
        (forms, first_w, up_w, down_w, factors, normed_a, rstd_a, attn_in, query, key, value,
         mixed, log_total, branch_a, normed_m, rstd_m, mlp_in, hidden_pre, hidden_act, branch_m) = saved[level]
        frames, patches = upstream.shape[:2]
        d_gate_m = jnp.sum(upstream * branch_m, axis=(0, 1))
        d_branch_m = (factors[5] * upstream).astype(low)
        grads[MATS * level + 2] = jnp.einsum(
            "fpd,fpjh->jdh", d_branch_m, hidden_act, preferred_element_type=jnp.float32
        ).astype(low)
        d_act = jnp.einsum("fpd,jdh->fpjh", d_branch_m, down_w, preferred_element_type=jnp.float32)
        slope_pull = jax.vjp(partial(jax.nn.gelu, approximate=True), hidden_pre)[1]
        d_pre = slope_pull(d_act)[0].astype(low)
        grads[MATS * level + 1] = jnp.einsum(
            "fpd,fpjh->jdh", mlp_in, d_pre, preferred_element_type=jnp.float32
        ).astype(low)
        d_mlp_in = jnp.einsum("fpjh,jdh->fpd", d_pre, up_w, preferred_element_type=jnp.float32)
        d_shift_m = jnp.sum(d_mlp_in, axis=(0, 1))
        d_scale_m = jnp.sum(d_mlp_in * normed_m, axis=(0, 1))
        upstream = upstream + normalize_back(d_mlp_in * (1.0 + factors[4]), normed_m, rstd_m)
        d_gate_a = jnp.sum(upstream * branch_a, axis=(0, 1))
        d_branch_a = (factors[2] * upstream).astype(low)
        grad_out = jnp.einsum("fpd,fpje->jde", d_branch_a, mixed, preferred_element_type=jnp.float32)
        d_mixed = jnp.einsum(
            "fpd,jde->fpje", d_branch_a, first_w[:, :, 3 * wide :], preferred_element_type=jnp.float32
        ).astype(low)
        d_mixed = d_mixed.reshape(frames, patches, tps, heads, HD)
        d_parts = attend_back(query, key, value, d_mixed, log_total, forms, scale)
        d_projected = jnp.stack(d_parts, axis=3).astype(low).reshape(frames, patches, tps, 3 * wide)
        grad_qkv = jnp.einsum("fpd,fpje->jde", attn_in, d_projected, preferred_element_type=jnp.float32)
        grads[MATS * level] = jnp.concatenate([grad_qkv, grad_out], axis=2).astype(low)
        d_attn_in = jnp.einsum(
            "fpje,jde->fpd", d_projected, first_w[:, :, : 3 * wide], preferred_element_type=jnp.float32
        )
        d_shift_a = jnp.sum(d_attn_in, axis=(0, 1))
        d_scale_a = jnp.sum(d_attn_in * normed_a, axis=(0, 1))
        upstream = upstream + normalize_back(d_attn_in * (1.0 + factors[1]), normed_a, rstd_a)
        d_mods[level] = jnp.stack([d_shift_a, d_scale_a, d_gate_a, d_shift_m, d_scale_m, d_gate_m])
        if level:
            if level % 2 == 1:
                upstream = patches_back(upstream.astype(low)).astype(jnp.float32)
            else:
                upstream = patches_whole(upstream.astype(low)).astype(jnp.float32)
    input_grad = frames_back(upstream.astype(low)).astype(jnp.float32)

    reduced = sum_grads([grads[m] for m in reversed(range(MATS * layers))])
    reduced = reduced.astype(jnp.float32)

    d_mod = lax.psum(jnp.stack(d_mods)[None], ("ctx", "tp"))
    d_mod_all = lax.all_gather(d_mod, "dp", axis=0, tiled=True)
    d_mod_mine = lax.dynamic_slice_in_dim(d_mod_all, tp_at * wide, wide, 3)
    grad_mod = jnp.einsum("cd,clke->ldke", cond_mine.astype(jnp.float32), d_mod_mine, precision=highest)
    cond_part = jnp.einsum("clke,ldke->cd", d_mod_mine, mod_low.astype(jnp.float32), precision=highest)
    cond_part = lax.all_gather(lax.psum(cond_part, "tp"), "dp", axis=1, tiled=True)
    cond_total = lax.dynamic_slice_in_dim(cond_part, dp_at * conditioning.shape[0], conditioning.shape[0], 0)
    cond_grad = jax.vjp(jax.nn.silu, conditioning)[1](cond_total)[0]

    order = list(reversed(range(MATS * layers)))
    per_level = [
        unpack(*[reduced[order.index(MATS * level + kind)] for kind in range(MATS)], qkv_weight[level])
        for level in range(layers)
    ]
    stacked = [jnp.stack([per_level[level][kind] for level in range(layers)]) for kind in range(4)]
    stacked.append(grad_mod)
    squares = jnp.zeros((), jnp.float32)
    for grad in stacked:
        squares = squares + jnp.sum(grad * grad)
    grad_norm = jnp.sqrt(lax.psum(squares, ("dp", "tp")))
    coef = CLIP_MAX / jnp.maximum(grad_norm, CLIP_MAX)
    updates = [
        adam_update(masters[kind], firsts[kind], seconds[kind], stacked[kind], coef) for kind in range(5)
    ]
    return (output[None], input_grad[None], cond_grad, grad_norm) + tuple(
        updates[kind][part] for part in range(4) for kind in range(5)
    )


def per_device(mesh_shape, inputs, conditioning, *states):
    if not by_hand(mesh_shape, inputs, states[0]):
        return per_device_plain(mesh_shape, inputs, conditioning, *states)
    masters, firsts, seconds, cotangent = states[:5], states[5:10], states[10:15], states[15]
    qkv_weight, out_weight, up_weight, down_weight, mod_weight = masters
    low = jnp.bfloat16
    highest = lax.Precision.HIGHEST
    layers = qkv_weight.shape[0]
    scale = HD ** (-0.5)
    dp_at, _, tp_at = place()
    tps, dps = mesh_shape["tp"], mesh_shape["dp"]
    rows = qkv_weight.shape[1]
    wide = qkv_weight.shape[3]
    heads = wide // HD
    width = inputs.shape[-1]

    shards = jnp.concatenate(
        [pack(qkv_weight[l], out_weight[l], up_weight[l], down_weight[l]) for l in range(layers)]
    )
    cond_low = jax.nn.silu(conditioning).astype(low)
    cond_all = lax.all_gather(cond_low, "dp", axis=0, tiled=True)
    cond_mine = lax.dynamic_slice_in_dim(cond_all, dp_at * rows, rows, 1)
    mod_low = mod_weight.astype(low)
    mod_part = jnp.einsum("cd,ldke->clke", cond_mine, mod_low, preferred_element_type=jnp.float32)
    mod_part = lax.psum_scatter(mod_part, "dp", scatter_dimension=0, tiled=True)
    modulation = lax.all_gather(mod_part, "tp", axis=3, tiled=True)[0]
    (full, output, cot_rows, hid, mid, bra, brm, xa, xm, qkv, mix, pre, act) = forward_pass(
        shards, inputs[0], cotangent[0], modulation, mesh_shape, heads
    )
    groups, chunk = cot_rows.shape[0], cot_rows.shape[4]
    tokens = xa.shape[1]
    upstream = cot_rows.reshape(tokens, width).astype(jnp.float32)
    grads = [None] * (MATS * layers)
    d_mods = [None] * layers
    for level in reversed(range(layers)):
        first_w, up_w, down_w = full[MATS * level], full[MATS * level + 1], full[MATS * level + 2]
        factors = modulation[level]
        normed_a, rstd_a = normalize(hid[level])
        normed_m, rstd_m = normalize(mid[level])
        if level % 2 == 0:
            forms, view = ("jgqhe,jgkhe->jghqk", "jghqk,jgkhe->jgqhe", "jghqk,jgqhe->jgkhe"), (tps, groups, GROUP, heads, HD)
        else:
            forms = ("jgqphe,jgkphe->jgphqk", "jgphqk,jgkphe->jgqphe", "jgphqk,jgqphe->jgkphe")
            view = (tps, groups, GROUP // chunk, chunk, heads, HD)
        query = qkv[level][:, :, :wide].reshape(view)
        key = qkv[level][:, :, LANES : LANES + wide].reshape(view)
        value = qkv[level][:, :, 3 * LANES - wide :].reshape(view)
        mixed = mix[level][:, :, LANES - wide :]
        _, log_total = attend(query, key, value, forms, scale)
        d_gate_m = jnp.sum(upstream * brm[level], axis=0)
        d_branch_m = (factors[5] * upstream).astype(low)
        grads[MATS * level + 2] = jnp.einsum("nd,jnh->jdh", d_branch_m, act[level], preferred_element_type=jnp.float32).astype(low)
        d_act = jnp.einsum("nd,jdh->jnh", d_branch_m, down_w, preferred_element_type=jnp.float32)
        slope_pull = jax.vjp(partial(jax.nn.gelu, approximate=True), pre[level])[1]
        d_pre = slope_pull(d_act)[0].astype(low)
        grads[MATS * level + 1] = jnp.einsum("nd,jnh->jdh", xm[level], d_pre, preferred_element_type=jnp.float32).astype(low)
        d_mlp_in = jnp.einsum("jnh,jdh->nd", d_pre, up_w, preferred_element_type=jnp.float32)
        d_shift_m = jnp.sum(d_mlp_in, axis=0)
        d_scale_m = jnp.sum(d_mlp_in * normed_m, axis=0)
        upstream = upstream + normalize_back(d_mlp_in * (1.0 + factors[4]), normed_m, rstd_m)
        d_gate_a = jnp.sum(upstream * bra[level], axis=0)
        d_branch_a = (factors[2] * upstream).astype(low)
        grad_out = jnp.einsum("nd,jne->jde", d_branch_a, mixed, preferred_element_type=jnp.float32)
        d_mixed = jnp.einsum("nd,jde->jne", d_branch_a, first_w[:, :, 3 * wide :], preferred_element_type=jnp.float32)
        d_mixed = d_mixed.astype(low).reshape(view)
        d_parts = attend_back(query, key, value, d_mixed, log_total, forms, scale)
        d_projected = jnp.concatenate([d.reshape(tps, tokens, wide) for d in d_parts], axis=2).astype(low)
        grad_qkv = jnp.einsum("nd,jne->jde", xa[level], d_projected, preferred_element_type=jnp.float32)
        grads[MATS * level] = jnp.concatenate([grad_qkv, grad_out], axis=2).astype(low)
        d_attn_in = jnp.einsum("jne,jde->nd", d_projected, first_w[:, :, : 3 * wide], preferred_element_type=jnp.float32)
        d_shift_a = jnp.sum(d_attn_in, axis=0)
        d_scale_a = jnp.sum(d_attn_in * normed_a, axis=0)
        upstream = upstream + normalize_back(d_attn_in * (1.0 + factors[1]), normed_a, rstd_a)
        d_mods[level] = jnp.stack([d_shift_a, d_scale_a, d_gate_a, d_shift_m, d_scale_m, d_gate_m])
        if level == 1:
            part = upstream.astype(low).reshape(groups, GROUP // chunk, chunk, width).transpose(1, 0, 2, 3)
            upstream = patches_back(part.reshape(GROUP // chunk, groups * chunk, width)).astype(jnp.float32)
            upstream = upstream.reshape(tokens, width)
    frames, strip = inputs.shape[1:3]
    upstream = upstream.reshape(frames // tps, strip * tps, width)
    input_grad = frames_back(upstream.astype(low)).astype(jnp.float32)
    output = output.reshape(frames, strip, width)

    reduced = reduce_grads([grads[m] for m in reversed(range(MATS * layers))], mesh_shape)
    reduced = reduced.astype(jnp.float32)

    d_mod = lax.psum(jnp.stack(d_mods)[None], ("ctx", "tp"))
    d_mod_all = lax.all_gather(d_mod, "dp", axis=0, tiled=True)
    d_mod_mine = lax.dynamic_slice_in_dim(d_mod_all, tp_at * wide, wide, 3)
    grad_mod = jnp.einsum("cd,clke->ldke", cond_mine.astype(jnp.float32), d_mod_mine, precision=highest)
    cond_part = jnp.einsum("clke,ldke->cd", d_mod_mine, mod_low.astype(jnp.float32), precision=highest)
    cond_part = lax.all_gather(lax.psum(cond_part, "tp"), "dp", axis=1, tiled=True)
    cond_total = lax.dynamic_slice_in_dim(cond_part, dp_at * conditioning.shape[0], conditioning.shape[0], 0)
    cond_grad = jax.vjp(jax.nn.silu, conditioning)[1](cond_total)[0]

    order = list(reversed(range(MATS * layers)))
    per_level = [
        unpack(*[reduced[order.index(MATS * level + kind)] for kind in range(MATS)], qkv_weight[level])
        for level in range(layers)
    ]
    stacked = [jnp.stack([per_level[level][kind] for level in range(layers)]) for kind in range(4)]
    stacked.append(grad_mod)
    squares = jnp.zeros((), jnp.float32)
    for grad in stacked:
        squares = squares + jnp.sum(grad * grad)
    grad_norm = jnp.sqrt(lax.psum(squares, ("dp", "tp")))
    coef = CLIP_MAX / jnp.maximum(grad_norm, CLIP_MAX)
    updates = [
        adam_update(masters[kind], firsts[kind], seconds[kind], stacked[kind], coef) for kind in range(5)
    ]
    return (output[None], input_grad[None], cond_grad, grad_norm) + tuple(
        updates[kind][part] for part in range(4) for kind in range(5)
    )


def solution(mesh):
    weights = (
        P(None, "dp", None, "tp"),
        P(None, "tp", "dp"),
        P(None, "dp", "tp"),
        P(None, "tp", "dp"),
        P(None, "dp", None, "tp"),
    )
    rows = P("dp", "ctx", "tp", None)
    return jax.shard_map(
        partial(per_device, dict(mesh.shape)),
        mesh=mesh,
        in_specs=(rows, P("dp", None)) + weights * 3 + (rows,),
        out_specs=(rows, rows, P("dp", None), P()) + weights * 4,
        check_vma=False,
    )
```

```python
from functools import partial

import jax
import jax.numpy as jnp
from jax import lax
from jax.experimental import pallas as pl
from jax.experimental.pallas import tpu as pltpu
from jax.sharding import PartitionSpec as P

HD = 72
STEP = 5
EPS_NORM = 1e-06
LEARN_RATE = 0.03
DECAY_RATE = 0.1
BETA_ONE = 0.5
BETA_TWO = 0.5
ADAM_EPS = 1e-08
CLIP_MAX = 1.0
MESH = pl.DeviceIdType.MESH
MATS = 3
VMEM_LIMIT = 60 * 1024 * 1024
LANES = 384
SLOTS = 4
GROUP = 256
SPATIAL_FORMS = ("fqjhe,fkjhe->fjhqk", "fjhqk,fkjhe->fqjhe", "fjhqk,fqjhe->fkjhe")
TEMPORAL_FORMS = ("qpjhe,kpjhe->pjhqk", "pjhqk,kpjhe->qpjhe", "pjhqk,qpjhe->kpjhe")


def normalize(rows):
    centred = rows - jnp.mean(rows, axis=-1, keepdims=True)
    rstd = lax.rsqrt(jnp.mean(centred * centred, axis=-1, keepdims=True) + EPS_NORM)
    return (centred * rstd, rstd)


def normalize_back(grad, normed, rstd):
    return rstd * (
        grad
        - jnp.mean(grad, axis=-1, keepdims=True)
        - normed * jnp.mean(grad * normed, axis=-1, keepdims=True)
    )


def attend(query, key, value, forms, scale):
    scores = jnp.einsum(forms[0], query, key, preferred_element_type=jnp.float32) * scale
    top = jnp.max(scores, axis=-1, keepdims=True)
    expo = jnp.exp(scores - top)
    total = jnp.sum(expo, axis=-1, keepdims=True)
    probs = (expo / total).astype(jnp.bfloat16)
    mixed = jnp.einsum(forms[1], probs, value, preferred_element_type=jnp.float32)
    return (mixed.astype(jnp.bfloat16), top + jnp.log(total))


def attend_back(query, key, value, d_mixed, log_total, forms, scale):
    scores = jnp.einsum(forms[0], query, key, preferred_element_type=jnp.float32) * scale
    probs = jnp.exp(scores - log_total)
    d_probs = jnp.einsum(forms[0], d_mixed, value, preferred_element_type=jnp.float32)
    d_scores = (probs * (d_probs - jnp.sum(probs * d_probs, axis=-1, keepdims=True))).astype(
        jnp.bfloat16
    )
    d_value = jnp.einsum(
        forms[2], probs.astype(jnp.bfloat16), d_mixed, preferred_element_type=jnp.float32
    )
    d_query = jnp.einsum(forms[1], d_scores, key, preferred_element_type=jnp.float32) * scale
    d_key = jnp.einsum(forms[2], d_scores, query, preferred_element_type=jnp.float32) * scale
    return (d_query, d_key, d_value)


def adam_update(master, first, second, grad, coef):
    clipped = coef * grad
    first_new = BETA_ONE * first + (1.0 - BETA_ONE) * clipped
    second_new = BETA_TWO * second + (1.0 - BETA_TWO) * clipped * clipped
    first_hat = first_new / (1.0 - BETA_ONE**STEP)
    second_hat = second_new / (1.0 - BETA_TWO**STEP)
    master_new = master - LEARN_RATE * (
        first_hat / (jnp.sqrt(second_hat) + ADAM_EPS) + DECAY_RATE * master
    )
    return (master_new, master_new.astype(jnp.bfloat16), first_new, second_new)


def place():
    return lax.axis_index("dp"), lax.axis_index("ctx"), lax.axis_index("tp")


def greet(peers):
    barrier = pltpu.get_barrier_semaphore()
    for peer in peers:
        pl.semaphore_signal(barrier, inc=1, device_id=peer, device_id_type=MESH)
    pl.semaphore_wait(barrier, len(peers))


def by_hand(mesh_shape, inputs, qkv_weight):
    tps, cs = mesh_shape["tp"], mesh_shape["ctx"]
    layers, rows, _, wide = qkv_weight.shape
    clips, frames, strip, width = inputs.shape
    return (
        mesh_shape["dp"] == 4 and cs == 2 and tps == 4 and clips == 1 and layers == 2 and rows % 32 == 0
        and wide == 4 * HD and 4 * wide == width and width % LANES == 0 and frames == 2 * tps
        and strip * tps == GROUP and frames * cs == 16 and strip == 64
    )


def gather_weights(shards):
    full = lax.all_gather(shards, "dp", axis=1, tiled=True)
    return lax.all_gather(full, "tp", axis=1, tiled=False)


class Links:
    def __init__(self, send_sem, recv_sem, local_sem):
        self.send_sem, self.recv_sem, self.local_sem = send_sem, recv_sem, local_sem
        self.used, self.used_local = 0, 0

    def remote(self, make):
        at = self.used
        self.used += 1

        def build(*args):
            src, dst, peer = make(*args)
            return pltpu.make_async_remote_copy(
                src_ref=src, dst_ref=dst, send_sem=self.send_sem.at[at], recv_sem=self.recv_sem.at[at],
                device_id=peer, device_id_type=MESH,
            )

        return build

    def local(self, src, dst):
        at = self.used_local
        self.used_local += 1
        return pltpu.make_async_copy(src, dst, self.local_sem.at[at])


def lane_mask(shape, low, high):
    lane = lax.broadcasted_iota(jnp.int32, shape, 1)
    return jnp.logical_and(lane >= low, lane < high)


def dot_nn(a, b):
    return lax.dot_general(a, b, (((1,), (0,)), ((), ())), preferred_element_type=jnp.float32)


def dot_nt(a, b):
    return lax.dot_general(a, b, (((1,), (1,)), ((), ())), preferred_element_type=jnp.float32)


def dot_tn(a, b):
    return lax.dot_general(a, b, (((0,), (0,)), ((), ())), preferred_element_type=jnp.float32)


def softmax_rows(scores, columns):
    if columns:
        rows = lax.broadcasted_iota(jnp.int32, scores.shape, 0)
        cols = lax.broadcasted_iota(jnp.int32, scores.shape, 1)
        scores = jnp.where((rows & (columns - 1)) == (cols & (columns - 1)), scores, -1e30)
    top = jnp.max(scores, axis=-1, keepdims=True)
    expo = jnp.exp(scores - top)
    return expo * (1.0 / jnp.sum(expo, axis=-1, keepdims=True))


def head_stack(rows, first, heads):
    return jnp.concatenate(
        [jnp.where(lane_mask(rows.shape, first + h * HD, first + (h + 1) * HD), rows, jnp.zeros_like(rows)) for h in range(heads)],
        axis=0,
    )


def head_merge(stacked, first, heads):
    size = stacked.shape[0] // heads
    total = jnp.zeros((size, stacked.shape[1]), stacked.dtype)
    for h in range(heads):
        part = stacked[h * size : (h + 1) * size]
        total = jnp.where(lane_mask(part.shape, first + h * HD, first + (h + 1) * HD), part, total)
    return total


def forward_kernel(tps, geometry, *refs):
    layers, frames, wide, heads = geometry
    (shard_ref, rows_ref, cot_ref, mod_ref,
     full_ref, out_ref, cot_out, hid_out, mid_out, bra_out, brm_out, xa_out, xm_out, qkv_out, mix_out, pre_out, act_out,
     hid, mid, acc_a, acc_m, x_a, x_m, wbuf, act, pre, qkv, mix, rows_in, moved, turned,
     send_sem, recv_sem, local_sem) = refs
    p, c, t = place()
    mats, rows, width = shard_ref.shape
    tokens = hid.shape[1]
    half = rows // 2
    own_half = pl.multiple_of(c * half, 16)
    beside, above, twin = (p ^ 1, c, t), (p ^ 2, c, t), (p, 1 - c, t)
    chain = [(p, c, lax.rem(t + k, tps)) for k in range(1, tps)]
    crossed = [(p, 1 - c, lax.rem(t + k, tps)) for k in range(1, tps)]
    greet(chain + crossed + [beside, above, twin])
    links = Links(send_sem, recv_sem, local_sem)
    split = tps // 2
    low = jnp.bfloat16

    def rows_of(owner):
        return pl.ds(pl.multiple_of(owner * rows + own_half, 16), half)

    def block(m, k, owner):
        return full_ref.at[m, lax.rem(t + tps - k, tps), rows_of(owner)]

    def column(m, owner):
        return full_ref.at[m, :, rows_of(owner)]

    def own(m):
        return shard_ref.at[m, pl.ds(own_half, half)]

    keep, along, to_x, to_y, corner, to_twin = {}, {}, {}, {}, {}, {}
    for m in range(mats):
        keep[m] = links.local(own(m), block(m, 0, p))
        for k in range(tps):
            if k:
                along[m, k] = links.remote(lambda m=m, k=k: (own(m), block(m, 0, p), chain[k - 1]))()
            source = own(m) if k == 0 else block(m, k, p)
            to_x[m, k] = links.remote(lambda m=m, k=k, s=source: (s, block(m, k, p), beside))()
            to_y[m, k] = links.remote(lambda m=m, k=k, s=source: (s, block(m, k, p), above))()
            if k < split:
                corner[m, k] = links.remote(lambda m=m, k=k: (block(m, k, p ^ 1), block(m, k, p ^ 1), above))()
            else:
                corner[m, k] = links.remote(lambda m=m, k=k: (block(m, k, p ^ 2), block(m, k, p ^ 2), beside))()
        for which in range(4):
            owner = (p, p ^ 1, p ^ 2, p ^ 3)[which]
            to_twin[m, which] = links.remote(lambda m=m, o=owner: (column(m, o), column(m, o), twin))()

    def unit(step):
        ahead, lead = divmod(step + 3, tps)
        if (lead == 0 or step == 0) and ahead < mats:
            for m in ([0, ahead] if step == 0 and lead == 0 and ahead else [ahead]):
                for j in range(1, tps):
                    along[m, j].start()
        if step < mats * tps:
            m, k = divmod(step, tps)
            if k == 0:
                keep[m].start()
                to_x[m, 0].start()
                to_y[m, 0].start()
            else:
                along[m, k].wait_recv()
                to_x[m, k].start()
                to_y[m, k].start()
            if k == tps - 1:
                keep[m].wait()
                to_twin[m, 0].start()
        if 0 <= step - 3 < mats * tps:
            m, k = divmod(step - 3, tps)
            to_x[m, k].wait_recv()
            if k < split:
                corner[m, k].start()
            to_y[m, k].wait_recv()
            if k >= split:
                corner[m, k].start()
            if k == tps - 1:
                to_twin[m, 1].start()
                to_twin[m, 2].start()
        if 0 <= step - 6 < mats * tps:
            m, k = divmod(step - 6, tps)
            corner[m, k].wait_recv()
            if k == tps - 1:
                to_twin[m, 3].start()

    progress = [0]

    def tick():
        if progress[0] < mats * tps + 6:
            unit(progress[0])
            progress[0] += 1

    def arrive(m):
        while progress[0] < tps * m + tps + 6:
            tick()
        for which in range(4):
            to_twin[m, which].wait_recv()

    loads = {}

    def fetch(m, j):
        if (m, j) not in loads and m < mats:
            loads[m, j] = links.local(full_ref.at[m, j], wbuf.at[(m * tps + j) % SLOTS])
            loads[m, j].start()

    flock = frames // tps
    patches = rows_in.shape[1]
    strip = patches // tps

    def strip_of(owner):
        return pl.ds(pl.multiple_of(owner * strip, 16), strip)

    spread_rows = [
        links.remote(lambda k=k: (rows_ref.at[chain[k - 1][2]], rows_in.at[:, strip_of(t)], chain[k - 1]))() for k in range(1, tps)
    ]
    keep_rows = links.local(rows_ref.at[t], rows_in.at[:, strip_of(t)])
    for copy in spread_rows:
        copy.start()
    keep_rows.start()

    part = strip // 2
    chunk = turned.shape[2]
    cot_copies = []
    for g in range(part // chunk):
        there = pl.ds(pl.multiple_of((1 - c) * part + g * chunk, 16), chunk)
        here = pl.ds(pl.multiple_of(c * part + g * chunk, 16), chunk)
        cot_copies.append(links.remote(lambda g=g, s=there: (cot_ref.at[:, :, s], cot_out.at[g, :, c], twin))())
        cot_copies.append(links.local(cot_ref.at[:, :, here], cot_out.at[g, :, c]))
    for copy in cot_copies:
        copy.start()

    saves = []

    def save(src, dst):
        copy = links.local(src, dst)
        copy.start()
        return copy

    def by_rows(body, size=64):
        def one(i, carry):
            body(pl.ds(pl.multiple_of(i * size, size), size))
            return carry

        lax.fori_loop(0, tokens // size, one, 0)

    def loop(count, body):
        def one(i, carry):
            body(i)
            return carry

        lax.fori_loop(0, count, one, 0)

    pending = {}

    def settle(name):
        if name in pending:
            for copy in pending.pop(name):
                copy.wait()

    for level in range(layers):
        factor = [mod_ref[level, k : k + 1, :] for k in range(6)]
        hidden = hid.at[level]
        middle = mid.at[level]
        temporal = level % 2 == 1
        first, second, third = MATS * level, MATS * level + 1, MATS * level + 2
        if level == 0:
            tick()
            tick()
            for copy in spread_rows:
                copy.wait_recv()
            keep_rows.wait()
            for f in range(flock):
                loop(patches // 64, lambda i, f=f: hidden.__setitem__(
                    pl.ds(pl.multiple_of(f * patches + i * 64, 64), 64),
                    rows_in[f, pl.ds(pl.multiple_of(i * 64, 64), 64), :].astype(jnp.float32)))
        settle("x_a")

        def enter(span, source=hidden, to=x_a, s=factor[0], r=factor[1]):
            normed, _ = normalize(source[span, :])
            to[span, :] = (normed * (1.0 + r) + s).astype(low)

        by_rows(enter)
        pending["x_a"] = [save(x_a, xa_out.at[level])]
        saves.append(save(hidden, hid_out.at[level]))
        settle("acc_a")
        acc_a[...] = jnp.zeros_like(acc_a)
        arrive(first)
        fetch(first, 0)
        for j in range(tps):
            tick()
            fetch(first, j + 1) if j + 1 < tps else None
            loads[first, j].wait()
            w = wbuf.at[(first * tps + j) % SLOTS]
            settle(("qkv", j % 2))
            settle(("mix", j % 2))
            qkv_j, mix_j = qkv.at[j % 2], mix.at[j % 2]

            def attention(g):
                span = pl.ds(pl.multiple_of(g * GROUP, GROUP), GROUP)
                x = x_a[span, :]
                q = dot_nn(x, w[:, 0:LANES])
                q = jnp.where(lane_mask(q.shape, 0, wide), q, 0.0).astype(low)
                k = pltpu.roll(dot_nn(x, w[:, 256 : 256 + LANES]), LANES - 32, 1)
                k = jnp.where(lane_mask(k.shape, 0, wide), k, 0.0).astype(low)
                v = pltpu.roll(dot_nn(x, w[:, 512 : 512 + LANES]), 32, 1)
                v = jnp.where(lane_mask(v.shape, LANES - wide, LANES), v, 0.0).astype(low)
                qkv_j[span, 0:LANES] = q
                qkv_j[span, LANES : 2 * LANES] = k
                qkv_j[span, 2 * LANES : 3 * LANES] = v
                scores = dot_nt(head_stack(q, 0, heads), k) * (HD ** (-0.5))
                probs = softmax_rows(scores, chunk if temporal else 0).astype(low)
                mixed = head_merge(dot_nn(probs, v), LANES - wide, heads).astype(low)
                mix_j[span, :] = mixed
                for i in range(width // LANES):
                    at = slice(i * LANES, (i + 1) * LANES)
                    acc_a[span, at] += dot_nt(mixed, w[at, 768 : 768 + LANES])

            loop(tokens // GROUP, attention)
            pending["qkv", j % 2] = [save(qkv_j, qkv_out.at[level, j])]
            pending["mix", j % 2] = [save(mix_j, mix_out.at[level, j])]
        settle("x_m")

        def between(span, hidden=hidden, middle=middle, gate=factor[2], s=factor[3], r=factor[4]):
            rows_mid = hidden[span, :] + gate * acc_a[span, :]
            middle[span, :] = rows_mid
            normed, _ = normalize(rows_mid)
            x_m[span, :] = (normed * (1.0 + r) + s).astype(low)

        by_rows(between)
        pending["acc_a"] = [save(acc_a, bra_out.at[level])]
        pending["x_m"] = [save(x_m, xm_out.at[level])]
        saves.append(save(middle, mid_out.at[level]))
        arrive(second)
        fetch(second, 0)
        for j in range(tps):
            tick()
            fetch(second, j + 1) if j + 1 < tps else None
            loads[second, j].wait()
            w = wbuf.at[(second * tps + j) % SLOTS]
            settle(("pre", j % 2))
            settle(("act", j))
            pre_j, act_j = pre.at[j % 2], act.at[j]

            def raise_up(i):
                at = pl.ds(pl.multiple_of(i * LANES, LANES), LANES)
                value = dot_nn(x_m[...], w[:, at])
                pre_j[:, at] = value
                act_j[:, at] = jax.nn.gelu(value, approximate=True).astype(low)

            loop(width // LANES, raise_up)
            pending["pre", j % 2] = [save(pre_j, pre_out.at[level, j])]
            pending["act", j] = [save(act_j, act_out.at[level, j])]
        settle("acc_m")
        acc_m[...] = jnp.zeros_like(acc_m)
        arrive(third)
        fetch(third, 0)
        for j in range(tps):
            tick()
            fetch(third, j + 1) if j + 1 < tps else None
            loads[third, j].wait()
            w = wbuf.at[(third * tps + j) % SLOTS]
            act_j = act.at[j]

            def lower(i):
                at = pl.ds(pl.multiple_of(i * LANES, LANES), LANES)
                acc_m[:, at] += dot_nt(act_j[...], w[at, :])

            loop(width // LANES, lower)
        if level + 1 < layers:
            def leave(span, middle=middle, gate=factor[5]):
                moved[span, :] = (middle[span, :] + gate * acc_m[span, :]).astype(low)

            by_rows(leave)
            pending["acc_m"] = [save(acc_m, brm_out.at[level])]
            away, stay = [], []
            here = (t * 2 + c) * flock
            for g in range(part // chunk):
                for f in range(flock):
                    goal = turned.at[g, here + f]
                    for peer in [None, twin] + chain + crossed:
                        _, pc, pt = peer or (p, c, t)
                        first_row = f * patches + pt * strip + pc * part + g * chunk
                        piece = moved.at[pl.ds(pl.multiple_of(first_row, 16), chunk)]
                        if peer is None:
                            stay.append(links.local(piece, goal))
                        else:
                            away.append(links.remote(lambda s=piece, d=goal, q=peer: (s, d, q))())
            for copy in away + stay:
                copy.start()
            tick()
            for copy in away:
                copy.wait()
            for copy in stay:
                copy.wait()
            nxt = hid.at[level + 1]
            for g in range(part // chunk):
                for f in range(turned.shape[1]):
                    base = (g * turned.shape[1] + f) * chunk
                    nxt[base : base + chunk, :] = turned[g, f].astype(jnp.float32)
        else:
            for g in range(part // chunk):
                for f in range(turned.shape[1]):
                    base = (g * turned.shape[1] + f) * chunk
                    span = slice(base, base + chunk)
                    turned[g, f] = (middle[span, :] + factor[5] * acc_m[span, :]).astype(low)
            pending["acc_m"] = [save(acc_m, brm_out.at[level])]
            home_copies = []
            for g in range(part // chunk):
                for ts in range(tps):
                    for f in range(flock):
                        to = pl.ds(pl.multiple_of(c * part + g * chunk, 16), chunk)
                        theirs = turned.at[g, (ts * 2 + 1 - c) * flock + f]
                        ours = turned.at[g, (ts * 2 + c) * flock + f]
                        home_copies.append(links.remote(lambda s=theirs, d=out_ref.at[ts, f, to]: (s, d, twin))())
                        home_copies.append(links.local(ours, out_ref.at[ts, f, to]))
            for copy in home_copies:
                copy.start()
    while progress[0] < mats * tps + 6:
        tick()
    for copy in saves + cot_copies + home_copies:
        copy.wait()
    for name in list(pending):
        settle(name)
    for copy in spread_rows:
        copy.wait_send()
    for m in range(mats):
        for which in range(4):
            to_twin[m, which].wait_send()
        for k in range(tps):
            if k:
                along[m, k].wait_send()
            to_x[m, k].wait_send()
            to_y[m, k].wait_send()
            corner[m, k].wait_send()


def forward_pass(shards, rows, cot, modulation, mesh_shape, heads):
    tps, dps, cs = mesh_shape["tp"], mesh_shape["dp"], mesh_shape["ctx"]
    mats, depth, width = shards.shape
    layers = mats // MATS
    frames, strip = rows.shape[:2]
    flock, wide = frames // tps, heads * HD
    tokens = frames * strip
    patches = strip * tps
    chunk = GROUP // (frames * cs)
    groups = strip // cs // chunk
    low, wider = jnp.bfloat16, jnp.float32
    sds = jax.ShapeDtypeStruct
    whole = pl.BlockSpec(memory_space=pl.ANY)
    return pl.pallas_call(
        partial(forward_kernel, tps, (layers, frames, wide, heads)),
        out_shape=[
            sds((mats, tps, dps * depth, width), low),
            sds((tps, flock, strip, width), low),
            sds((groups, tps, cs, flock, chunk, width), low),
            sds((layers, tokens, width), wider),
            sds((layers, tokens, width), wider),
            sds((layers, tokens, width), wider),
            sds((layers, tokens, width), wider),
            sds((layers, tokens, width), low),
            sds((layers, tokens, width), low),
            sds((layers, tps, tokens, 3 * LANES), low),
            sds((layers, tps, tokens, LANES), low),
            sds((layers, tps, tokens, width), wider),
            sds((layers, tps, tokens, width), low),
        ],
        in_specs=[whole, whole, whole, pl.BlockSpec(memory_space=pltpu.VMEM)],
        out_specs=[whole] * 13,
        scratch_shapes=[
            pltpu.VMEM((layers, tokens, width), wider),
            pltpu.VMEM((layers, tokens, width), wider),
            pltpu.VMEM((tokens, width), wider),
            pltpu.VMEM((tokens, width), wider),
            pltpu.VMEM((tokens, width), low),
            pltpu.VMEM((tokens, width), low),
            pltpu.VMEM((SLOTS, dps * depth, width), low),
            pltpu.VMEM((tps, tokens, width), low),
            pltpu.VMEM((2, tokens, width), wider),
            pltpu.VMEM((2, tokens, 3 * LANES), low),
            pltpu.VMEM((2, tokens, LANES), low),
            pltpu.VMEM((flock, patches, width), low),
            pltpu.VMEM((tokens, width), low),
            pltpu.VMEM((groups, frames * cs, chunk, width), low),
            pltpu.SemaphoreType.DMA((200,)),
            pltpu.SemaphoreType.DMA((200,)),
            pltpu.SemaphoreType.DMA((120,)),
        ],
        compiler_params=pltpu.CompilerParams(
            collective_id=0, has_side_effects=True, vmem_limit_bytes=VMEM_LIMIT
        ),
        name="forward_pass",
    )(shards, rows.reshape(tps, flock, strip, width), cot.reshape(tps, flock, strip, width), modulation)


def gelu_slope(v):
    root, cubic = 0.7978845608028654, 0.044715
    square = v * v
    bend = jnp.tanh(root * v * (1.0 + cubic * square))
    return 0.5 * (1.0 + bend) + 0.5 * v * (1.0 - bend * bend) * (root * (1.0 + 3.0 * cubic * square))


def backward_kernel(tps, geometry, *refs):
    layers, frames, wide, heads = geometry
    (full_ref, cot_ref, mod_ref, hid_ref, mid_ref, bra_ref, brm_ref, xa_ref, xm_ref, qkv_ref, mix_ref, pre_ref, act_ref,
     red_ref, home_ref, dmod_ref,
     tot, grad, twin_in, corner_in, beside_in, above_in, chain_in, last,
     g, dacc, lhs, x, wbuf, side, pre, dpre, mix, branch, base, dproj, arrived,
     send_sem, recv_sem, local_sem, free_sem) = refs
    p, c, t = place()
    mats = full_ref.shape[0]
    half, width = last.shape
    rows = 2 * half
    depth = full_ref.shape[2]
    dps = depth // rows
    tokens = g.shape[0]
    low = jnp.bfloat16
    mine = pl.ds(pl.multiple_of(c * half, 16), half)
    theirs = pl.ds(pl.multiple_of((1 - c) * half, 16), half)
    beside, above, twin = (p ^ 1, c, t), (p ^ 2, c, t), (p, 1 - c, t)
    chain = [(p, c, lax.rem(t + k, tps)) for k in range(1, tps)]
    crossed = [(p, 1 - c, lax.rem(t + k, tps)) for k in range(1, tps)]
    greet(chain + crossed + [beside, above, twin])
    links = Links(send_sem, recv_sem, local_sem)
    split = tps // 2
    units = mats * tps
    kinds = [(level, kind) for level in reversed(range(layers)) for kind in (2, 1, 0)]

    TWIN, CORNER, BESIDE, ABOVE, CHAIN = 0, tps, 2 * tps, 3 * tps, 4 * tps

    def credit(slot, peer, u, gap):
        if u + gap < units:
            pl.semaphore_signal(free_sem.at[slot], inc=1, device_id=peer, device_id_type=MESH)

    def spend(slot, u, gap):
        if u >= gap:
            pl.semaphore_wait(free_sem.at[slot], 1)

    to_twin, to_corner, to_x, to_y, along, finish, keep = {}, {}, {}, {}, {}, {}, {}
    for u in range(units):
        n, i = divmod(u, tps)
        here = tot.at[n % 2, i]
        to_twin[u] = links.remote(lambda u=u: (grad.at[u % 2, :, theirs], twin_in.at[u % 2], twin))()
        via = beside if i < split else above
        to_corner[u] = links.remote(lambda h=here, i=i, v=via: (h.at[p ^ 3], corner_in.at[i], v))()
        to_x[u] = links.remote(lambda h=here, i=i: (h.at[p ^ 1], beside_in.at[i], beside))()
        to_y[u] = links.remote(lambda h=here, i=i: (h.at[p ^ 2], above_in.at[i], above))()
        if i < tps - 1:
            along[u] = links.remote(lambda h=here, i=i: (h.at[p], chain_in.at[i], chain[i]))()
        else:
            level, kind = kinds[n]
            goal = red_ref.at[MATS * level + kind, mine]
            finish[n] = links.remote(lambda d=goal: (last, d, twin))()
            keep[n] = links.local(last, goal)

    def plus(a, b):
        return (a.astype(jnp.float32) + b.astype(jnp.float32)).astype(low)

    def release(u):
        if u >= 2:
            to_twin[u - 2].wait_send()
        n, i = divmod(u, tps)
        if n >= 2:
            old = u - 2 * tps
            to_corner[old].wait_send()
            to_x[old].wait_send()
            to_y[old].wait_send()
            if i < tps - 1:
                along[old].wait_send()

    def stage_a(u):
        spend(TWIN + u % 2, u, 2)
        to_twin[u].start()

    def stage_b(u):
        n, i = divmod(u, tps)
        to_twin[u].wait_recv()
        here = tot.at[n % 2, i]

        def one(q, carry):
            here[q] = plus(grad[u % 2, q, mine], twin_in[u % 2, q])
            return carry

        lax.fori_loop(0, dps, one, 0)
        credit(TWIN + u % 2, twin, u, 2)
        spend(CORNER + i, u, tps)
        to_corner[u].start()
        if i < split:
            spend(BESIDE + i, u, tps)
            to_x[u].start()
        else:
            spend(ABOVE + i, u, tps)
            to_y[u].start()

    def stage_c(u):
        n, i = divmod(u, tps)
        here = tot.at[n % 2, i]
        to_corner[u].wait_recv()
        if i < split:
            here[p ^ 2] = plus(here[p ^ 2], corner_in[i])
            credit(CORNER + i, beside, u, tps)
            spend(ABOVE + i, u, tps)
            to_y[u].start()
        else:
            here[p ^ 1] = plus(here[p ^ 1], corner_in[i])
            credit(CORNER + i, above, u, tps)
            spend(BESIDE + i, u, tps)
            to_x[u].start()

    def stage_d(u):
        n, i = divmod(u, tps)
        here = tot.at[n % 2, i]
        to_x[u].wait_recv()
        to_y[u].wait_recv()
        own = here[p].astype(jnp.float32) + beside_in[i].astype(jnp.float32) + above_in[i].astype(jnp.float32)
        credit(BESIDE + i, beside, u, tps)
        credit(ABOVE + i, above, u, tps)
        if i < tps - 1:
            here[p] = own.astype(low)
            spend(CHAIN + i, u, tps)
            along[u].start()
            return
        for k in range(tps - 1):
            along[u - tps + 1 + k].wait_recv()
            own = own + chain_in[k].astype(jnp.float32)
            credit(CHAIN + k, (p, c, lax.rem(t + tps - 1 - k, tps)), u - tps + 1 + k, tps)
        if n:
            finish[n - 1].wait_send()
            keep[n - 1].wait()
        last[...] = own.astype(low)
        finish[n].start()
        keep[n].start()

    reached = [0, 0, 0]

    def advance(done):
        for which, (stage, lag) in enumerate(((stage_b, 1), (stage_c, 2), (stage_d, 4))):
            while reached[which] < units and reached[which] + lag <= done - 1:
                stage(reached[which])
                reached[which] += 1

    loads = {}

    def fetch(u):
        if u >= units or u in loads:
            return
        n, i = divmod(u, tps)
        level, kind = kinds[n]
        owner = lax.rem(t + 1 + i, tps)
        copies = [links.local(full_ref.at[MATS * level + kind, owner], wbuf.at[u % 2])]
        if kind == 2:
            copies.append(links.local(act_ref.at[level, owner], side.at[u % 2]))
        if kind == 0:
            copies.append(links.local(qkv_ref.at[level, owner], side.at[u % 2]))
            copies.append(links.local(mix_ref.at[level, owner], mix.at[u % 2]))
        for copy in copies:
            copy.start()
        loads[u] = copies

    def bring(src, dst):
        copy = links.local(src, dst)
        copy.start()
        return copy

    def by_rows(body, size=64):
        def one(i, carry):
            body(pl.ds(pl.multiple_of(i * size, size), size))
            return carry

        lax.fori_loop(0, tokens // size, one, 0)

    def loop(count, body):
        def one(i, carry):
            body(i)
            return carry

        lax.fori_loop(0, count, one, 0)

    def column_sum(level, k, value):
        dmod_ref[level, k] += jnp.sum(value.reshape(value.shape[0] // 8, 8, width), axis=0)

    def lanes(i):
        return pl.ds(pl.multiple_of(i * LANES, LANES), LANES)

    def put(u, at, value):
        grad[u % 2, :, :, at] = value.astype(low).reshape(dps, rows, LANES)

    dmod_ref[...] = jnp.zeros_like(dmod_ref)
    top = layers - 1
    fetch(0)
    first = bring(cot_ref, arrived)
    branch_load, base_load = bring(brm_ref.at[top], branch), bring(mid_ref.at[top], base)
    first.wait()
    g[...] = arrived[...].astype(jnp.float32)
    tail = []

    for level in reversed(range(layers)):
        factor = [mod_ref[level, k : k + 1, :] for k in range(6)]
        temporal = level % 2 == 1
        chunk = GROUP // (2 * frames)
        start = kinds.index((level, 2)) * tps
        x_load = bring(xm_ref.at[level], x)
        branch_load.wait()

        def open_m(span, gate=factor[5], level=level):
            value = g[span, :]
            column_sum(level, 5, value * branch[span, :])
            lhs[span, :] = (gate * value).astype(low)

        by_rows(open_m)
        branch_load = bring(bra_ref.at[level], branch)
        for i in range(tps):
            u = start + i
            owner = lax.rem(t + 1 + i, tps)
            pre_load = bring(pre_ref.at[level, owner], pre)
            release(u)
            for copy in loads[u]:
                copy.wait()
            fetch(u + 1)
            w, act = wbuf.at[u % 2], side.at[u % 2]
            pre_load.wait()

            def third(k, u=u, i=i, w=w, act=act):
                at = lanes(k)
                put(u, at, dot_tn(lhs[...], act[:, at]))
                d_act = dot_nn(lhs[...], w[:, at])
                dpre[i, :, at] = (d_act * gelu_slope(pre[:, at])).astype(low)

            loop(width // LANES, third)
            stage_a(u)
            advance(u + 1)
        dacc[...] = jnp.zeros_like(dacc)
        x_load.wait()
        for i in range(tps):
            u = start + tps + i
            release(u)
            for copy in loads[u]:
                copy.wait()
            fetch(u + 1)
            w = wbuf.at[u % 2]

            def second(k, u=u, i=i, w=w):
                at = lanes(k)
                put(u, at, dot_tn(x[...], dpre[i, :, at]))
                dacc[:, at] += dot_nt(dpre[i], w[at, :])

            loop(width // LANES, second)
            stage_a(u)
            advance(u + 1)
        x_load = bring(xa_ref.at[level], x)
        base_load.wait()
        branch_load.wait()

        def turn_back(span, source, s_at, r_at, r):
            normed, rstd = normalize(source[span, :])
            d = dacc[span, :]
            column_sum(level, s_at, d)
            column_sum(level, r_at, d * normed)
            return g[span, :] + normalize_back(d * (1.0 + r), normed, rstd)

        def close_m(span, r=factor[4], gate=factor[2], level=level):
            value = turn_back(span, base, 3, 4, r)
            g[span, :] = value
            column_sum(level, 2, value * branch[span, :])
            lhs[span, :] = (gate * value).astype(low)

        by_rows(close_m)
        base_load = bring(hid_ref.at[level], base)
        if level:
            branch_load = bring(brm_ref.at[level - 1], branch)
        dacc[...] = jnp.zeros_like(dacc)
        x_load.wait()
        for i in range(tps):
            u = start + 2 * tps + i
            release(u)
            for copy in loads[u]:
                copy.wait()
            fetch(u + 1)
            w, qkv_j, mix_j = wbuf.at[u % 2], side.at[u % 2], mix.at[u % 2]

            def attention(k, w=w, qkv_j=qkv_j, temporal=temporal, chunk=chunk):
                span = pl.ds(pl.multiple_of(k * GROUP, GROUP), GROUP)
                scale = HD ** (-0.5)
                low_v = LANES - wide
                d_mix = dot_nn(lhs[span, :], w[:, 768 : 768 + LANES]).astype(low)
                d_mix4 = head_stack(d_mix, low_v, heads)
                query4 = head_stack(qkv_j[span, 0:LANES], 0, heads)
                key, value = qkv_j[span, LANES : 2 * LANES], qkv_j[span, 2 * LANES : 3 * LANES]
                probs = softmax_rows(dot_nt(query4, key) * scale, chunk if temporal else 0)
                d_probs = dot_nt(d_mix4, value)
                d_scores = (probs * (d_probs - jnp.sum(probs * d_probs, axis=-1, keepdims=True))).astype(low)
                d_value = pltpu.roll(dot_tn(probs.astype(low), d_mix4), LANES - 32, 1)
                d_query = head_merge(dot_nn(d_scores, key), 0, heads) * scale
                d_key = pltpu.roll(dot_tn(d_scores, query4), 32, 1) * scale
                dproj[span, 0:256] = d_query[:, 0:256].astype(low)
                dproj[span, 256:384] = (d_query[:, 256:384] + d_key[:, 0:128]).astype(low)
                dproj[span, 384:512] = d_key[:, 128:256].astype(low)
                dproj[span, 512:640] = (d_key[:, 256:384] + d_value[:, 0:128]).astype(low)
                dproj[span, 640:896] = d_value[:, 128:384].astype(low)
                dproj[span, 896:1152] = jnp.zeros((GROUP, 256), low)

            loop(tokens // GROUP, attention)
            for k in range(width // LANES):
                at = slice(k * LANES, (k + 1) * LANES)
                value = dot_tn(x[...], dproj[:, at])
                if k == width // LANES - 1:
                    value = value + dot_tn(lhs[...], mix_j[...])
                put(u, at, value)
                dacc[:, at] += dot_nt(dproj[:, 0:896], w[at, 0:896])
            stage_a(u)
            advance(u + 1)
        base_load.wait()

        def close_a(span, r=factor[1], level=level):
            value = turn_back(span, base, 0, 1, r)
            g[span, :] = value
            lhs[span, :] = value.astype(low)

        by_rows(close_a)
        strip = home_ref.shape[1]
        part, flock = strip // 2, frames // tps
        patches = strip * tps
        if level:
            base_load = bring(mid_ref.at[level - 1], base)
            away, stay = [], []
            for k in range(part // chunk):
                for f in range(flock):
                    to = pl.ds(pl.multiple_of(f * patches + t * strip + c * part + k * chunk, 16), chunk)
                    for peer in [None, twin] + chain + crossed:
                        _, pc, pt = peer or (p, c, t)
                        row = (k * 2 * frames + (pt * 2 + pc) * flock + f) * chunk
                        piece = lhs.at[pl.ds(pl.multiple_of(row, 16), chunk)]
                        if peer is None:
                            stay.append(links.local(piece, arrived.at[to]))
                        else:
                            away.append(links.remote(lambda s=piece, d=arrived.at[to], q=peer: (s, d, q))())
            for copy in away + stay:
                copy.start()
            for copy in away + stay:
                copy.wait()
            g[...] = arrived[...].astype(jnp.float32)
        else:
            for f in range(flock):
                for peer in [None] + chain:
                    pt = t if peer is None else peer[2]
                    piece = lhs.at[pl.ds(pl.multiple_of(f * patches + pt * strip, 16), strip)]
                    goal = home_ref.at[t * flock + f]
                    if peer is None:
                        tail.append(links.local(piece, goal))
                    else:
                        tail.append(links.remote(lambda s=piece, d=goal, q=peer: (s, d, q))())
            for copy in tail:
                copy.start()
    for extra in range(1, 5):
        advance(units + extra)
    for u in range(units):
        if u >= units - 2:
            to_twin[u].wait_send()
        if u >= units - 2 * tps:
            to_corner[u].wait_send()
            to_x[u].wait_send()
            to_y[u].wait_send()
            if u in along:
                along[u].wait_send()
    for n in range(mats):
        finish[n].wait_recv()
    finish[mats - 1].wait_send()
    keep[mats - 1].wait()
    for copy in tail:
        copy.wait()


def backward_pass(full, cot_rows, modulation, saved, mesh_shape, frames, strip, heads):
    tps, dps = mesh_shape["tp"], mesh_shape["dp"]
    mats, _, depth, width = full.shape
    layers, tokens = saved[0].shape[:2]
    rows = depth // dps
    half = rows // 2
    low, wider = jnp.bfloat16, jnp.float32
    sds = jax.ShapeDtypeStruct
    whole = pl.BlockSpec(memory_space=pl.ANY)
    near = pl.BlockSpec(memory_space=pltpu.VMEM)
    return pl.pallas_call(
        partial(backward_kernel, tps, (layers, frames, heads * HD, heads)),
        out_shape=[
            sds((mats, rows, width), low),
            sds((frames, strip, width), low),
            sds((layers, 6, 8, width), wider),
        ],
        in_specs=[whole, whole, near] + [whole] * 10,
        out_specs=[whole, whole, near],
        scratch_shapes=[
            pltpu.VMEM((2, tps, dps, half, width), low),
            pltpu.VMEM((2, dps, rows, width), low),
            pltpu.VMEM((2, dps, half, width), low),
            pltpu.VMEM((tps, half, width), low),
            pltpu.VMEM((tps, half, width), low),
            pltpu.VMEM((tps, half, width), low),
            pltpu.VMEM((tps - 1, half, width), low),
            pltpu.VMEM((half, width), low),
            pltpu.VMEM((tokens, width), wider),
            pltpu.VMEM((tokens, width), wider),
            pltpu.VMEM((tokens, width), low),
            pltpu.VMEM((tokens, width), low),
            pltpu.VMEM((2, depth, width), low),
            pltpu.VMEM((2, tokens, width), low),
            pltpu.VMEM((tokens, width), wider),
            pltpu.VMEM((tps, tokens, width), low),
            pltpu.VMEM((2, tokens, LANES), low),
            pltpu.VMEM((tokens, width), wider),
            pltpu.VMEM((tokens, width), wider),
            pltpu.VMEM((tokens, width), low),
            pltpu.VMEM((tokens, width), low),
            pltpu.SemaphoreType.DMA((160,)),
            pltpu.SemaphoreType.DMA((160,)),
            pltpu.SemaphoreType.DMA((96,)),
            pltpu.SemaphoreType.REGULAR((5 * tps,)),
        ],
        compiler_params=pltpu.CompilerParams(
            collective_id=1, has_side_effects=True, vmem_limit_bytes=VMEM_LIMIT
        ),
        name="backward_pass",
    )(full, cot_rows.reshape(tokens, width), modulation, *saved)


def sum_grads(grads):
    parts = []
    for grad in grads:
        part = lax.psum_scatter(grad, "tp", scatter_dimension=0, tiled=True)[0]
        part = lax.psum_scatter(part, "dp", scatter_dimension=0, tiled=True)
        parts.append(lax.psum(part, "ctx"))
    return jnp.stack(parts)


def pack(qkv, out, up, down):
    rows = qkv.shape[0]
    low = jnp.bfloat16
    first = jnp.concatenate([qkv.astype(low).reshape(rows, -1), out.astype(low).T], axis=1)
    return jnp.stack([first, up.astype(low), down.astype(low).T])


def unpack(first, second, third, like):
    rows, _, wide = like.shape
    cut = 3 * wide
    return (first[:, :cut].reshape(rows, 3, wide), first[:, cut:].T, second, third.T)


def frames_whole(rows):
    return lax.all_to_all(rows, "tp", 0, 1, tiled=True)


def frames_back(rows):
    return lax.all_to_all(rows, "tp", 1, 0, tiled=True)


def patches_whole(rows):
    return lax.all_to_all(rows, ("tp", "ctx"), 1, 0, tiled=True)


def patches_back(rows):
    return lax.all_to_all(rows, ("tp", "ctx"), 0, 1, tiled=True)


def columns_home(rows, mesh_shape):
    frames, patches, width = rows.shape
    tps, cs = mesh_shape["tp"], mesh_shape["ctx"]
    split = rows.reshape(tps, cs, frames // (tps * cs), patches, width)
    split = split.transpose(1, 0, 2, 3, 4).reshape(cs, frames // cs, patches, width)
    return lax.all_to_all(split, "ctx", 0, 2, tiled=True)[0]


def columns_away(rows, mesh_shape):
    tps, cs = mesh_shape["tp"], mesh_shape["ctx"]
    frames, patches, width = rows.shape
    split = lax.all_to_all(rows[None], "ctx", 2, 0, tiled=True)
    split = split.reshape(cs, tps, frames // tps, patches // cs, width).transpose(1, 0, 2, 3, 4)
    return split.reshape(frames * cs, patches // cs, width)


def per_device_plain(mesh_shape, inputs, conditioning, *states):
    masters, firsts, seconds, cotangent = states[:5], states[5:10], states[10:15], states[15]
    qkv_weight, out_weight, up_weight, down_weight, mod_weight = masters
    low = jnp.bfloat16
    highest = lax.Precision.HIGHEST
    layers = qkv_weight.shape[0]
    scale = HD ** (-0.5)
    dp_at, _, tp_at = place()
    tps, dps = mesh_shape["tp"], mesh_shape["dp"]
    rows = qkv_weight.shape[1]
    wide = qkv_weight.shape[3]
    heads = wide // HD
    width = inputs.shape[-1]

    shards = jnp.concatenate(
        [pack(qkv_weight[l], out_weight[l], up_weight[l], down_weight[l]) for l in range(layers)]
    )
    full = gather_weights(shards)

    cond_low = jax.nn.silu(conditioning).astype(low)
    cond_all = lax.all_gather(cond_low, "dp", axis=0, tiled=True)
    cond_mine = lax.dynamic_slice_in_dim(cond_all, dp_at * rows, rows, 1)
    mod_low = mod_weight.astype(low)
    mod_part = jnp.einsum("cd,ldke->clke", cond_mine, mod_low, preferred_element_type=jnp.float32)
    mod_part = lax.psum_scatter(mod_part, "dp", scatter_dimension=0, tiled=True)
    modulation = lax.all_gather(mod_part, "tp", axis=3, tiled=True)[0]

    hidden = frames_whole(inputs[0]).astype(jnp.float32)
    saved = []
    for level in range(layers):
        if level:
            if level % 2 == 1:
                hidden = patches_whole(hidden.astype(low)).astype(jnp.float32)
            else:
                hidden = patches_back(hidden.astype(low)).astype(jnp.float32)
        forms = SPATIAL_FORMS if level % 2 == 0 else TEMPORAL_FORMS
        first_w, up_w, down_w = full[MATS * level], full[MATS * level + 1], full[MATS * level + 2]
        factors = modulation[level]
        frames, patches = hidden.shape[:2]
        normed_a, rstd_a = normalize(hidden)
        attn_in = (normed_a * (1.0 + factors[1]) + factors[0]).astype(low)
        projected = jnp.einsum(
            "fpd,jde->fpje", attn_in, first_w[:, :, : 3 * wide], preferred_element_type=jnp.float32
        ).astype(low)
        projected = projected.reshape(frames, patches, tps, 3, heads, HD)
        query, key, value = (projected[:, :, :, s] for s in range(3))
        mixed, log_total = attend(query, key, value, forms, scale)
        mixed = mixed.reshape(frames, patches, tps, wide)
        branch_a = jnp.einsum(
            "fpje,jde->fpd", mixed, first_w[:, :, 3 * wide :], preferred_element_type=jnp.float32
        )
        middle = hidden + factors[2] * branch_a
        normed_m, rstd_m = normalize(middle)
        mlp_in = (normed_m * (1.0 + factors[4]) + factors[3]).astype(low)
        hidden_pre = jnp.einsum("fpd,jdh->fpjh", mlp_in, up_w, preferred_element_type=jnp.float32)
        hidden_act = jax.nn.gelu(hidden_pre, approximate=True).astype(low)
        branch_m = jnp.einsum("fpjh,jdh->fpd", hidden_act, down_w, preferred_element_type=jnp.float32)
        saved.append(
            (forms, first_w, up_w, down_w, factors, normed_a, rstd_a, attn_in, query, key, value,
             mixed, log_total, branch_a, normed_m, rstd_m, mlp_in, hidden_pre, hidden_act, branch_m)
        )
        hidden = middle + factors[5] * branch_m
    temporal_end = layers % 2 == 0
    output = hidden.astype(low)
    output = columns_home(output, mesh_shape) if temporal_end else frames_back(output)
    upstream = columns_away(cotangent[0], mesh_shape) if temporal_end else frames_whole(cotangent[0])
    upstream = upstream.astype(jnp.float32)

    grads = [None] * (MATS * layers)
    d_mods = [None] * layers
    for level in reversed(range(layers)):
        (forms, first_w, up_w, down_w, factors, normed_a, rstd_a, attn_in, query, key, value,
         mixed, log_total, branch_a, normed_m, rstd_m, mlp_in, hidden_pre, hidden_act, branch_m) = saved[level]
        frames, patches = upstream.shape[:2]
        d_gate_m = jnp.sum(upstream * branch_m, axis=(0, 1))
        d_branch_m = (factors[5] * upstream).astype(low)
        grads[MATS * level + 2] = jnp.einsum(
            "fpd,fpjh->jdh", d_branch_m, hidden_act, preferred_element_type=jnp.float32
        ).astype(low)
        d_act = jnp.einsum("fpd,jdh->fpjh", d_branch_m, down_w, preferred_element_type=jnp.float32)
        slope_pull = jax.vjp(partial(jax.nn.gelu, approximate=True), hidden_pre)[1]
        d_pre = slope_pull(d_act)[0].astype(low)
        grads[MATS * level + 1] = jnp.einsum(
            "fpd,fpjh->jdh", mlp_in, d_pre, preferred_element_type=jnp.float32
        ).astype(low)
        d_mlp_in = jnp.einsum("fpjh,jdh->fpd", d_pre, up_w, preferred_element_type=jnp.float32)
        d_shift_m = jnp.sum(d_mlp_in, axis=(0, 1))
        d_scale_m = jnp.sum(d_mlp_in * normed_m, axis=(0, 1))
        upstream = upstream + normalize_back(d_mlp_in * (1.0 + factors[4]), normed_m, rstd_m)
        d_gate_a = jnp.sum(upstream * branch_a, axis=(0, 1))
        d_branch_a = (factors[2] * upstream).astype(low)
        grad_out = jnp.einsum("fpd,fpje->jde", d_branch_a, mixed, preferred_element_type=jnp.float32)
        d_mixed = jnp.einsum(
            "fpd,jde->fpje", d_branch_a, first_w[:, :, 3 * wide :], preferred_element_type=jnp.float32
        ).astype(low)
        d_mixed = d_mixed.reshape(frames, patches, tps, heads, HD)
        d_parts = attend_back(query, key, value, d_mixed, log_total, forms, scale)
        d_projected = jnp.stack(d_parts, axis=3).astype(low).reshape(frames, patches, tps, 3 * wide)
        grad_qkv = jnp.einsum("fpd,fpje->jde", attn_in, d_projected, preferred_element_type=jnp.float32)
        grads[MATS * level] = jnp.concatenate([grad_qkv, grad_out], axis=2).astype(low)
        d_attn_in = jnp.einsum(
            "fpje,jde->fpd", d_projected, first_w[:, :, : 3 * wide], preferred_element_type=jnp.float32
        )
        d_shift_a = jnp.sum(d_attn_in, axis=(0, 1))
        d_scale_a = jnp.sum(d_attn_in * normed_a, axis=(0, 1))
        upstream = upstream + normalize_back(d_attn_in * (1.0 + factors[1]), normed_a, rstd_a)
        d_mods[level] = jnp.stack([d_shift_a, d_scale_a, d_gate_a, d_shift_m, d_scale_m, d_gate_m])
        if level:
            if level % 2 == 1:
                upstream = patches_back(upstream.astype(low)).astype(jnp.float32)
            else:
                upstream = patches_whole(upstream.astype(low)).astype(jnp.float32)
    input_grad = frames_back(upstream.astype(low)).astype(jnp.float32)

    reduced = sum_grads([grads[m] for m in reversed(range(MATS * layers))])
    reduced = reduced.astype(jnp.float32)

    d_mod = lax.psum(jnp.stack(d_mods)[None], ("ctx", "tp"))
    d_mod_all = lax.all_gather(d_mod, "dp", axis=0, tiled=True)
    d_mod_mine = lax.dynamic_slice_in_dim(d_mod_all, tp_at * wide, wide, 3)
    grad_mod = jnp.einsum("cd,clke->ldke", cond_mine.astype(jnp.float32), d_mod_mine, precision=highest)
    cond_part = jnp.einsum("clke,ldke->cd", d_mod_mine, mod_low.astype(jnp.float32), precision=highest)
    cond_part = lax.all_gather(lax.psum(cond_part, "tp"), "dp", axis=1, tiled=True)
    cond_total = lax.dynamic_slice_in_dim(cond_part, dp_at * conditioning.shape[0], conditioning.shape[0], 0)
    cond_grad = jax.vjp(jax.nn.silu, conditioning)[1](cond_total)[0]

    order = list(reversed(range(MATS * layers)))
    per_level = [
        unpack(*[reduced[order.index(MATS * level + kind)] for kind in range(MATS)], qkv_weight[level])
        for level in range(layers)
    ]
    stacked = [jnp.stack([per_level[level][kind] for level in range(layers)]) for kind in range(4)]
    stacked.append(grad_mod)
    squares = jnp.zeros((), jnp.float32)
    for grad in stacked:
        squares = squares + jnp.sum(grad * grad)
    grad_norm = jnp.sqrt(lax.psum(squares, ("dp", "tp")))
    coef = CLIP_MAX / jnp.maximum(grad_norm, CLIP_MAX)
    updates = [
        adam_update(masters[kind], firsts[kind], seconds[kind], stacked[kind], coef) for kind in range(5)
    ]
    return (output[None], input_grad[None], cond_grad, grad_norm) + tuple(
        updates[kind][part] for part in range(4) for kind in range(5)
    )


def per_device(mesh_shape, inputs, conditioning, *states):
    if not by_hand(mesh_shape, inputs, states[0]):
        return per_device_plain(mesh_shape, inputs, conditioning, *states)
    masters, firsts, seconds, cotangent = states[:5], states[5:10], states[10:15], states[15]
    qkv_weight, out_weight, up_weight, down_weight, mod_weight = masters
    low = jnp.bfloat16
    highest = lax.Precision.HIGHEST
    layers = qkv_weight.shape[0]
    scale = HD ** (-0.5)
    dp_at, _, tp_at = place()
    tps, dps = mesh_shape["tp"], mesh_shape["dp"]
    rows = qkv_weight.shape[1]
    wide = qkv_weight.shape[3]
    heads = wide // HD
    width = inputs.shape[-1]

    shards = jnp.concatenate(
        [pack(qkv_weight[l], out_weight[l], up_weight[l], down_weight[l]) for l in range(layers)]
    )
    cond_low = jax.nn.silu(conditioning).astype(low)
    cond_all = lax.all_gather(cond_low, "dp", axis=0, tiled=True)
    cond_mine = lax.dynamic_slice_in_dim(cond_all, dp_at * rows, rows, 1)
    mod_low = mod_weight.astype(low)
    mod_part = jnp.einsum("cd,ldke->clke", cond_mine, mod_low, preferred_element_type=jnp.float32)
    mod_part = lax.psum_scatter(mod_part, "dp", scatter_dimension=0, tiled=True)
    modulation = lax.all_gather(mod_part, "tp", axis=3, tiled=True)[0]
    (full, output, cot_rows, hid, mid, bra, brm, xa, xm, qkv, mix, pre, act) = forward_pass(
        shards, inputs[0], cotangent[0], modulation, mesh_shape, heads
    )
    frames, strip = inputs.shape[1:3]
    reduced, home, d_mods = backward_pass(
        full, cot_rows, modulation, (hid, mid, bra, brm, xa, xm, qkv, mix, pre, act), mesh_shape, frames, strip, heads
    )
    input_grad = home.astype(jnp.float32)
    d_mods = jnp.sum(d_mods, axis=2)
    output = output.reshape(frames, strip, width)
    reduced = reduced.astype(jnp.float32)

    d_mod = lax.psum(d_mods[None], ("ctx", "tp"))
    d_mod_all = lax.all_gather(d_mod, "dp", axis=0, tiled=True)
    d_mod_mine = lax.dynamic_slice_in_dim(d_mod_all, tp_at * wide, wide, 3)
    grad_mod = jnp.einsum("cd,clke->ldke", cond_mine.astype(jnp.float32), d_mod_mine, precision=highest)
    cond_part = jnp.einsum("clke,ldke->cd", d_mod_mine, mod_low.astype(jnp.float32), precision=highest)
    cond_part = lax.all_gather(lax.psum(cond_part, "tp"), "dp", axis=1, tiled=True)
    cond_total = lax.dynamic_slice_in_dim(cond_part, dp_at * conditioning.shape[0], conditioning.shape[0], 0)
    cond_grad = jax.vjp(jax.nn.silu, conditioning)[1](cond_total)[0]

    per_level = [
        unpack(*[reduced[MATS * level + kind] for kind in range(MATS)], qkv_weight[level])
        for level in range(layers)
    ]
    stacked = [jnp.stack([per_level[level][kind] for level in range(layers)]) for kind in range(4)]
    stacked.append(grad_mod)
    squares = jnp.zeros((), jnp.float32)
    for grad in stacked:
        squares = squares + jnp.sum(grad * grad)
    grad_norm = jnp.sqrt(lax.psum(squares, ("dp", "tp")))
    coef = CLIP_MAX / jnp.maximum(grad_norm, CLIP_MAX)
    updates = [
        adam_update(masters[kind], firsts[kind], seconds[kind], stacked[kind], coef) for kind in range(5)
    ]
    return (output[None], input_grad[None], cond_grad, grad_norm) + tuple(
        updates[kind][part] for part in range(4) for kind in range(5)
    )


def solution(mesh):
    weights = (
        P(None, "dp", None, "tp"),
        P(None, "tp", "dp"),
        P(None, "dp", "tp"),
        P(None, "tp", "dp"),
        P(None, "dp", None, "tp"),
    )
    rows = P("dp", "ctx", "tp", None)
    return jax.shard_map(
        partial(per_device, dict(mesh.shape)),
        mesh=mesh,
        in_specs=(rows, P("dp", None)) + weights * 3 + (rows,),
        out_specs=(rows, rows, P("dp", None), P()) + weights * 4,
        check_vma=False,
    )
```

```python
from functools import partial

import jax
import jax.numpy as jnp
from jax import lax
from jax.experimental import pallas as pl
from jax.experimental.pallas import tpu as pltpu
from jax.sharding import PartitionSpec as P

HD = 72
STEP = 5
EPS_NORM = 1e-06
LEARN_RATE = 0.03
DECAY_RATE = 0.1
BETA_ONE = 0.5
BETA_TWO = 0.5
ADAM_EPS = 1e-08
CLIP_MAX = 1.0
MESH = pl.DeviceIdType.MESH
MATS = 3
VMEM_LIMIT = 62 * 1024 * 1024
LANES = 384
SLOTS = 2
GROUP = 256
SPATIAL_FORMS = ("fqjhe,fkjhe->fjhqk", "fjhqk,fkjhe->fqjhe", "fjhqk,fqjhe->fkjhe")
TEMPORAL_FORMS = ("qpjhe,kpjhe->pjhqk", "pjhqk,kpjhe->qpjhe", "pjhqk,qpjhe->kpjhe")


def normalize(rows):
    centred = rows - jnp.mean(rows, axis=-1, keepdims=True)
    rstd = lax.rsqrt(jnp.mean(centred * centred, axis=-1, keepdims=True) + EPS_NORM)
    return (centred * rstd, rstd)


def normalize_back(grad, normed, rstd):
    return rstd * (
        grad
        - jnp.mean(grad, axis=-1, keepdims=True)
        - normed * jnp.mean(grad * normed, axis=-1, keepdims=True)
    )


def attend(query, key, value, forms, scale):
    scores = jnp.einsum(forms[0], query, key, preferred_element_type=jnp.float32) * scale
    top = jnp.max(scores, axis=-1, keepdims=True)
    expo = jnp.exp(scores - top)
    total = jnp.sum(expo, axis=-1, keepdims=True)
    probs = (expo / total).astype(jnp.bfloat16)
    mixed = jnp.einsum(forms[1], probs, value, preferred_element_type=jnp.float32)
    return (mixed.astype(jnp.bfloat16), top + jnp.log(total))


def attend_back(query, key, value, d_mixed, log_total, forms, scale):
    scores = jnp.einsum(forms[0], query, key, preferred_element_type=jnp.float32) * scale
    probs = jnp.exp(scores - log_total)
    d_probs = jnp.einsum(forms[0], d_mixed, value, preferred_element_type=jnp.float32)
    d_scores = (probs * (d_probs - jnp.sum(probs * d_probs, axis=-1, keepdims=True))).astype(
        jnp.bfloat16
    )
    d_value = jnp.einsum(
        forms[2], probs.astype(jnp.bfloat16), d_mixed, preferred_element_type=jnp.float32
    )
    d_query = jnp.einsum(forms[1], d_scores, key, preferred_element_type=jnp.float32) * scale
    d_key = jnp.einsum(forms[2], d_scores, query, preferred_element_type=jnp.float32) * scale
    return (d_query, d_key, d_value)


def adam_update(master, first, second, grad, coef):
    clipped = coef * grad
    first_new = BETA_ONE * first + (1.0 - BETA_ONE) * clipped
    second_new = BETA_TWO * second + (1.0 - BETA_TWO) * clipped * clipped
    first_hat = first_new / (1.0 - BETA_ONE**STEP)
    second_hat = second_new / (1.0 - BETA_TWO**STEP)
    master_new = master - LEARN_RATE * (
        first_hat / (jnp.sqrt(second_hat) + ADAM_EPS) + DECAY_RATE * master
    )
    return (master_new, master_new.astype(jnp.bfloat16), first_new, second_new)


def place():
    return lax.axis_index("dp"), lax.axis_index("ctx"), lax.axis_index("tp")


def greet(peers):
    barrier = pltpu.get_barrier_semaphore()
    for peer in peers:
        pl.semaphore_signal(barrier, inc=1, device_id=peer, device_id_type=MESH)
    pl.semaphore_wait(barrier, len(peers))


def by_hand(mesh_shape, inputs, qkv_weight):
    tps, cs = mesh_shape["tp"], mesh_shape["ctx"]
    layers, rows, _, wide = qkv_weight.shape
    clips, frames, strip, width = inputs.shape
    return (
        mesh_shape["dp"] == 4 and cs == 2 and tps == 4 and clips == 1 and layers == 2 and rows % 32 == 0
        and wide == 4 * HD and 4 * wide == width and width % LANES == 0 and frames == 2 * tps
        and strip * tps == GROUP and frames * cs == 16 and strip == 64
    )


def gather_weights(shards):
    full = lax.all_gather(shards, "dp", axis=1, tiled=True)
    return lax.all_gather(full, "tp", axis=1, tiled=False)


class Links:
    def __init__(self, send_sem, recv_sem, local_sem):
        self.send_sem, self.recv_sem, self.local_sem = send_sem, recv_sem, local_sem
        self.used, self.used_local = 0, 0

    def remote(self, make):
        at = self.used
        self.used += 1

        def build(*args):
            src, dst, peer = make(*args)
            return pltpu.make_async_remote_copy(
                src_ref=src, dst_ref=dst, send_sem=self.send_sem.at[at], recv_sem=self.recv_sem.at[at],
                device_id=peer, device_id_type=MESH,
            )

        return build

    def local(self, src, dst):
        at = self.used_local
        self.used_local += 1
        return pltpu.make_async_copy(src, dst, self.local_sem.at[at])


def lane_mask(shape, low, high):
    lane = lax.broadcasted_iota(jnp.int32, shape, 1)
    return jnp.logical_and(lane >= low, lane < high)


def dot_nn(a, b):
    return lax.dot_general(a, b, (((1,), (0,)), ((), ())), preferred_element_type=jnp.float32)


def dot_nt(a, b):
    return lax.dot_general(a, b, (((1,), (1,)), ((), ())), preferred_element_type=jnp.float32)


def dot_tn(a, b):
    return lax.dot_general(a, b, (((0,), (0,)), ((), ())), preferred_element_type=jnp.float32)


def softmax_rows(scores, columns):
    if columns:
        rows = lax.broadcasted_iota(jnp.int32, scores.shape, 0)
        cols = lax.broadcasted_iota(jnp.int32, scores.shape, 1)
        scores = jnp.where((rows & (columns - 1)) == (cols & (columns - 1)), scores, -1e30)
    top = jnp.max(scores, axis=-1, keepdims=True)
    expo = jnp.exp(scores - top)
    return expo * (1.0 / jnp.sum(expo, axis=-1, keepdims=True))


def head_stack(rows, first, heads):
    return jnp.concatenate(
        [jnp.where(lane_mask(rows.shape, first + h * HD, first + (h + 1) * HD), rows, jnp.zeros_like(rows)) for h in range(heads)],
        axis=0,
    )


def head_merge(stacked, first, heads):
    size = stacked.shape[0] // heads
    total = jnp.zeros((size, stacked.shape[1]), stacked.dtype)
    for h in range(heads):
        part = stacked[h * size : (h + 1) * size]
        total = jnp.where(lane_mask(part.shape, first + h * HD, first + (h + 1) * HD), part, total)
    return total


def forward_kernel(tps, geometry, *refs):
    layers, frames, wide, heads = geometry
    (qkv_w, out_w, up_w, down_w, mod_w, cond_ref, rows_ref, cot_ref,
     full_ref, out_ref, cot_out, hid_out, mid_out, bra_out, brm_out, xa_out, xm_out, qkv_out, mix_out, pre_out, act_out, mod_ref, cond_in,
     hid, mid, acc_a, acc_m, x_a, x_m, wbuf, act, pre, qkv, mix, rows_in, moved, turned,
     packed, wide_in, out_in, up_in, down_in, mod_in, part, part_in, columns,
     send_sem, recv_sem, local_sem) = refs
    p, c, t = place()
    mats, rows, width = packed.shape
    tokens = hid.shape[1]
    half = rows // 2
    own_half = pl.multiple_of(c * half, 16)
    beside, above, twin = (p ^ 1, c, t), (p ^ 2, c, t), (p, 1 - c, t)
    chain = [(p, c, lax.rem(t + k, tps)) for k in range(1, tps)]
    crossed = [(p, 1 - c, lax.rem(t + k, tps)) for k in range(1, tps)]
    plane = [(p ^ k, c, t) for k in range(1, 4)]
    links = Links(send_sem, recv_sem, local_sem)
    low = jnp.bfloat16

    arrivals = {}
    for level in range(layers):
        arrivals[level] = (
            links.local(qkv_w.at[level], wide_in.at[level]), links.local(out_w.at[level], out_in.at[level]),
            links.local(up_w.at[level], up_in.at[level]), links.local(down_w.at[level], down_in.at[level]),
        )
        for copy in arrivals[level]:
            copy.start()
    mod_loads = [links.local(mod_w.at[k // 2, pl.ds(3 * (k % 2), 3)], mod_in.at[k % 2]) for k in range(2 * layers)]
    mod_loads[0].start()
    mod_loads[1].start()
    greet(chain + crossed + plane + [twin])
    cond_copies = [links.remote(lambda q=q: (cond_ref.at[q[0]], cond_in.at[p], q))() for q in plane]
    cond_own = links.local(cond_ref.at[p], cond_in.at[p])
    for copy in cond_copies + [cond_own]:
        copy.start()

    def rows_of(owner):
        return pl.ds(pl.multiple_of(owner * rows + own_half, 16), half)

    def block(m, k, owner):
        return full_ref.at[m, lax.rem(t + tps - k, tps), rows_of(owner)]

    def column(m, owner):
        return full_ref.at[m, :, rows_of(owner)]

    def own(m):
        return packed.at[m, pl.ds(own_half, half)]

    keep, along, to_x, to_y, corner, to_twin = {}, {}, {}, {}, {}, {}
    for m in range(mats):
        keep[m] = links.local(own(m), block(m, 0, p))
        for k in range(tps):
            if k:
                along[m, k] = links.remote(lambda m=m, k=k: (own(m), block(m, 0, p), chain[k - 1]))()
            source = own(m) if k == 0 else block(m, k, p)
            to_x[m, k] = links.remote(lambda m=m, k=k, s=source: (s, block(m, k, p), beside))()
            to_y[m, k] = links.remote(lambda m=m, k=k, s=source: (s, block(m, k, p), above))()
            if k % 2 == 0:
                corner[m, k] = links.remote(lambda m=m, k=k: (block(m, k, p ^ 1), block(m, k, p ^ 1), above))()
            else:
                corner[m, k] = links.remote(lambda m=m, k=k: (block(m, k, p ^ 2), block(m, k, p ^ 2), beside))()
        for which in range(4):
            owner = (p, p ^ 1, p ^ 2, p ^ 3)[which]
            to_twin[m, which] = links.remote(lambda m=m, o=owner: (column(m, o), column(m, o), twin))()

    def unit(step):
        for m in range(1, mats):
            if step == (tps - 1 if m == 1 else tps * (m - 1) + 1):
                for j in range(1, tps):
                    along[m, j].start()
        if step < mats * tps:
            m, k = divmod(step, tps)
            if k:
                along[m, k].wait_recv()
                to_x[m, k].start()
                to_y[m, k].start()
            if k == tps - 1:
                keep[m].wait()
                to_twin[m, 0].start()
        if 0 <= step - 3 < mats * tps:
            m, k = divmod(step - 3, tps)
            to_x[m, k].wait_recv()
            if k % 2 == 0:
                corner[m, k].start()
            to_y[m, k].wait_recv()
            if k % 2:
                corner[m, k].start()
            if k == tps - 1:
                to_twin[m, 1].start()
                to_twin[m, 2].start()
        if 0 <= step - 6 < mats * tps:
            m, k = divmod(step - 6, tps)
            corner[m, k].wait_recv()
            if k == tps - 1:
                to_twin[m, 3].start()

    def prepare(m):
        level, kind = divmod(m, MATS)
        if kind == 0:
            arrivals[level][0].wait()
            arrivals[level][1].wait()
            for k in range(3):
                packed[m, :, k * wide : (k + 1) * wide] = wide_in[level, k].astype(low)
            packed[m, :, 3 * wide :] = out_in[level].T.astype(low)
        elif kind == 1:
            arrivals[level][2].wait()
            packed[m] = up_in[level].astype(low)
        else:
            arrivals[level][3].wait()
            packed[m] = down_in[level].T.astype(low)
        keep[m].start()
        to_x[m, 0].start()
        to_y[m, 0].start()
        if m == 0:
            for j in range(1, tps):
                along[m, j].start()

    for m in range(mats):
        prepare(m)

    for copy in cond_copies:
        copy.wait_recv()
    cond_own.wait()
    cond_rows = cond_in[...].reshape(-1, rows).astype(low)
    for k in range(2 * layers):
        mod_loads[k].wait()
        for j in range(3):
            value = dot_nn(cond_rows, mod_in[k % 2, j].astype(low))
            part[:, 3 * k + j] = value.reshape(part.shape[0], 8, wide)
        if k + 2 < 2 * layers:
            mod_loads[k + 2].start()
    part_copies = [links.remote(lambda q=q: (part.at[q[0]], part_in.at[p], q))() for q in plane]
    for copy in part_copies:
        copy.start()
    part_in[p] = part[p]
    for copy in part_copies:
        copy.wait_recv()
    columns[t] = part_in[0] + part_in[1] + part_in[2] + part_in[3]
    column_copies = [links.remote(lambda q=q: (columns.at[t], columns.at[t], q))() for q in chain]
    for copy in column_copies:
        copy.start()
    for copy in column_copies:
        copy.wait_recv()
    for k in range(6 * layers):
        for j in range(tps):
            mod_ref[k // 6, k % 6, :, j * wide : (j + 1) * wide] = columns[j, k]

    progress = [0]

    def tick():
        if progress[0] < mats * tps + 6:
            unit(progress[0])
            progress[0] += 1

    def arrive(m):
        while progress[0] < tps * m + tps + 6:
            tick()
        for which in range(4):
            to_twin[m, which].wait_recv()

    loads = {}

    def fetch(m, j):
        if (m, j) not in loads and m < mats:
            loads[m, j] = links.local(full_ref.at[m, j], wbuf.at[(m * tps + j) % SLOTS])
            loads[m, j].start()

    flock = frames // tps
    patches = rows_in.shape[1]
    strip = patches // tps

    def strip_of(owner):
        return pl.ds(pl.multiple_of(owner * strip, 16), strip)

    spread_rows = [
        links.remote(lambda k=k: (rows_ref.at[chain[k - 1][2]], rows_in.at[:, strip_of(t)], chain[k - 1]))() for k in range(1, tps)
    ]
    keep_rows = links.local(rows_ref.at[t], rows_in.at[:, strip_of(t)])

    part = strip // 2
    chunk = turned.shape[2]
    cot_copies = []
    for g in range(part // chunk):
        there = pl.ds(pl.multiple_of((1 - c) * part + g * chunk, 16), chunk)
        here = pl.ds(pl.multiple_of(c * part + g * chunk, 16), chunk)
        cot_copies.append(links.remote(lambda g=g, s=there: (cot_ref.at[:, :, s], cot_out.at[g, :, c], twin))())
        cot_copies.append(links.local(cot_ref.at[:, :, here], cot_out.at[g, :, c]))
    for copy in cot_copies:
        copy.start()

    saves = []

    def save(src, dst):
        copy = links.local(src, dst)
        copy.start()
        return copy

    def by_rows(body, size=64):
        def one(i, carry):
            body(pl.ds(pl.multiple_of(i * size, size), size))
            return carry

        lax.fori_loop(0, tokens // size, one, 0)

    def loop(count, body):
        def one(i, carry):
            body(i)
            return carry

        lax.fori_loop(0, count, one, 0)

    pending = {}

    def settle(name):
        if name in pending:
            for copy in pending.pop(name):
                copy.wait()

    for level in range(layers):
        factor = [mod_ref[level, k, 0:1, :] for k in range(6)]
        hidden = hid.at[level]
        middle = mid.at[level]
        temporal = level % 2 == 1
        first, second, third = MATS * level, MATS * level + 1, MATS * level + 2
        if level == 0:
            for _ in range(tps):
                tick()
            for copy in spread_rows + [keep_rows]:
                copy.start()
            tick()
            for copy in spread_rows:
                copy.wait_recv()
            keep_rows.wait()
            for f in range(flock):
                loop(patches // 64, lambda i, f=f: hidden.__setitem__(
                    pl.ds(pl.multiple_of(f * patches + i * 64, 64), 64),
                    rows_in[f, pl.ds(pl.multiple_of(i * 64, 64), 64), :].astype(jnp.float32)))
        settle("x_a")

        def enter(span, source=hidden, to=x_a, s=factor[0], r=factor[1]):
            normed, _ = normalize(source[span, :])
            to[span, :] = (normed * (1.0 + r) + s).astype(low)

        by_rows(enter)
        pending["x_a"] = [save(x_a, xa_out.at[level])]
        saves.append(save(hidden, hid_out.at[level]))
        settle("acc_a")
        acc_a[...] = jnp.zeros_like(acc_a)
        arrive(first)
        fetch(first, 0)
        for j in range(tps):
            tick()
            fetch(first, j + 1) if j + 1 < tps else None
            loads[first, j].wait()
            w = wbuf.at[(first * tps + j) % SLOTS]
            settle(("qkv", j % 2))
            settle(("mix", j % 2))
            qkv_j, mix_j = qkv.at[j % 2], mix.at[j % 2]

            def attention(g):
                span = pl.ds(pl.multiple_of(g * GROUP, GROUP), GROUP)
                x = x_a[span, :]
                q = dot_nn(x, w[:, 0:LANES])
                q = jnp.where(lane_mask(q.shape, 0, wide), q, 0.0).astype(low)
                k = pltpu.roll(dot_nn(x, w[:, 256 : 256 + LANES]), LANES - 32, 1)
                k = jnp.where(lane_mask(k.shape, 0, wide), k, 0.0).astype(low)
                v = pltpu.roll(dot_nn(x, w[:, 512 : 512 + LANES]), 32, 1)
                v = jnp.where(lane_mask(v.shape, LANES - wide, LANES), v, 0.0).astype(low)
                qkv_j[span, 0:LANES] = q
                qkv_j[span, LANES : 2 * LANES] = k
                qkv_j[span, 2 * LANES : 3 * LANES] = v
                scores = dot_nt(head_stack(q, 0, heads), k) * (HD ** (-0.5))
                probs = softmax_rows(scores, chunk if temporal else 0).astype(low)
                mixed = head_merge(dot_nn(probs, v), LANES - wide, heads).astype(low)
                mix_j[span, :] = mixed
                for i in range(width // LANES):
                    at = slice(i * LANES, (i + 1) * LANES)
                    acc_a[span, at] += dot_nt(mixed, w[at, 768 : 768 + LANES])

            loop(tokens // GROUP, attention)
            pending["qkv", j % 2] = [save(qkv_j, qkv_out.at[level, j])]
            pending["mix", j % 2] = [save(mix_j, mix_out.at[level, j])]
        settle("x_m")

        def between(span, hidden=hidden, middle=middle, gate=factor[2], s=factor[3], r=factor[4]):
            rows_mid = hidden[span, :] + gate * acc_a[span, :]
            middle[span, :] = rows_mid
            normed, _ = normalize(rows_mid)
            x_m[span, :] = (normed * (1.0 + r) + s).astype(low)

        by_rows(between)
        pending["acc_a"] = [save(acc_a, bra_out.at[level])]
        pending["x_m"] = [save(x_m, xm_out.at[level])]
        saves.append(save(middle, mid_out.at[level]))
        arrive(second)
        fetch(second, 0)
        for j in range(tps):
            tick()
            fetch(second, j + 1) if j + 1 < tps else None
            loads[second, j].wait()
            w = wbuf.at[(second * tps + j) % SLOTS]
            settle(("pre", j % 2))
            settle(("act", j))
            pre_j, act_j = pre.at[j % 2], act.at[j]

            def raise_up(i):
                at = pl.ds(pl.multiple_of(i * LANES, LANES), LANES)
                value = dot_nn(x_m[...], w[:, at])
                pre_j[:, at] = value
                act_j[:, at] = jax.nn.gelu(value, approximate=True).astype(low)

            loop(width // LANES, raise_up)
            pending["pre", j % 2] = [save(pre_j, pre_out.at[level, j])]
            pending["act", j] = [save(act_j, act_out.at[level, j])]
        settle("acc_m")
        acc_m[...] = jnp.zeros_like(acc_m)
        arrive(third)
        fetch(third, 0)
        for j in range(tps):
            tick()
            fetch(third, j + 1) if j + 1 < tps else None
            loads[third, j].wait()
            w = wbuf.at[(third * tps + j) % SLOTS]
            act_j = act.at[j]

            def lower(i):
                at = pl.ds(pl.multiple_of(i * LANES, LANES), LANES)
                acc_m[:, at] += dot_nt(act_j[...], w[at, :])

            loop(width // LANES, lower)
        if level + 1 < layers:
            def leave(span, middle=middle, gate=factor[5]):
                moved[span, :] = (middle[span, :] + gate * acc_m[span, :]).astype(low)

            by_rows(leave)
            pending["acc_m"] = [save(acc_m, brm_out.at[level])]
            away, stay = [], []
            here = (t * 2 + c) * flock
            for g in range(part // chunk):
                for f in range(flock):
                    goal = turned.at[g, here + f]
                    for peer in [None, twin] + chain + crossed:
                        _, pc, pt = peer or (p, c, t)
                        first_row = f * patches + pt * strip + pc * part + g * chunk
                        piece = moved.at[pl.ds(pl.multiple_of(first_row, 16), chunk)]
                        if peer is None:
                            stay.append(links.local(piece, goal))
                        else:
                            away.append(links.remote(lambda s=piece, d=goal, q=peer: (s, d, q))())
            for copy in away + stay:
                copy.start()
            tick()
            for copy in away:
                copy.wait()
            for copy in stay:
                copy.wait()
            nxt = hid.at[level + 1]
            for g in range(part // chunk):
                for f in range(turned.shape[1]):
                    base = (g * turned.shape[1] + f) * chunk
                    nxt[base : base + chunk, :] = turned[g, f].astype(jnp.float32)
        else:
            for g in range(part // chunk):
                for f in range(turned.shape[1]):
                    base = (g * turned.shape[1] + f) * chunk
                    span = slice(base, base + chunk)
                    turned[g, f] = (middle[span, :] + factor[5] * acc_m[span, :]).astype(low)
            pending["acc_m"] = [save(acc_m, brm_out.at[level])]
            home_copies = []
            for g in range(part // chunk):
                for ts in range(tps):
                    for f in range(flock):
                        to = pl.ds(pl.multiple_of(c * part + g * chunk, 16), chunk)
                        theirs = turned.at[g, (ts * 2 + 1 - c) * flock + f]
                        ours = turned.at[g, (ts * 2 + c) * flock + f]
                        home_copies.append(links.remote(lambda s=theirs, d=out_ref.at[ts, f, to]: (s, d, twin))())
                        home_copies.append(links.local(ours, out_ref.at[ts, f, to]))
            for copy in home_copies:
                copy.start()
    while progress[0] < mats * tps + 6:
        tick()
    for copy in saves + cot_copies + home_copies:
        copy.wait()
    for name in list(pending):
        settle(name)
    for copy in spread_rows + cond_copies + part_copies + column_copies:
        copy.wait_send()
    for m in range(mats):
        for which in range(4):
            to_twin[m, which].wait_send()
        for k in range(tps):
            if k:
                along[m, k].wait_send()
            to_x[m, k].wait_send()
            to_y[m, k].wait_send()
            corner[m, k].wait_send()


def forward_pass(masters, cond, rows, cot, mesh_shape):
    tps, dps, cs = mesh_shape["tp"], mesh_shape["dp"], mesh_shape["ctx"]
    qkv_w, out_w, up_w, down_w, mod_w = masters
    layers, _, depth, wide = qkv_w.shape
    heads = wide // HD
    mats, width = MATS * layers, rows.shape[-1]
    frames, strip = rows.shape[:2]
    flock = frames // tps
    tokens = frames * strip
    patches = strip * tps
    chunk = GROUP // (frames * cs)
    groups = strip // cs // chunk
    low, wider = jnp.bfloat16, jnp.float32
    sds = jax.ShapeDtypeStruct
    whole = pl.BlockSpec(memory_space=pl.ANY)
    return pl.pallas_call(
        partial(forward_kernel, tps, (layers, frames, wide, heads)),
        out_shape=[
            sds((mats, tps, dps * depth, width), low),
            sds((tps, flock, strip, width), low),
            sds((groups, tps, cs, flock, chunk, width), low),
            sds((layers, tokens, width), wider),
            sds((layers, tokens, width), wider),
            sds((layers, tokens, width), wider),
            sds((layers, tokens, width), wider),
            sds((layers, tokens, width), low),
            sds((layers, tokens, width), low),
            sds((layers, tps, tokens, 3 * LANES), low),
            sds((layers, tps, tokens, LANES), low),
            sds((layers, tps, tokens, width), wider),
            sds((layers, tps, tokens, width), low),
            sds((layers, 6, 8, width), wider),
            sds((dps, 8, depth), wider),
        ],
        in_specs=[whole] * 8,
        out_specs=[whole] * 13 + [pl.BlockSpec(memory_space=pltpu.VMEM)] * 2,
        scratch_shapes=[
            pltpu.VMEM((layers, tokens, width), wider),
            pltpu.VMEM((layers, tokens, width), wider),
            pltpu.VMEM((tokens, width), wider),
            pltpu.VMEM((tokens, width), wider),
            pltpu.VMEM((tokens, width), low),
            pltpu.VMEM((tokens, width), low),
            pltpu.VMEM((SLOTS, dps * depth, width), low),
            pltpu.VMEM((tps, tokens, width), low),
            pltpu.VMEM((2, tokens, width), wider),
            pltpu.VMEM((2, tokens, 3 * LANES), low),
            pltpu.VMEM((2, tokens, LANES), low),
            pltpu.VMEM((flock, patches, width), low),
            pltpu.VMEM((tokens, width), low),
            pltpu.VMEM((groups, frames * cs, chunk, width), low),
            pltpu.VMEM((mats, depth, width), low),
            pltpu.VMEM(qkv_w.shape, wider),
            pltpu.VMEM(out_w.shape, wider),
            pltpu.VMEM(up_w.shape, wider),
            pltpu.VMEM(down_w.shape, wider),
            pltpu.VMEM((2, 3, depth, wide), wider),
            pltpu.VMEM((dps, 6 * layers, 8, wide), wider),
            pltpu.VMEM((dps, 6 * layers, 8, wide), wider),
            pltpu.VMEM((tps, 6 * layers, 8, wide), wider),
            pltpu.SemaphoreType.DMA((200,)),
            pltpu.SemaphoreType.DMA((200,)),
            pltpu.SemaphoreType.DMA((140,)),
        ],
        compiler_params=pltpu.CompilerParams(
            collective_id=0, has_side_effects=True, vmem_limit_bytes=VMEM_LIMIT
        ),
        name="forward_pass",
    )(qkv_w, out_w, up_w, down_w, mod_w, cond, rows.reshape(tps, flock, strip, width), cot.reshape(tps, flock, strip, width))


def gelu_slope(v):
    root, cubic = 0.7978845608028654, 0.044715
    square = v * v
    bend = jnp.tanh(root * v * (1.0 + cubic * square))
    return 0.5 * (1.0 + bend) + 0.5 * v * (1.0 - bend * bend) * (root * (1.0 + 3.0 * cubic * square))


def backward_kernel(tps, geometry, *refs):
    layers, frames, wide, heads = geometry
    (full_ref, cot_ref, mod_ref, cond_in, mod_w, hid_ref, mid_ref, bra_ref, brm_ref, xa_ref, xm_ref, qkv_ref, mix_ref, pre_ref, act_ref,
     red_ref, home_ref, d_all, d_cond, norm_ref,
     tot, grad, twin_in, corner_in, beside_in, above_in, chain_in, last,
     g, dacc, lhs, x, wbuf, side, pre, dpre, mix, branch, base, dproj, arrived,
     dmod_ref, d_cut, d_in, mod_in, z_in, squares, norm_in, norm_line,
     send_sem, recv_sem, local_sem, free_sem) = refs
    p, c, t = place()
    mats = full_ref.shape[0]
    half, width = last.shape
    rows = 2 * half
    depth = full_ref.shape[2]
    dps = depth // rows
    tokens = g.shape[0]
    low = jnp.bfloat16
    mine = pl.ds(pl.multiple_of(c * half, 16), half)
    theirs = pl.ds(pl.multiple_of((1 - c) * half, 16), half)
    beside, above, twin = (p ^ 1, c, t), (p ^ 2, c, t), (p, 1 - c, t)
    chain = [(p, c, lax.rem(t + k, tps)) for k in range(1, tps)]
    crossed = [(p, 1 - c, lax.rem(t + k, tps)) for k in range(1, tps)]
    plane = [(p ^ k, c, t) for k in range(1, 4)]
    across = [(p ^ k, 1 - c, t) for k in range(1, 4)]
    greet(chain + crossed + plane + across + [twin])
    links = Links(send_sem, recv_sem, local_sem)
    units = mats * tps
    kinds = [(level, kind) for level in reversed(range(layers)) for kind in (2, 1, 0)]

    TWIN, CORNER, BESIDE, ABOVE, CHAIN = 0, tps, 2 * tps, 3 * tps, 4 * tps

    def credit(slot, peer, u, gap):
        if u + gap < units:
            pl.semaphore_signal(free_sem.at[slot], inc=1, device_id=peer, device_id_type=MESH)

    def spend(slot, u, gap):
        if u >= gap:
            pl.semaphore_wait(free_sem.at[slot], 1)

    to_twin, to_corner, to_x, to_y, along, finish, keep = {}, {}, {}, {}, {}, {}, {}
    for u in range(units):
        n, i = divmod(u, tps)
        here = tot.at[n % 2, i]
        to_twin[u] = links.remote(lambda u=u: (grad.at[u % 2, :, theirs], twin_in.at[u % 2], twin))()
        via = beside if i % 2 == 0 else above
        to_corner[u] = links.remote(lambda h=here, i=i, v=via: (h.at[p ^ 3], corner_in.at[i], v))()
        to_x[u] = links.remote(lambda h=here, i=i: (h.at[p ^ 1], beside_in.at[i], beside))()
        to_y[u] = links.remote(lambda h=here, i=i: (h.at[p ^ 2], above_in.at[i], above))()
        if i < tps - 1:
            along[u] = links.remote(lambda h=here, i=i: (h.at[p], chain_in.at[i], chain[i]))()
        else:
            level, kind = kinds[n]
            goal = red_ref.at[MATS * level + kind, mine]
            finish[n] = links.remote(lambda d=goal: (last, d, twin))()
            keep[n] = links.local(last, goal)

    def plus(a, b):
        return (a.astype(jnp.float32) + b.astype(jnp.float32)).astype(low)

    def release(u):
        if u >= 2:
            to_twin[u - 2].wait_send()
        n, i = divmod(u, tps)
        if n >= 2:
            old = u - 2 * tps
            to_corner[old].wait_send()
            to_x[old].wait_send()
            to_y[old].wait_send()
            if i < tps - 1:
                along[old].wait_send()

    def stage_a(u):
        spend(TWIN + u % 2, u, 2)
        to_twin[u].start()

    def stage_b(u):
        n, i = divmod(u, tps)
        to_twin[u].wait_recv()
        here = tot.at[n % 2, i]

        def one(q, carry):
            here[q] = plus(grad[u % 2, q, mine], twin_in[u % 2, q])
            return carry

        lax.fori_loop(0, dps, one, 0)
        credit(TWIN + u % 2, twin, u, 2)
        spend(CORNER + i, u, tps)
        to_corner[u].start()
        if i % 2 == 0:
            spend(BESIDE + i, u, tps)
            to_x[u].start()
        else:
            spend(ABOVE + i, u, tps)
            to_y[u].start()

    def stage_c(u):
        n, i = divmod(u, tps)
        here = tot.at[n % 2, i]
        to_corner[u].wait_recv()
        if i % 2 == 0:
            here[p ^ 2] = plus(here[p ^ 2], corner_in[i])
            credit(CORNER + i, beside, u, tps)
            spend(ABOVE + i, u, tps)
            to_y[u].start()
        else:
            here[p ^ 1] = plus(here[p ^ 1], corner_in[i])
            credit(CORNER + i, above, u, tps)
            spend(BESIDE + i, u, tps)
            to_x[u].start()

    def stage_d(u):
        n, i = divmod(u, tps)
        here = tot.at[n % 2, i]
        to_x[u].wait_recv()
        to_y[u].wait_recv()
        own = here[p].astype(jnp.float32) + beside_in[i].astype(jnp.float32) + above_in[i].astype(jnp.float32)
        credit(BESIDE + i, beside, u, tps)
        credit(ABOVE + i, above, u, tps)
        if i < tps - 1:
            here[p] = own.astype(low)
            spend(CHAIN + i, u, tps)
            along[u].start()
            return
        for k in range(tps - 1):
            along[u - tps + 1 + k].wait_recv()
            own = own + chain_in[k].astype(jnp.float32)
            credit(CHAIN + k, (p, c, lax.rem(t + tps - 1 - k, tps)), u - tps + 1 + k, tps)
        if n:
            finish[n - 1].wait_send()
            keep[n - 1].wait()
        last[...] = own.astype(low)
        kept = last[...].astype(jnp.float32)
        squares[...] += jnp.sum((kept * kept).reshape(half // 8, 8, width), axis=0)
        finish[n].start()
        keep[n].start()

    reached = [0, 0, 0]

    def advance(done):
        for which, (stage, lag) in enumerate(((stage_d, 5), (stage_b, 1), (stage_c, 3))):
            while reached[which] < units and reached[which] + lag <= done - 1:
                stage(reached[which])
                reached[which] += 1

    loads = {}

    def fetch(u):
        if u >= units or u in loads:
            return
        n, i = divmod(u, tps)
        level, kind = kinds[n]
        owner = lax.rem(t + 1 + i, tps)
        copies = [links.local(full_ref.at[MATS * level + kind, owner], wbuf.at[u % 2])]
        if kind == 2:
            copies.append(links.local(act_ref.at[level, owner], side.at[u % 2]))
        if kind == 0:
            copies.append(links.local(qkv_ref.at[level, owner], side.at[u % 2]))
            copies.append(links.local(mix_ref.at[level, owner], mix.at[u % 2]))
        for copy in copies:
            copy.start()
        loads[u] = copies

    def bring(src, dst):
        copy = links.local(src, dst)
        copy.start()
        return copy

    def by_rows(body, size=64):
        def one(i, carry):
            body(pl.ds(pl.multiple_of(i * size, size), size))
            return carry

        lax.fori_loop(0, tokens // size, one, 0)

    def loop(count, body):
        def one(i, carry):
            body(i)
            return carry

        lax.fori_loop(0, count, one, 0)

    def column_sum(level, k, value):
        dmod_ref[level, k] += jnp.sum(value.reshape(value.shape[0] // 8, 8, width), axis=0)

    def lanes(i):
        return pl.ds(pl.multiple_of(i * LANES, LANES), LANES)

    def put(u, at, value):
        grad[u % 2, :, :, at] = value.astype(low).reshape(dps, rows, LANES)

    dmod_ref[...] = jnp.zeros_like(dmod_ref)
    squares[...] = jnp.zeros_like(squares)
    d_cut[...] = jnp.zeros_like(d_cut)
    top = layers - 1
    fetch(0)
    first = bring(cot_ref, arrived)
    branch_load, base_load = bring(brm_ref.at[top], branch), bring(mid_ref.at[top], base)
    first.wait()
    g[...] = arrived[...].astype(jnp.float32)
    tail = []

    for level in reversed(range(layers)):
        factor = [mod_ref[level, k, 0:1, :] for k in range(6)]
        temporal = level % 2 == 1
        chunk = GROUP // (2 * frames)
        start = kinds.index((level, 2)) * tps
        x_load = bring(xm_ref.at[level], x)
        branch_load.wait()

        def open_m(span, gate=factor[5], level=level):
            value = g[span, :]
            column_sum(level, 5, value * branch[span, :])
            lhs[span, :] = (gate * value).astype(low)

        by_rows(open_m)
        branch_load = bring(bra_ref.at[level], branch)
        for i in range(tps):
            u = start + i
            owner = lax.rem(t + 1 + i, tps)
            pre_load = bring(pre_ref.at[level, owner], pre)
            release(u)
            for copy in loads[u]:
                copy.wait()
            fetch(u + 1)
            w, act = wbuf.at[u % 2], side.at[u % 2]
            pre_load.wait()

            def third(k, u=u, i=i, w=w, act=act):
                at = lanes(k)
                put(u, at, dot_tn(lhs[...], act[:, at]))
                d_act = dot_nn(lhs[...], w[:, at])
                dpre[i, :, at] = (d_act * gelu_slope(pre[:, at])).astype(low)

            loop(width // LANES, third)
            stage_a(u)
            advance(u + 1)
        dacc[...] = jnp.zeros_like(dacc)
        x_load.wait()
        for i in range(tps):
            u = start + tps + i
            release(u)
            for copy in loads[u]:
                copy.wait()
            fetch(u + 1)
            w = wbuf.at[u % 2]

            def second(k, u=u, i=i, w=w):
                at = lanes(k)
                put(u, at, dot_tn(x[...], dpre[i, :, at]))
                dacc[:, at] += dot_nt(dpre[i], w[at, :])

            loop(width // LANES, second)
            stage_a(u)
            advance(u + 1)
        x_load = bring(xa_ref.at[level], x)
        base_load.wait()
        branch_load.wait()

        def turn_back(span, source, s_at, r_at, r):
            normed, rstd = normalize(source[span, :])
            d = dacc[span, :]
            column_sum(level, s_at, d)
            column_sum(level, r_at, d * normed)
            return g[span, :] + normalize_back(d * (1.0 + r), normed, rstd)

        def close_m(span, r=factor[4], gate=factor[2], level=level):
            value = turn_back(span, base, 3, 4, r)
            g[span, :] = value
            column_sum(level, 2, value * branch[span, :])
            lhs[span, :] = (gate * value).astype(low)

        by_rows(close_m)
        base_load = bring(hid_ref.at[level], base)
        if level:
            branch_load = bring(brm_ref.at[level - 1], branch)
        dacc[...] = jnp.zeros_like(dacc)
        x_load.wait()
        for i in range(tps):
            u = start + 2 * tps + i
            release(u)
            for copy in loads[u]:
                copy.wait()
            fetch(u + 1)
            w, qkv_j, mix_j = wbuf.at[u % 2], side.at[u % 2], mix.at[u % 2]

            def attention(k, w=w, qkv_j=qkv_j, temporal=temporal, chunk=chunk):
                span = pl.ds(pl.multiple_of(k * GROUP, GROUP), GROUP)
                scale = HD ** (-0.5)
                low_v = LANES - wide
                d_mix = dot_nn(lhs[span, :], w[:, 768 : 768 + LANES]).astype(low)
                d_mix4 = head_stack(d_mix, low_v, heads)
                query4 = head_stack(qkv_j[span, 0:LANES], 0, heads)
                key, value = qkv_j[span, LANES : 2 * LANES], qkv_j[span, 2 * LANES : 3 * LANES]
                probs = softmax_rows(dot_nt(query4, key) * scale, chunk if temporal else 0)
                d_probs = dot_nt(d_mix4, value)
                d_scores = (probs * (d_probs - jnp.sum(probs * d_probs, axis=-1, keepdims=True))).astype(low)
                d_value = pltpu.roll(dot_tn(probs.astype(low), d_mix4), LANES - 32, 1)
                d_query = head_merge(dot_nn(d_scores, key), 0, heads) * scale
                d_key = pltpu.roll(dot_tn(d_scores, query4), 32, 1) * scale
                dproj[span, 0:256] = d_query[:, 0:256].astype(low)
                dproj[span, 256:384] = (d_query[:, 256:384] + d_key[:, 0:128]).astype(low)
                dproj[span, 384:512] = d_key[:, 128:256].astype(low)
                dproj[span, 512:640] = (d_key[:, 256:384] + d_value[:, 0:128]).astype(low)
                dproj[span, 640:896] = d_value[:, 128:384].astype(low)
                dproj[span, 896:1152] = jnp.zeros((GROUP, 256), low)

            loop(tokens // GROUP, attention)
            for k in range(width // LANES):
                at = slice(k * LANES, (k + 1) * LANES)
                value = dot_tn(x[...], dproj[:, at])
                if k == width // LANES - 1:
                    value = value + dot_tn(lhs[...], mix_j[...])
                put(u, at, value)
                dacc[:, at] += dot_nt(dproj[:, 0:896], w[at, 0:896])
            stage_a(u)
            advance(u + 1)
        base_load.wait()

        def close_a(span, r=factor[1], level=level):
            value = turn_back(span, base, 0, 1, r)
            g[span, :] = value
            lhs[span, :] = value.astype(low)

        by_rows(close_a)
        strip = home_ref.shape[1]
        part, flock = strip // 2, frames // tps
        patches = strip * tps
        if level:
            base_load = bring(mid_ref.at[level - 1], base)
            away, stay = [], []
            for k in range(part // chunk):
                for f in range(flock):
                    to = pl.ds(pl.multiple_of(f * patches + t * strip + c * part + k * chunk, 16), chunk)
                    for peer in [None, twin] + chain + crossed:
                        _, pc, pt = peer or (p, c, t)
                        row = (k * 2 * frames + (pt * 2 + pc) * flock + f) * chunk
                        piece = lhs.at[pl.ds(pl.multiple_of(row, 16), chunk)]
                        if peer is None:
                            stay.append(links.local(piece, arrived.at[to]))
                        else:
                            away.append(links.remote(lambda s=piece, d=arrived.at[to], q=peer: (s, d, q))())
            for copy in away + stay:
                copy.start()
            for copy in away + stay:
                copy.wait()
            g[...] = arrived[...].astype(jnp.float32)
        else:
            for f in range(flock):
                for peer in [None] + chain:
                    pt = t if peer is None else peer[2]
                    piece = lhs.at[pl.ds(pl.multiple_of(f * patches + pt * strip, 16), strip)]
                    goal = home_ref.at[t * flock + f]
                    if peer is None:
                        tail.append(links.local(piece, goal))
                    else:
                        tail.append(links.remote(lambda s=piece, d=goal, q=peer: (s, d, q))())
            for copy in tail:
                copy.start()

    for k in range(6 * layers):
        line = jnp.sum(dmod_ref[k // 6, k % 6], axis=0, keepdims=True)
        for j in range(tps):
            d_cut[j, k : k + 1, :] = line[:, j * wide : (j + 1) * wide]
    own_slot = 2 * t + c
    cuts = [links.remote(lambda q=q: (d_cut.at[q[2]], d_in.at[own_slot], q))() for q in chain + crossed + [twin]]
    for copy in cuts:
        copy.start()
    d_in[own_slot] = d_cut[t]
    advance(units + 1)
    for copy in cuts:
        copy.wait_recv()
    total = d_in[0]
    for k in range(1, 2 * tps):
        total = total + d_in[k]
    d_all[p] = total
    clips = [links.remote(lambda q=q: (d_all.at[p], d_all.at[p], q))() for q in plane]
    for copy in clips:
        copy.start()
    advance(units + 2)
    for copy in clips:
        copy.wait_recv()

    share = jnp.zeros((8, rows), jnp.float32)
    for k in range(2 * layers):
        load = bring(mod_w.at[k // 2, pl.ds(3 * (k % 2), 3)], mod_in)
        load.wait()
        for j in range(3):
            at = 3 * k + j
            lines = jnp.concatenate([d_all[q, at : at + 1, :] for q in range(dps)] + [jnp.zeros((8 - dps, wide), jnp.float32)], axis=0)
            coarse = lines.astype(low)
            fine = (lines - coarse.astype(jnp.float32)).astype(low)
            weight = mod_in[j].astype(low)
            share = share + dot_nt(coarse, weight) + dot_nt(fine, weight)
    z_in[t] = share
    shares = [links.remote(lambda q=q: (z_in.at[t], z_in.at[t], q))() for q in chain]
    for copy in shares:
        copy.start()
    advance(units + 3)
    for copy in shares:
        copy.wait_recv()
    total = z_in[0]
    for k in range(1, tps):
        total = total + z_in[k]
    d_cond[p] = total
    homes = [links.remote(lambda q=q: (d_cond.at[p], d_cond.at[p], q))() for q in plane]
    for copy in homes:
        copy.start()
    advance(units + 4)

    gram = jnp.zeros((1, 1), jnp.float32)
    for a in range(dps):
        for b in range(dps):
            left = jnp.sum(cond_in[a, 0:1, :] * cond_in[b, 0:1, :], axis=1, keepdims=True)
            for level in range(layers):
                both = d_all[a, 6 * level : 6 * level + 6, :] * d_all[b, 6 * level : 6 * level + 6, :]
                right = jnp.sum(jnp.sum(both, axis=1, keepdims=True), axis=0, keepdims=True)
                gram = gram + left * right
    advance(units + 5)
    line = jnp.sum(jnp.sum(squares[...], axis=1, keepdims=True), axis=0, keepdims=True) + 0.5 * gram
    slot = 2 * p + c
    norm_in[slot] = jnp.broadcast_to(line, norm_ref.shape)
    sums = [links.remote(lambda q=q: (norm_in.at[slot], norm_in.at[slot], q))() for q in plane + across + [twin]]
    for copy in sums:
        copy.start()
    for copy in sums:
        copy.wait_recv()
    total = norm_in[0]
    for k in range(1, 2 * dps):
        total = total + norm_in[k]
    norm_line[t] = total
    lines = [links.remote(lambda q=q: (norm_line.at[t], norm_line.at[t], q))() for q in chain]
    for copy in lines:
        copy.start()
    for copy in lines:
        copy.wait_recv()
    total = norm_line[0]
    for k in range(1, tps):
        total = total + norm_line[k]
    norm_ref[...] = total
    for copy in homes:
        copy.wait_recv()
    for copy in cuts + clips + shares + homes + sums + lines:
        copy.wait_send()
    for u in range(units):
        if u >= units - 2:
            to_twin[u].wait_send()
        if u >= units - 2 * tps:
            to_corner[u].wait_send()
            to_x[u].wait_send()
            to_y[u].wait_send()
            if u in along:
                along[u].wait_send()
    for n in range(mats):
        finish[n].wait_recv()
    finish[mats - 1].wait_send()
    keep[mats - 1].wait()
    for copy in tail:
        copy.wait()


def backward_pass(full, cot_rows, modulation, cond_rows, mod_w, saved, mesh_shape, frames, strip):
    tps, dps = mesh_shape["tp"], mesh_shape["dp"]
    mats, _, depth, width = full.shape
    layers, tokens = saved[0].shape[:2]
    rows = depth // dps
    half = rows // 2
    wide = mod_w.shape[-1]
    heads = wide // HD
    low, wider = jnp.bfloat16, jnp.float32
    sds = jax.ShapeDtypeStruct
    whole = pl.BlockSpec(memory_space=pl.ANY)
    near = pl.BlockSpec(memory_space=pltpu.VMEM)
    return pl.pallas_call(
        partial(backward_kernel, tps, (layers, frames, heads * HD, heads)),
        out_shape=[
            sds((mats, rows, width), low),
            sds((frames, strip, width), low),
            sds((dps, 16, wide), wider),
            sds((dps, 8, rows), wider),
            sds((8, 128), wider),
        ],
        in_specs=[whole, whole, near, near] + [whole] * 11,
        out_specs=[whole, whole, near, near, near],
        scratch_shapes=[
            pltpu.VMEM((2, tps, dps, half, width), low),
            pltpu.VMEM((2, dps, rows, width), low),
            pltpu.VMEM((2, dps, half, width), low),
            pltpu.VMEM((tps, half, width), low),
            pltpu.VMEM((tps, half, width), low),
            pltpu.VMEM((tps, half, width), low),
            pltpu.VMEM((tps - 1, half, width), low),
            pltpu.VMEM((half, width), low),
            pltpu.VMEM((tokens, width), wider),
            pltpu.VMEM((tokens, width), wider),
            pltpu.VMEM((tokens, width), low),
            pltpu.VMEM((tokens, width), low),
            pltpu.VMEM((2, depth, width), low),
            pltpu.VMEM((2, tokens, width), low),
            pltpu.VMEM((tokens, width), wider),
            pltpu.VMEM((tps, tokens, width), low),
            pltpu.VMEM((2, tokens, LANES), low),
            pltpu.VMEM((tokens, width), wider),
            pltpu.VMEM((tokens, width), wider),
            pltpu.VMEM((tokens, width), low),
            pltpu.VMEM((tokens, width), low),
            pltpu.VMEM((layers, 6, 8, width), wider),
            pltpu.VMEM((tps, 16, wide), wider),
            pltpu.VMEM((2 * tps, 16, wide), wider),
            pltpu.VMEM((3, rows, wide), wider),
            pltpu.VMEM((tps, 8, rows), wider),
            pltpu.VMEM((8, width), wider),
            pltpu.VMEM((2 * dps, 8, 128), wider),
            pltpu.VMEM((tps, 8, 128), wider),
            pltpu.SemaphoreType.DMA((200,)),
            pltpu.SemaphoreType.DMA((200,)),
            pltpu.SemaphoreType.DMA((110,)),
            pltpu.SemaphoreType.REGULAR((5 * tps,)),
        ],
        compiler_params=pltpu.CompilerParams(
            collective_id=1, has_side_effects=True, vmem_limit_bytes=VMEM_LIMIT
        ),
        name="backward_pass",
    )(full, cot_rows.reshape(tokens, width), modulation, cond_rows, mod_w, *saved)


def sum_grads(grads):
    parts = []
    for grad in grads:
        part = lax.psum_scatter(grad, "tp", scatter_dimension=0, tiled=True)[0]
        part = lax.psum_scatter(part, "dp", scatter_dimension=0, tiled=True)
        parts.append(lax.psum(part, "ctx"))
    return jnp.stack(parts)


def update_kernel(wide, red_ref, norm_ref, cond_ref, lines_ref, *refs):
    masters, firsts, seconds = refs[0:5], refs[5:10], refs[10:15]
    news, copies, moments, squares = refs[15:20], refs[20:25], refs[25:30], refs[30:35]
    level, part = pl.program_id(0), pl.program_id(1)
    coef = CLIP_MAX / jnp.maximum(jnp.sqrt(norm_ref[0:1, 0:1]), CLIP_MAX)

    def step(kind, at, grad):
        new, copy, moment, square = adam_update(masters[kind][at], firsts[kind][at], seconds[kind][at], grad, coef)
        news[kind][at] = new
        copies[kind][at] = copy
        moments[kind][at] = moment
        squares[kind][at] = square

    rows = masters[0].shape[2]
    span = pl.ds(pl.multiple_of(part * rows, 32), rows)
    first = red_ref[0, span, :].astype(jnp.float32)
    for k in range(3):
        step(0, (0, k), first[:, k * wide : (k + 1) * wide])
    step(2, 0, red_ref[1, span, :].astype(jnp.float32))
    for k in range(3):

        @pl.when(part == k)
        def _(k=k):
            at = slice(k * LANES, (k + 1) * LANES)
            step(3, 0, red_ref[2, :, at].astype(jnp.float32).T)

    @pl.when(part == 0)
    def _():
        step(1, 0, red_ref[0, :, 3 * wide :].astype(jnp.float32).T)

    for k in range(2):
        lines = lines_ref[level * 6 + part * 2 + k]
        grad = cond_ref[:, 0:1] * lines[0:1, :]
        for q in range(1, lines_ref.shape[1]):
            grad = grad + cond_ref[:, q : q + 1] * lines[q : q + 1, :]
        step(4, (0, k), grad)


def update_all(reduced, norm, cond_columns, lines, masters, firsts, seconds):
    layers, _, rows, wide = masters[0].shape
    width = reduced.shape[-1]
    parts = 3
    blocks = (
        pl.BlockSpec((1, 3, rows // parts, wide), lambda l, q: (l, 0, q, 0)),
        pl.BlockSpec((1, wide, rows), lambda l, q: (l, 0, 0)),
        pl.BlockSpec((1, rows // parts, width), lambda l, q: (l, q, 0)),
        pl.BlockSpec((1, width // parts, rows), lambda l, q: (l, q, 0)),
        pl.BlockSpec((1, 6 // parts, rows, wide), lambda l, q: (l, q, 0, 0)),
    )
    small = [pl.BlockSpec(a.shape, lambda l, q, n=a.ndim: (0,) * n) for a in (norm, cond_columns, lines)]
    shapes = [[jax.ShapeDtypeStruct(w.shape, kind) for w in masters] for kind in (jnp.float32, jnp.bfloat16, jnp.float32, jnp.float32)]
    return pl.pallas_call(
        partial(update_kernel, wide),
        grid=(layers, parts),
        out_shape=sum(shapes, []),
        in_specs=[pl.BlockSpec((MATS, rows, width), lambda l, q: (l, 0, 0))] + small + list(blocks) * 3,
        out_specs=list(blocks) * 4,
        compiler_params=pltpu.CompilerParams(vmem_limit_bytes=VMEM_LIMIT),
        name="update_all",
    )(reduced, norm, cond_columns, lines, *masters, *firsts, *seconds)


def pack(qkv, out, up, down):
    rows = qkv.shape[0]
    low = jnp.bfloat16
    first = jnp.concatenate([qkv.astype(low).reshape(rows, -1), out.astype(low).T], axis=1)
    return jnp.stack([first, up.astype(low), down.astype(low).T])


def unpack(first, second, third, like):
    rows, _, wide = like.shape
    cut = 3 * wide
    return (first[:, :cut].reshape(rows, 3, wide), first[:, cut:].T, second, third.T)


def frames_whole(rows):
    return lax.all_to_all(rows, "tp", 0, 1, tiled=True)


def frames_back(rows):
    return lax.all_to_all(rows, "tp", 1, 0, tiled=True)


def patches_whole(rows):
    return lax.all_to_all(rows, ("tp", "ctx"), 1, 0, tiled=True)


def patches_back(rows):
    return lax.all_to_all(rows, ("tp", "ctx"), 0, 1, tiled=True)


def columns_home(rows, mesh_shape):
    frames, patches, width = rows.shape
    tps, cs = mesh_shape["tp"], mesh_shape["ctx"]
    split = rows.reshape(tps, cs, frames // (tps * cs), patches, width)
    split = split.transpose(1, 0, 2, 3, 4).reshape(cs, frames // cs, patches, width)
    return lax.all_to_all(split, "ctx", 0, 2, tiled=True)[0]


def columns_away(rows, mesh_shape):
    tps, cs = mesh_shape["tp"], mesh_shape["ctx"]
    frames, patches, width = rows.shape
    split = lax.all_to_all(rows[None], "ctx", 2, 0, tiled=True)
    split = split.reshape(cs, tps, frames // tps, patches // cs, width).transpose(1, 0, 2, 3, 4)
    return split.reshape(frames * cs, patches // cs, width)


def per_device_plain(mesh_shape, inputs, conditioning, *states):
    masters, firsts, seconds, cotangent = states[:5], states[5:10], states[10:15], states[15]
    qkv_weight, out_weight, up_weight, down_weight, mod_weight = masters
    low = jnp.bfloat16
    highest = lax.Precision.HIGHEST
    layers = qkv_weight.shape[0]
    scale = HD ** (-0.5)
    dp_at, _, tp_at = place()
    tps, dps = mesh_shape["tp"], mesh_shape["dp"]
    rows = qkv_weight.shape[1]
    wide = qkv_weight.shape[3]
    heads = wide // HD
    width = inputs.shape[-1]

    shards = jnp.concatenate(
        [pack(qkv_weight[l], out_weight[l], up_weight[l], down_weight[l]) for l in range(layers)]
    )
    full = gather_weights(shards)

    cond_low = jax.nn.silu(conditioning).astype(low)
    cond_all = lax.all_gather(cond_low, "dp", axis=0, tiled=True)
    cond_mine = lax.dynamic_slice_in_dim(cond_all, dp_at * rows, rows, 1)
    mod_low = mod_weight.astype(low)
    mod_part = jnp.einsum("cd,ldke->clke", cond_mine, mod_low, preferred_element_type=jnp.float32)
    mod_part = lax.psum_scatter(mod_part, "dp", scatter_dimension=0, tiled=True)
    modulation = lax.all_gather(mod_part, "tp", axis=3, tiled=True)[0]

    hidden = frames_whole(inputs[0]).astype(jnp.float32)
    saved = []
    for level in range(layers):
        if level:
            if level % 2 == 1:
                hidden = patches_whole(hidden.astype(low)).astype(jnp.float32)
            else:
                hidden = patches_back(hidden.astype(low)).astype(jnp.float32)
        forms = SPATIAL_FORMS if level % 2 == 0 else TEMPORAL_FORMS
        first_w, up_w, down_w = full[MATS * level], full[MATS * level + 1], full[MATS * level + 2]
        factors = modulation[level]
        frames, patches = hidden.shape[:2]
        normed_a, rstd_a = normalize(hidden)
        attn_in = (normed_a * (1.0 + factors[1]) + factors[0]).astype(low)
        projected = jnp.einsum(
            "fpd,jde->fpje", attn_in, first_w[:, :, : 3 * wide], preferred_element_type=jnp.float32
        ).astype(low)
        projected = projected.reshape(frames, patches, tps, 3, heads, HD)
        query, key, value = (projected[:, :, :, s] for s in range(3))
        mixed, log_total = attend(query, key, value, forms, scale)
        mixed = mixed.reshape(frames, patches, tps, wide)
        branch_a = jnp.einsum(
            "fpje,jde->fpd", mixed, first_w[:, :, 3 * wide :], preferred_element_type=jnp.float32
        )
        middle = hidden + factors[2] * branch_a
        normed_m, rstd_m = normalize(middle)
        mlp_in = (normed_m * (1.0 + factors[4]) + factors[3]).astype(low)
        hidden_pre = jnp.einsum("fpd,jdh->fpjh", mlp_in, up_w, preferred_element_type=jnp.float32)
        hidden_act = jax.nn.gelu(hidden_pre, approximate=True).astype(low)
        branch_m = jnp.einsum("fpjh,jdh->fpd", hidden_act, down_w, preferred_element_type=jnp.float32)
        saved.append(
            (forms, first_w, up_w, down_w, factors, normed_a, rstd_a, attn_in, query, key, value,
             mixed, log_total, branch_a, normed_m, rstd_m, mlp_in, hidden_pre, hidden_act, branch_m)
        )
        hidden = middle + factors[5] * branch_m
    temporal_end = layers % 2 == 0
    output = hidden.astype(low)
    output = columns_home(output, mesh_shape) if temporal_end else frames_back(output)
    upstream = columns_away(cotangent[0], mesh_shape) if temporal_end else frames_whole(cotangent[0])
    upstream = upstream.astype(jnp.float32)

    grads = [None] * (MATS * layers)
    d_mods = [None] * layers
    for level in reversed(range(layers)):
        (forms, first_w, up_w, down_w, factors, normed_a, rstd_a, attn_in, query, key, value,
         mixed, log_total, branch_a, normed_m, rstd_m, mlp_in, hidden_pre, hidden_act, branch_m) = saved[level]
        frames, patches = upstream.shape[:2]
        d_gate_m = jnp.sum(upstream * branch_m, axis=(0, 1))
        d_branch_m = (factors[5] * upstream).astype(low)
        grads[MATS * level + 2] = jnp.einsum(
            "fpd,fpjh->jdh", d_branch_m, hidden_act, preferred_element_type=jnp.float32
        ).astype(low)
        d_act = jnp.einsum("fpd,jdh->fpjh", d_branch_m, down_w, preferred_element_type=jnp.float32)
        slope_pull = jax.vjp(partial(jax.nn.gelu, approximate=True), hidden_pre)[1]
        d_pre = slope_pull(d_act)[0].astype(low)
        grads[MATS * level + 1] = jnp.einsum(
            "fpd,fpjh->jdh", mlp_in, d_pre, preferred_element_type=jnp.float32
        ).astype(low)
        d_mlp_in = jnp.einsum("fpjh,jdh->fpd", d_pre, up_w, preferred_element_type=jnp.float32)
        d_shift_m = jnp.sum(d_mlp_in, axis=(0, 1))
        d_scale_m = jnp.sum(d_mlp_in * normed_m, axis=(0, 1))
        upstream = upstream + normalize_back(d_mlp_in * (1.0 + factors[4]), normed_m, rstd_m)
        d_gate_a = jnp.sum(upstream * branch_a, axis=(0, 1))
        d_branch_a = (factors[2] * upstream).astype(low)
        grad_out = jnp.einsum("fpd,fpje->jde", d_branch_a, mixed, preferred_element_type=jnp.float32)
        d_mixed = jnp.einsum(
            "fpd,jde->fpje", d_branch_a, first_w[:, :, 3 * wide :], preferred_element_type=jnp.float32
        ).astype(low)
        d_mixed = d_mixed.reshape(frames, patches, tps, heads, HD)
        d_parts = attend_back(query, key, value, d_mixed, log_total, forms, scale)
        d_projected = jnp.stack(d_parts, axis=3).astype(low).reshape(frames, patches, tps, 3 * wide)
        grad_qkv = jnp.einsum("fpd,fpje->jde", attn_in, d_projected, preferred_element_type=jnp.float32)
        grads[MATS * level] = jnp.concatenate([grad_qkv, grad_out], axis=2).astype(low)
        d_attn_in = jnp.einsum(
            "fpje,jde->fpd", d_projected, first_w[:, :, : 3 * wide], preferred_element_type=jnp.float32
        )
        d_shift_a = jnp.sum(d_attn_in, axis=(0, 1))
        d_scale_a = jnp.sum(d_attn_in * normed_a, axis=(0, 1))
        upstream = upstream + normalize_back(d_attn_in * (1.0 + factors[1]), normed_a, rstd_a)
        d_mods[level] = jnp.stack([d_shift_a, d_scale_a, d_gate_a, d_shift_m, d_scale_m, d_gate_m])
        if level:
            if level % 2 == 1:
                upstream = patches_back(upstream.astype(low)).astype(jnp.float32)
            else:
                upstream = patches_whole(upstream.astype(low)).astype(jnp.float32)
    input_grad = frames_back(upstream.astype(low)).astype(jnp.float32)

    reduced = sum_grads([grads[m] for m in reversed(range(MATS * layers))])
    reduced = reduced.astype(jnp.float32)

    d_mod = lax.psum(jnp.stack(d_mods)[None], ("ctx", "tp"))
    d_mod_all = lax.all_gather(d_mod, "dp", axis=0, tiled=True)
    d_mod_mine = lax.dynamic_slice_in_dim(d_mod_all, tp_at * wide, wide, 3)
    grad_mod = jnp.einsum("cd,clke->ldke", cond_mine.astype(jnp.float32), d_mod_mine, precision=highest)
    cond_part = jnp.einsum("clke,ldke->cd", d_mod_mine, mod_low.astype(jnp.float32), precision=highest)
    cond_part = lax.all_gather(lax.psum(cond_part, "tp"), "dp", axis=1, tiled=True)
    cond_total = lax.dynamic_slice_in_dim(cond_part, dp_at * conditioning.shape[0], conditioning.shape[0], 0)
    cond_grad = jax.vjp(jax.nn.silu, conditioning)[1](cond_total)[0]

    order = list(reversed(range(MATS * layers)))
    per_level = [
        unpack(*[reduced[order.index(MATS * level + kind)] for kind in range(MATS)], qkv_weight[level])
        for level in range(layers)
    ]
    stacked = [jnp.stack([per_level[level][kind] for level in range(layers)]) for kind in range(4)]
    stacked.append(grad_mod)
    squares = jnp.zeros((), jnp.float32)
    for grad in stacked:
        squares = squares + jnp.sum(grad * grad)
    grad_norm = jnp.sqrt(lax.psum(squares, ("dp", "tp")))
    coef = CLIP_MAX / jnp.maximum(grad_norm, CLIP_MAX)
    updates = [
        adam_update(masters[kind], firsts[kind], seconds[kind], stacked[kind], coef) for kind in range(5)
    ]
    return (output[None], input_grad[None], cond_grad, grad_norm) + tuple(
        updates[kind][part] for part in range(4) for kind in range(5)
    )


def per_device(mesh_shape, inputs, conditioning, *states):
    if not by_hand(mesh_shape, inputs, states[0]):
        return per_device_plain(mesh_shape, inputs, conditioning, *states)
    states, cotangent = states[:15], states[15]
    states = [s.transpose(0, 2, 1, 3) if s.ndim == 4 else s for s in states]
    masters, firsts, seconds = states[:5], states[5:10], states[10:15]
    dp_at, _, _ = place()
    dps = mesh_shape["dp"]
    frames, strip, width = inputs.shape[1:]
    layers, _, rows, wide = masters[0].shape

    cond_low = jax.nn.silu(conditioning).astype(jnp.bfloat16).astype(jnp.float32)
    cond = jnp.broadcast_to(cond_low.reshape(dps, 1, rows), (dps, 8, rows))
    full, output, cot_rows, *saved, modulation, cond_rows = forward_pass(masters, cond, inputs[0], cotangent[0], mesh_shape)
    reduced, home, d_all, d_cond, norm = backward_pass(
        full, cot_rows, modulation, cond_rows, masters[4], saved, mesh_shape, frames, strip
    )
    updates = update_all(
        reduced, norm, cond_rows[:, 0, :].T, d_all[:, : 6 * layers].transpose(1, 0, 2), masters, firsts, seconds
    )
    updates = [u.transpose(0, 2, 1, 3) if u.ndim == 4 else u for u in updates]
    d_cond = lax.dynamic_slice_in_dim(d_cond, dp_at, 1, 1).reshape(1, dps * rows)
    cond_grad = jax.vjp(jax.nn.silu, conditioning)[1](d_cond)[0]
    input_grad = home.astype(jnp.float32)
    output = output.reshape(1, frames, strip, width)
    return (output, input_grad[None], cond_grad, jnp.sqrt(norm[0, 0])) + tuple(updates)


def solution(mesh):
    weights = (
        P(None, "dp", None, "tp"),
        P(None, "tp", "dp"),
        P(None, "dp", "tp"),
        P(None, "tp", "dp"),
        P(None, "dp", None, "tp"),
    )
    rows = P("dp", "ctx", "tp", None)
    return jax.shard_map(
        partial(per_device, dict(mesh.shape)),
        mesh=mesh,
        in_specs=(rows, P("dp", None)) + weights * 3 + (rows,),
        out_specs=(rows, rows, P("dp", None), P()) + weights * 4,
        check_vma=False,
    )
```

```python
from functools import partial

import jax
import jax.numpy as jnp
from jax import lax
from jax.experimental import pallas as pl
from jax.experimental.pallas import tpu as pltpu
from jax.sharding import PartitionSpec as P

HD = 72
STEP = 5
EPS_NORM = 1e-06
LEARN_RATE = 0.03
DECAY_RATE = 0.1
BETA_ONE = 0.5
BETA_TWO = 0.5
ADAM_EPS = 1e-08
CLIP_MAX = 1.0
MESH = pl.DeviceIdType.MESH
MATS = 3
VMEM_LIMIT = 62 * 1024 * 1024
LANES = 384
SLOTS = 2
GROUP = 256
LAGS = (5, 1, 3)
RING = 4
SPATIAL_FORMS = ("fqjhe,fkjhe->fjhqk", "fjhqk,fkjhe->fqjhe", "fjhqk,fqjhe->fkjhe")
TEMPORAL_FORMS = ("qpjhe,kpjhe->pjhqk", "pjhqk,kpjhe->qpjhe", "pjhqk,qpjhe->kpjhe")


def normalize(rows):
    centred = rows - jnp.mean(rows, axis=-1, keepdims=True)
    rstd = lax.rsqrt(jnp.mean(centred * centred, axis=-1, keepdims=True) + EPS_NORM)
    return (centred * rstd, rstd)


def normalize_back(grad, normed, rstd):
    return rstd * (
        grad
        - jnp.mean(grad, axis=-1, keepdims=True)
        - normed * jnp.mean(grad * normed, axis=-1, keepdims=True)
    )


def attend(query, key, value, forms, scale):
    scores = jnp.einsum(forms[0], query, key, preferred_element_type=jnp.float32) * scale
    top = jnp.max(scores, axis=-1, keepdims=True)
    expo = jnp.exp(scores - top)
    total = jnp.sum(expo, axis=-1, keepdims=True)
    probs = (expo / total).astype(jnp.bfloat16)
    mixed = jnp.einsum(forms[1], probs, value, preferred_element_type=jnp.float32)
    return (mixed.astype(jnp.bfloat16), top + jnp.log(total))


def attend_back(query, key, value, d_mixed, log_total, forms, scale):
    scores = jnp.einsum(forms[0], query, key, preferred_element_type=jnp.float32) * scale
    probs = jnp.exp(scores - log_total)
    d_probs = jnp.einsum(forms[0], d_mixed, value, preferred_element_type=jnp.float32)
    d_scores = (probs * (d_probs - jnp.sum(probs * d_probs, axis=-1, keepdims=True))).astype(
        jnp.bfloat16
    )
    d_value = jnp.einsum(
        forms[2], probs.astype(jnp.bfloat16), d_mixed, preferred_element_type=jnp.float32
    )
    d_query = jnp.einsum(forms[1], d_scores, key, preferred_element_type=jnp.float32) * scale
    d_key = jnp.einsum(forms[2], d_scores, query, preferred_element_type=jnp.float32) * scale
    return (d_query, d_key, d_value)


def adam_update(master, first, second, grad, coef):
    clipped = coef * grad
    first_new = BETA_ONE * first + (1.0 - BETA_ONE) * clipped
    second_new = BETA_TWO * second + (1.0 - BETA_TWO) * clipped * clipped
    first_hat = first_new / (1.0 - BETA_ONE**STEP)
    second_hat = second_new / (1.0 - BETA_TWO**STEP)
    master_new = master - LEARN_RATE * (
        first_hat / (jnp.sqrt(second_hat) + ADAM_EPS) + DECAY_RATE * master
    )
    return (master_new, master_new.astype(jnp.bfloat16), first_new, second_new)


def place():
    return lax.axis_index("dp"), lax.axis_index("ctx"), lax.axis_index("tp")


def greet(peers):
    barrier = pltpu.get_barrier_semaphore()
    for peer in peers:
        pl.semaphore_signal(barrier, inc=1, device_id=peer, device_id_type=MESH)
    pl.semaphore_wait(barrier, len(peers))


def by_hand(mesh_shape, inputs, qkv_weight):
    tps, cs = mesh_shape["tp"], mesh_shape["ctx"]
    layers, rows, _, wide = qkv_weight.shape
    clips, frames, strip, width = inputs.shape
    return (
        mesh_shape["dp"] == 4 and cs == 2 and tps == 4 and clips == 1 and layers == 2 and rows % 32 == 0
        and wide == 4 * HD and 4 * wide == width and width % LANES == 0 and frames == 2 * tps
        and strip * tps == GROUP and frames * cs == 16 and strip == 64
    )


def gather_weights(shards):
    full = lax.all_gather(shards, "dp", axis=1, tiled=True)
    return lax.all_gather(full, "tp", axis=1, tiled=False)


class Links:
    def __init__(self, send_sem, recv_sem, local_sem):
        self.send_sem, self.recv_sem, self.local_sem = send_sem, recv_sem, local_sem
        self.used, self.used_local = 0, 0

    def remote(self, make):
        at = self.used
        self.used += 1

        def build(*args):
            src, dst, peer = make(*args)
            return pltpu.make_async_remote_copy(
                src_ref=src, dst_ref=dst, send_sem=self.send_sem.at[at], recv_sem=self.recv_sem.at[at],
                device_id=peer, device_id_type=MESH,
            )

        return build

    def local(self, src, dst):
        at = self.used_local
        self.used_local += 1
        return pltpu.make_async_copy(src, dst, self.local_sem.at[at])


def lane_mask(shape, low, high):
    lane = lax.broadcasted_iota(jnp.int32, shape, 1)
    return jnp.logical_and(lane >= low, lane < high)


def dot_nn(a, b):
    return lax.dot_general(a, b, (((1,), (0,)), ((), ())), preferred_element_type=jnp.float32)


def dot_nt(a, b):
    return lax.dot_general(a, b, (((1,), (1,)), ((), ())), preferred_element_type=jnp.float32)


def dot_tn(a, b):
    return lax.dot_general(a, b, (((0,), (0,)), ((), ())), preferred_element_type=jnp.float32)


def softmax_rows(scores, columns):
    if columns:
        rows = lax.broadcasted_iota(jnp.int32, scores.shape, 0)
        cols = lax.broadcasted_iota(jnp.int32, scores.shape, 1)
        scores = jnp.where((rows & (columns - 1)) == (cols & (columns - 1)), scores, -1e30)
    top = jnp.max(scores, axis=-1, keepdims=True)
    expo = jnp.exp(scores - top)
    return expo * (1.0 / jnp.sum(expo, axis=-1, keepdims=True))


def head_stack(rows, first, heads):
    return jnp.concatenate(
        [jnp.where(lane_mask(rows.shape, first + h * HD, first + (h + 1) * HD), rows, jnp.zeros_like(rows)) for h in range(heads)],
        axis=0,
    )


def head_merge(stacked, first, heads):
    size = stacked.shape[0] // heads
    total = jnp.zeros((size, stacked.shape[1]), stacked.dtype)
    for h in range(heads):
        part = stacked[h * size : (h + 1) * size]
        total = jnp.where(lane_mask(part.shape, first + h * HD, first + (h + 1) * HD), part, total)
    return total


def forward_kernel(tps, geometry, *refs):
    layers, frames, wide, heads = geometry
    (qkv_w, out_w, up_w, down_w, mod_w, cond_ref, rows_ref, cot_ref,
     full_ref, out_ref, cot_out, hid_out, mid_out, bra_out, brm_out, xa_out, xm_out, qkv_out, mix_out, pre_out, act_out, mod_ref, cond_in,
     hid, mid, acc_a, acc_m, x_a, x_m, wbuf, act, pre, qkv, mix, rows_in, moved, turned,
     packed, wide_in, out_in, up_in, down_in, mod_in, part, part_in, columns,
     send_sem, recv_sem, local_sem) = refs
    p, c, t = place()
    mats, rows, width = packed.shape
    tokens = hid.shape[1]
    half = rows // 2
    own_half = pl.multiple_of(c * half, 16)
    beside, above, twin = (p ^ 1, c, t), (p ^ 2, c, t), (p, 1 - c, t)
    chain = [(p, c, lax.rem(t + k, tps)) for k in range(1, tps)]
    crossed = [(p, 1 - c, lax.rem(t + k, tps)) for k in range(1, tps)]
    plane = [(p ^ k, c, t) for k in range(1, 4)]
    links = Links(send_sem, recv_sem, local_sem)
    low = jnp.bfloat16

    arrivals = {}
    for level in range(layers):
        arrivals[level] = (
            links.local(qkv_w.at[level], wide_in.at[level]), links.local(out_w.at[level], out_in.at[level]),
            links.local(up_w.at[level], up_in.at[level]), links.local(down_w.at[level], down_in.at[level]),
        )
        for copy in arrivals[level]:
            copy.start()
    mod_loads = [links.local(mod_w.at[k // 2, pl.ds(3 * (k % 2), 3)], mod_in.at[k % 2]) for k in range(2 * layers)]
    mod_loads[0].start()
    mod_loads[1].start()
    greet(chain + crossed + plane + [twin])
    cond_copies = [links.remote(lambda q=q: (cond_ref.at[q[0]], cond_in.at[p], q))() for q in plane]
    cond_own = links.local(cond_ref.at[p], cond_in.at[p])
    for copy in cond_copies + [cond_own]:
        copy.start()

    def rows_of(owner):
        return pl.ds(pl.multiple_of(owner * rows + own_half, 16), half)

    def block(m, k, owner):
        return full_ref.at[m, lax.rem(t + tps - k, tps), rows_of(owner)]

    def column(m, owner):
        return full_ref.at[m, :, rows_of(owner)]

    def own(m):
        return packed.at[m, pl.ds(own_half, half)]

    keep, along, to_x, to_y, corner, to_twin = {}, {}, {}, {}, {}, {}
    for m in range(mats):
        keep[m] = links.local(own(m), block(m, 0, p))
        for k in range(tps):
            if k:
                along[m, k] = links.remote(lambda m=m, k=k: (own(m), block(m, 0, p), chain[k - 1]))()
            source = own(m) if k == 0 else block(m, k, p)
            to_x[m, k] = links.remote(lambda m=m, k=k, s=source: (s, block(m, k, p), beside))()
            to_y[m, k] = links.remote(lambda m=m, k=k, s=source: (s, block(m, k, p), above))()
            if k % 2 == 0:
                corner[m, k] = links.remote(lambda m=m, k=k: (block(m, k, p ^ 1), block(m, k, p ^ 1), above))()
            else:
                corner[m, k] = links.remote(lambda m=m, k=k: (block(m, k, p ^ 2), block(m, k, p ^ 2), beside))()
        for which in range(4):
            owner = (p, p ^ 1, p ^ 2, p ^ 3)[which]
            to_twin[m, which] = links.remote(lambda m=m, o=owner: (column(m, o), column(m, o), twin))()

    def unit(step):
        for m in range(1, mats):
            if step == (tps - 1 if m == 1 else tps * (m - 1) + 1):
                for j in range(1, tps):
                    along[m, j].start()
        if step < mats * tps:
            m, k = divmod(step, tps)
            if k:
                along[m, k].wait_recv()
                to_x[m, k].start()
                to_y[m, k].start()
            if k == tps - 1:
                keep[m].wait()
                to_twin[m, 0].start()
        if 0 <= step - 3 < mats * tps:
            m, k = divmod(step - 3, tps)
            to_x[m, k].wait_recv()
            if k % 2 == 0:
                corner[m, k].start()
            to_y[m, k].wait_recv()
            if k % 2:
                corner[m, k].start()
            if k == tps - 1:
                to_twin[m, 1].start()
                to_twin[m, 2].start()
        if 0 <= step - 6 < mats * tps:
            m, k = divmod(step - 6, tps)
            corner[m, k].wait_recv()
            if k == tps - 1:
                to_twin[m, 3].start()

    def prepare(m):
        level, kind = divmod(m, MATS)
        if kind == 0:
            arrivals[level][0].wait()
            arrivals[level][1].wait()
            for k in range(3):
                packed[m, :, k * wide : (k + 1) * wide] = wide_in[level, k].astype(low)
            packed[m, :, 3 * wide :] = out_in[level].T.astype(low)
        elif kind == 1:
            arrivals[level][2].wait()
            packed[m] = up_in[level].astype(low)
        else:
            arrivals[level][3].wait()
            packed[m] = down_in[level].astype(low)
        keep[m].start()
        to_x[m, 0].start()
        to_y[m, 0].start()
        if m == 0:
            for j in range(1, tps):
                along[m, j].start()

    prepare(0)
    for copy in cond_copies:
        copy.wait_recv()
    cond_own.wait()
    cond_rows = cond_in[...].reshape(-1, rows).astype(low)
    for k in range(2 * layers):
        mod_loads[k].wait()
        for j in range(3):
            value = dot_nn(cond_rows, mod_in[k % 2, j].astype(low))
            part[:, 3 * k + j] = value.reshape(part.shape[0], 8, wide)
        if k + 2 < 2 * layers:
            mod_loads[k + 2].start()
    part_copies = [links.remote(lambda q=q: (part.at[q[0]], part_in.at[p], q))() for q in plane]
    for copy in part_copies:
        copy.start()
    part_in[p] = part[p]
    for m in range(1, mats):
        prepare(m)
    column_copies = [links.remote(lambda q=q: (columns.at[t], columns.at[t], q))() for q in chain]

    def add_parts():
        for copy in part_copies:
            copy.wait_recv()
        columns[t] = part_in[0] + part_in[1] + part_in[2] + part_in[3]
        for copy in column_copies:
            copy.start()

    def join_columns():
        for copy in column_copies:
            copy.wait_recv()
        for k in range(6 * layers):
            for j in range(tps):
                mod_ref[k // 6, k % 6, :, j * wide : (j + 1) * wide] = columns[j, k]

    progress = [0]

    def tick():
        if progress[0] < mats * tps + 6:
            unit(progress[0])
            progress[0] += 1

    def arrive(m):
        while progress[0] < tps * m + tps + 6:
            tick()
        for which in range(4):
            to_twin[m, which].wait_recv()

    loads = {}

    def fetch(m, j):
        if (m, j) not in loads and m < mats:
            loads[m, j] = links.local(full_ref.at[m, j], wbuf.at[(m * tps + j) % SLOTS])
            loads[m, j].start()

    flock = frames // tps
    patches = rows_in.shape[1]
    strip = patches // tps

    def strip_of(owner):
        return pl.ds(pl.multiple_of(owner * strip, 16), strip)

    spread_rows = [
        links.remote(lambda k=k: (rows_ref.at[chain[k - 1][2]], rows_in.at[:, strip_of(t)], chain[k - 1]))() for k in range(1, tps)
    ]
    keep_rows = links.local(rows_ref.at[t], rows_in.at[:, strip_of(t)])

    part = strip // 2
    chunk = turned.shape[2]
    cot_copies = []
    for g in range(part // chunk):
        there = pl.ds(pl.multiple_of((1 - c) * part + g * chunk, 16), chunk)
        here = pl.ds(pl.multiple_of(c * part + g * chunk, 16), chunk)
        cot_copies.append(links.remote(lambda g=g, s=there: (cot_ref.at[:, :, s], cot_out.at[g, :, c], twin))())
        cot_copies.append(links.local(cot_ref.at[:, :, here], cot_out.at[g, :, c]))
    for copy in cot_copies:
        copy.start()

    saves = []

    def save(src, dst):
        copy = links.local(src, dst)
        copy.start()
        return copy

    def by_rows(body, size=64):
        def one(i, carry):
            body(pl.ds(pl.multiple_of(i * size, size), size))
            return carry

        lax.fori_loop(0, tokens // size, one, 0)

    def loop(count, body):
        def one(i, carry):
            body(i)
            return carry

        lax.fori_loop(0, count, one, 0)

    pending = {}

    def settle(name):
        if name in pending:
            for copy in pending.pop(name):
                copy.wait()

    for level in range(layers):
        hidden = hid.at[level]
        middle = mid.at[level]
        temporal = level % 2 == 1
        first, second, third = MATS * level, MATS * level + 1, MATS * level + 2
        if level == 0:
            tick()
            tick()
            add_parts()
            tick()
            tick()
            for copy in spread_rows + [keep_rows]:
                copy.start()
            tick()
            join_columns()
            for copy in spread_rows:
                copy.wait_recv()
            keep_rows.wait()
            for f in range(flock):
                loop(patches // 64, lambda i, f=f: hidden.__setitem__(
                    pl.ds(pl.multiple_of(f * patches + i * 64, 64), 64),
                    rows_in[f, pl.ds(pl.multiple_of(i * 64, 64), 64), :].astype(jnp.float32)))
        settle("x_a")
        factor = [mod_ref[level, k, 0:1, :] for k in range(6)]

        def enter(span, source=hidden, to=x_a, s=factor[0], r=factor[1]):
            normed, _ = normalize(source[span, :])
            to[span, :] = (normed * (1.0 + r) + s).astype(low)

        by_rows(enter)
        pending["x_a"] = [save(x_a, xa_out.at[level])]
        saves.append(save(hidden, hid_out.at[level]))
        settle("acc_a")
        acc_a[...] = jnp.zeros_like(acc_a)
        arrive(first)
        fetch(first, 0)
        for j in range(tps):
            tick()
            fetch(first, j + 1) if j + 1 < tps else None
            loads[first, j].wait()
            w = wbuf.at[(first * tps + j) % SLOTS]
            settle(("qkv", j % 2))
            settle(("mix", j % 2))
            qkv_j, mix_j = qkv.at[j % 2], mix.at[j % 2]

            def attention(g):
                span = pl.ds(pl.multiple_of(g * GROUP, GROUP), GROUP)
                x = x_a[span, :]
                q = dot_nn(x, w[:, 0:LANES])
                q = jnp.where(lane_mask(q.shape, 0, wide), q, 0.0).astype(low)
                k = pltpu.roll(dot_nn(x, w[:, 256 : 256 + LANES]), LANES - 32, 1)
                k = jnp.where(lane_mask(k.shape, 0, wide), k, 0.0).astype(low)
                v = pltpu.roll(dot_nn(x, w[:, 512 : 512 + LANES]), 32, 1)
                v = jnp.where(lane_mask(v.shape, LANES - wide, LANES), v, 0.0).astype(low)
                qkv_j[span, 0:LANES] = q
                qkv_j[span, LANES : 2 * LANES] = k
                qkv_j[span, 2 * LANES : 3 * LANES] = v
                scores = dot_nt(head_stack(q, 0, heads), k) * (HD ** (-0.5))
                probs = softmax_rows(scores, chunk if temporal else 0).astype(low)
                mixed = head_merge(dot_nn(probs, v), LANES - wide, heads).astype(low)
                mix_j[span, :] = mixed
                for i in range(width // LANES):
                    at = slice(i * LANES, (i + 1) * LANES)
                    acc_a[span, at] += dot_nt(mixed, w[at, 768 : 768 + LANES])

            loop(tokens // GROUP, attention)
            pending["qkv", j % 2] = [save(qkv_j, qkv_out.at[level, j])]
            pending["mix", j % 2] = [save(mix_j, mix_out.at[level, j])]
        settle("x_m")

        def between(span, hidden=hidden, middle=middle, gate=factor[2], s=factor[3], r=factor[4]):
            rows_mid = hidden[span, :] + gate * acc_a[span, :]
            middle[span, :] = rows_mid
            normed, _ = normalize(rows_mid)
            x_m[span, :] = (normed * (1.0 + r) + s).astype(low)

        by_rows(between)
        pending["acc_a"] = [save(acc_a, bra_out.at[level])]
        pending["x_m"] = [save(x_m, xm_out.at[level])]
        saves.append(save(middle, mid_out.at[level]))
        arrive(second)
        fetch(second, 0)
        for j in range(tps):
            tick()
            fetch(second, j + 1) if j + 1 < tps else None
            loads[second, j].wait()
            w = wbuf.at[(second * tps + j) % SLOTS]
            settle(("pre", j % 2))
            settle(("act", j))
            pre_j, act_j = pre.at[j % 2], act.at[j]

            def raise_up(i):
                at = pl.ds(pl.multiple_of(i * LANES, LANES), LANES)
                value = dot_nn(x_m[...], w[:, at])
                pre_j[:, at] = value
                act_j[:, at] = jax.nn.gelu(value, approximate=True).astype(low)

            loop(width // LANES, raise_up)
            pending["pre", j % 2] = [save(pre_j, pre_out.at[level, j])]
            pending["act", j] = [save(act_j, act_out.at[level, j])]
        settle("acc_m")
        acc_m[...] = jnp.zeros_like(acc_m)
        arrive(third)
        fetch(third, 0)
        for j in range(tps):
            tick()
            fetch(third, j + 1) if j + 1 < tps else None
            loads[third, j].wait()
            w = wbuf.at[(third * tps + j) % SLOTS]
            act_j = act.at[j]

            def lower(i):
                at = pl.ds(pl.multiple_of(i * LANES, LANES), LANES)
                acc_m[:, at] += dot_nt(act_j[...], w[at, :])

            loop(width // LANES, lower)
        if level + 1 < layers:
            def leave(span, middle=middle, gate=factor[5]):
                moved[span, :] = (middle[span, :] + gate * acc_m[span, :]).astype(low)

            by_rows(leave)
            pending["acc_m"] = [save(acc_m, brm_out.at[level])]
            away, stay = [], []
            here = (t * 2 + c) * flock
            for g in range(part // chunk):
                for f in range(flock):
                    goal = turned.at[g, here + f]
                    for peer in [None, twin] + chain + crossed:
                        _, pc, pt = peer or (p, c, t)
                        first_row = f * patches + pt * strip + pc * part + g * chunk
                        piece = moved.at[pl.ds(pl.multiple_of(first_row, 16), chunk)]
                        if peer is None:
                            stay.append(links.local(piece, goal))
                        else:
                            away.append(links.remote(lambda s=piece, d=goal, q=peer: (s, d, q))())
            for copy in away + stay:
                copy.start()
            tick()
            for copy in away:
                copy.wait()
            for copy in stay:
                copy.wait()
            nxt = hid.at[level + 1]
            for g in range(part // chunk):
                for f in range(turned.shape[1]):
                    base = (g * turned.shape[1] + f) * chunk
                    nxt[base : base + chunk, :] = turned[g, f].astype(jnp.float32)
        else:
            for g in range(part // chunk):
                for f in range(turned.shape[1]):
                    base = (g * turned.shape[1] + f) * chunk
                    span = slice(base, base + chunk)
                    turned[g, f] = (middle[span, :] + factor[5] * acc_m[span, :]).astype(low)
            pending["acc_m"] = [save(acc_m, brm_out.at[level])]
            home_copies = []
            for g in range(part // chunk):
                for ts in range(tps):
                    for f in range(flock):
                        to = pl.ds(pl.multiple_of(c * part + g * chunk, 16), chunk)
                        theirs = turned.at[g, (ts * 2 + 1 - c) * flock + f]
                        ours = turned.at[g, (ts * 2 + c) * flock + f]
                        home_copies.append(links.remote(lambda s=theirs, d=out_ref.at[ts, f, to]: (s, d, twin))())
                        home_copies.append(links.local(ours, out_ref.at[ts, f, to]))
            for copy in home_copies:
                copy.start()
    while progress[0] < mats * tps + 6:
        tick()
    for copy in saves + cot_copies + home_copies:
        copy.wait()
    for name in list(pending):
        settle(name)
    for copy in spread_rows + cond_copies + part_copies + column_copies:
        copy.wait_send()
    for m in range(mats):
        for which in range(4):
            to_twin[m, which].wait_send()
        for k in range(tps):
            if k:
                along[m, k].wait_send()
            to_x[m, k].wait_send()
            to_y[m, k].wait_send()
            corner[m, k].wait_send()


def forward_pass(masters, cond, rows, cot, mesh_shape):
    tps, dps, cs = mesh_shape["tp"], mesh_shape["dp"], mesh_shape["ctx"]
    qkv_w, out_w, up_w, down_w, mod_w = masters
    layers, _, depth, wide = qkv_w.shape
    heads = wide // HD
    mats, width = MATS * layers, rows.shape[-1]
    frames, strip = rows.shape[:2]
    flock = frames // tps
    tokens = frames * strip
    patches = strip * tps
    chunk = GROUP // (frames * cs)
    groups = strip // cs // chunk
    low, wider = jnp.bfloat16, jnp.float32
    sds = jax.ShapeDtypeStruct
    whole = pl.BlockSpec(memory_space=pl.ANY)
    return pl.pallas_call(
        partial(forward_kernel, tps, (layers, frames, wide, heads)),
        out_shape=[
            sds((mats, tps, dps * depth, width), low),
            sds((tps, flock, strip, width), low),
            sds((groups, tps, cs, flock, chunk, width), low),
            sds((layers, tokens, width), wider),
            sds((layers, tokens, width), wider),
            sds((layers, tokens, width), wider),
            sds((layers, tokens, width), wider),
            sds((layers, tokens, width), low),
            sds((layers, tokens, width), low),
            sds((layers, tps, tokens, 3 * LANES), low),
            sds((layers, tps, tokens, LANES), low),
            sds((layers, tps, tokens, width), wider),
            sds((layers, tps, tokens, width), low),
            sds((layers, 6, 8, width), wider),
            sds((dps, 8, depth), wider),
        ],
        in_specs=[whole] * 8,
        out_specs=[whole] * 13 + [pl.BlockSpec(memory_space=pltpu.VMEM)] * 2,
        scratch_shapes=[
            pltpu.VMEM((layers, tokens, width), wider),
            pltpu.VMEM((layers, tokens, width), wider),
            pltpu.VMEM((tokens, width), wider),
            pltpu.VMEM((tokens, width), wider),
            pltpu.VMEM((tokens, width), low),
            pltpu.VMEM((tokens, width), low),
            pltpu.VMEM((SLOTS, dps * depth, width), low),
            pltpu.VMEM((tps, tokens, width), low),
            pltpu.VMEM((2, tokens, width), wider),
            pltpu.VMEM((2, tokens, 3 * LANES), low),
            pltpu.VMEM((2, tokens, LANES), low),
            pltpu.VMEM((flock, patches, width), low),
            pltpu.VMEM((tokens, width), low),
            pltpu.VMEM((groups, frames * cs, chunk, width), low),
            pltpu.VMEM((mats, depth, width), low),
            pltpu.VMEM(qkv_w.shape, wider),
            pltpu.VMEM(out_w.shape, wider),
            pltpu.VMEM(up_w.shape, wider),
            pltpu.VMEM(down_w.shape, wider),
            pltpu.VMEM((2, 3, depth, wide), wider),
            pltpu.VMEM((dps, 6 * layers, 8, wide), wider),
            pltpu.VMEM((dps, 6 * layers, 8, wide), wider),
            pltpu.VMEM((tps, 6 * layers, 8, wide), wider),
            pltpu.SemaphoreType.DMA((200,)),
            pltpu.SemaphoreType.DMA((200,)),
            pltpu.SemaphoreType.DMA((140,)),
        ],
        compiler_params=pltpu.CompilerParams(
            collective_id=0, has_side_effects=True, vmem_limit_bytes=VMEM_LIMIT
        ),
        name="forward_pass",
    )(qkv_w, out_w, up_w, down_w, mod_w, cond, rows.reshape(tps, flock, strip, width), cot.reshape(tps, flock, strip, width))


def gelu_slope(v):
    root, cubic = 0.7978845608028654, 0.044715
    square = v * v
    bend = jnp.tanh(root * v * (1.0 + cubic * square))
    return 0.5 * (1.0 + bend) + 0.5 * v * (1.0 - bend * bend) * (root * (1.0 + 3.0 * cubic * square))


def backward_kernel(tps, geometry, *refs):
    layers, frames, wide, heads = geometry
    (full_ref, cot_ref, mod_ref, cond_in, mod_w, hid_ref, mid_ref, bra_ref, brm_ref, xa_ref, xm_ref, qkv_ref, mix_ref, pre_ref, act_ref,
     red_ref, home_ref, d_all, d_cond, norm_ref,
     tot, grad, twin_in, corner_in, beside_in, above_in, chain_in, last,
     g, dacc, lhs, x, wbuf, side, pre, dpre, mix, branch, base, arrived,
     dmod_ref, d_cut, d_in, mod_in, z_in, squares, norm_in, norm_line,
     send_sem, recv_sem, local_sem, free_sem) = refs
    p, c, t = place()
    mats = full_ref.shape[0]
    half, width = last.shape
    rows = 2 * half
    depth = full_ref.shape[2]
    dps = depth // rows
    tokens = g.shape[0]
    low = jnp.bfloat16
    mine = pl.ds(pl.multiple_of(c * half, 16), half)
    theirs = pl.ds(pl.multiple_of((1 - c) * half, 16), half)
    beside, above, twin = (p ^ 1, c, t), (p ^ 2, c, t), (p, 1 - c, t)
    chain = [(p, c, lax.rem(t + k, tps)) for k in range(1, tps)]
    crossed = [(p, 1 - c, lax.rem(t + k, tps)) for k in range(1, tps)]
    plane = [(p ^ k, c, t) for k in range(1, 4)]
    across = [(p ^ k, 1 - c, t) for k in range(1, 4)]
    greet(chain + crossed + plane + across + [twin])
    links = Links(send_sem, recv_sem, local_sem)
    units = mats * tps
    kinds = [(level, kind) for level in reversed(range(layers)) for kind in (2, 1, 0)]

    TWIN, CHAIN, CORNER, BESIDE, ABOVE = 0, 2, 2 + tps, 2 + tps + RING, 2 + tps + 2 * RING

    def credit(slot, peer, u, gap):
        if u + gap < units:
            pl.semaphore_signal(free_sem.at[slot], inc=1, device_id=peer, device_id_type=MESH)

    def spend(slot, u, gap):
        if u >= gap:
            pl.semaphore_wait(free_sem.at[slot], 1)

    to_twin, to_corner, to_x, to_y, along, finish, keep = {}, {}, {}, {}, {}, {}, {}
    for u in range(units):
        n, i = divmod(u, tps)
        here = tot.at[n % 2, i]
        to_twin[u] = links.remote(lambda u=u: (grad.at[u % 2, :, theirs], twin_in.at[u % 2], twin))()
        via = beside if i % 2 == 0 else above
        to_corner[u] = links.remote(lambda h=here, u=u, v=via: (h.at[p ^ 3], corner_in.at[u % RING], v))()
        to_x[u] = links.remote(lambda h=here, u=u: (h.at[p ^ 1], beside_in.at[u % RING], beside))()
        to_y[u] = links.remote(lambda h=here, u=u: (h.at[p ^ 2], above_in.at[u % RING], above))()
        if i < tps - 1:
            along[u] = links.remote(lambda h=here, i=i: (h.at[p], chain_in.at[i], chain[i]))()
        else:
            level, kind = kinds[n]
            goal = red_ref.at[MATS * level + kind, mine]
            finish[n] = links.remote(lambda d=goal: (last, d, twin))()
            keep[n] = links.local(last, goal)

    def plus(a, b):
        return (a.astype(jnp.float32) + b.astype(jnp.float32)).astype(low)

    def release(u):
        if u >= 2:
            to_twin[u - 2].wait_send()
        n, i = divmod(u, tps)
        if n >= 2:
            old = u - 2 * tps
            to_corner[old].wait_send()
            to_x[old].wait_send()
            to_y[old].wait_send()
            if i < tps - 1:
                along[old].wait_send()

    def stage_a(u):
        spend(TWIN + u % 2, u, 2)
        to_twin[u].start()

    def stage_b(u):
        n, i = divmod(u, tps)
        to_twin[u].wait_recv()
        here = tot.at[n % 2, i]

        def one(q, carry):
            here[q] = plus(grad[u % 2, q, mine], twin_in[u % 2, q])
            return carry

        lax.fori_loop(0, dps, one, 0)
        credit(TWIN + u % 2, twin, u, 2)
        spend(CORNER + u % RING, u, RING)
        to_corner[u].start()

    def stage_c(u):
        n, i = divmod(u, tps)
        here = tot.at[n % 2, i]
        to_corner[u].wait_recv()
        if i % 2 == 0:
            here[p ^ 2] = plus(here[p ^ 2], corner_in[u % RING])
            credit(CORNER + u % RING, beside, u, RING)
        else:
            here[p ^ 1] = plus(here[p ^ 1], corner_in[u % RING])
            credit(CORNER + u % RING, above, u, RING)
        spend(ABOVE + u % RING, u, RING)
        to_y[u].start()
        spend(BESIDE + u % RING, u, RING)
        to_x[u].start()

    def stage_d(u):
        n, i = divmod(u, tps)
        here = tot.at[n % 2, i]
        to_x[u].wait_recv()
        to_y[u].wait_recv()
        own = here[p].astype(jnp.float32) + beside_in[u % RING].astype(jnp.float32) + above_in[u % RING].astype(jnp.float32)
        credit(BESIDE + u % RING, beside, u, RING)
        credit(ABOVE + u % RING, above, u, RING)
        if i < tps - 1:
            here[p] = own.astype(low)
            spend(CHAIN + i, u, tps)
            along[u].start()
            return
        for k in range(tps - 1):
            along[u - tps + 1 + k].wait_recv()
            own = own + chain_in[k].astype(jnp.float32)
            credit(CHAIN + k, (p, c, lax.rem(t + tps - 1 - k, tps)), u - tps + 1 + k, tps)
        if n:
            finish[n - 1].wait_send()
            keep[n - 1].wait()
        last[...] = own.astype(low)
        kept = last[...].astype(jnp.float32)
        squares[...] += jnp.sum((kept * kept).reshape(half // 8, 8, width), axis=0)
        finish[n].start()
        keep[n].start()

    reached = [0, 0, 0]

    def advance(done, extra=0):
        for which, (stage, lag) in enumerate(zip((stage_d, stage_b, stage_c), LAGS)):
            while reached[which] < min(units, done) and reached[which] + lag <= done + extra - 1:
                stage(reached[which])
                reached[which] += 1

    loads = {}

    def fetch(u):
        if u >= units or u in loads:
            return
        n, i = divmod(u, tps)
        level, kind = kinds[n]
        owner = lax.rem(t + 1 + i, tps)
        copies = [links.local(full_ref.at[MATS * level + kind, owner], wbuf.at[u % 2])]
        if kind == 2:
            copies.append(links.local(act_ref.at[level, owner], side.at[u % 2]))
        if kind == 0:
            copies.append(links.local(qkv_ref.at[level, owner], side.at[u % 2]))
            copies.append(links.local(mix_ref.at[level, owner], mix.at[i]))
        for copy in copies:
            copy.start()
        loads[u] = copies

    def bring(src, dst):
        copy = links.local(src, dst)
        copy.start()
        return copy

    def by_rows(body, size=64):
        def one(i, carry):
            body(pl.ds(pl.multiple_of(i * size, size), size))
            return carry

        lax.fori_loop(0, tokens // size, one, 0)

    def loop(count, body):
        def one(i, carry):
            body(i)
            return carry

        lax.fori_loop(0, count, one, 0)

    def column_sum(level, k, value):
        dmod_ref[level, k] += jnp.sum(value.reshape(value.shape[0] // 8, 8, width), axis=0)

    def lanes(i):
        return pl.ds(pl.multiple_of(i * LANES, LANES), LANES)

    def put(u, at, value):
        grad[u % 2, :, :, at] = value.astype(low).reshape(dps, rows, LANES)

    dmod_ref[...] = jnp.zeros_like(dmod_ref)
    squares[...] = jnp.zeros_like(squares)
    d_cut[...] = jnp.zeros_like(d_cut)
    top = layers - 1
    fetch(0)
    first = bring(cot_ref, arrived)
    branch_load, base_load = bring(brm_ref.at[top], branch), bring(mid_ref.at[top], base)
    first.wait()
    g[...] = arrived[...].astype(jnp.float32)
    tail, remotes = [], []

    def send_all(pairs):
        copies = [links.remote(lambda v=v: v)() for v in pairs]
        for copy in copies:
            copy.start()
        remotes.extend(copies)
        return copies

    flying = {}
    own_slot = 2 * t + c

    def landed(name):
        for copy in flying[name]:
            copy.wait_recv()

    def added(ref, count):
        total = ref[0]
        for k in range(1, count):
            total = total + ref[k]
        return total

    def cut_columns():
        mod_loads[0].start()
        for k in range(6 * layers):
            line = jnp.sum(dmod_ref[k // 6, k % 6], axis=0, keepdims=True)
            for j in range(tps):
                d_cut[j, k : k + 1, :] = line[:, j * wide : (j + 1) * wide]
        flying["cut"] = send_all([(d_cut.at[q[2]], d_in.at[own_slot], q) for q in chain + crossed + [twin]])
        d_in[own_slot] = d_cut[t]

    def share_clips():
        landed("cut")
        d_all[p] = added(d_in, 2 * tps)
        flying["clips"] = send_all([(d_all.at[p], d_all.at[p], q) for q in plane])

    def share_rows():
        landed("clips")
        share = jnp.zeros((8, rows), jnp.float32)
        for k in range(2 * layers):
            mod_loads[k].wait()
            for j in range(3):
                at = 3 * k + j
                lines = jnp.concatenate([d_all[q, at : at + 1, :] for q in range(dps)] + [jnp.zeros((8 - dps, wide), jnp.float32)], axis=0)
                coarse = lines.astype(low)
                fine = (lines - coarse.astype(jnp.float32)).astype(low)
                weight = mod_in[j].astype(low)
                share = share + dot_nt(coarse, weight) + dot_nt(fine, weight)
            if k + 1 < 2 * layers:
                mod_loads[k + 1].start()
        z_in[t] = share
        flying["shares"] = send_all([(z_in.at[t], z_in.at[t], q) for q in chain])

    def rows_home():
        landed("shares")
        d_cond[p] = added(z_in, tps)
        flying["homes"] = send_all([(d_cond.at[p], d_cond.at[p], q) for q in plane])
        conds = jnp.concatenate([cond_in[a, 0:1, :] for a in range(dps)], axis=0)
        gram = jnp.zeros((1, wide), jnp.float32)
        for b in range(dps):
            left = jnp.sum(conds * cond_in[b, 0:1, :], axis=1, keepdims=True)
            for a in range(dps):
                gram = gram + left[a : a + 1, 0:1] * jnp.sum(d_all[a] * d_all[b], axis=0, keepdims=True)
        squares[0:1, 0:wide] += 0.5 * gram

    def norm_of_all():
        line = jnp.sum(jnp.sum(squares[...], axis=0, keepdims=True), axis=1, keepdims=True)
        slot = 2 * p + c
        norm_in[slot] = jnp.broadcast_to(line, norm_ref.shape)
        flying["plane"] = send_all([(norm_in.at[slot], norm_in.at[slot], q) for q in plane + across + [twin]])
        landed("plane")
        norm_line[t] = added(norm_in, 2 * dps)
        flying["line"] = send_all([(norm_line.at[t], norm_line.at[t], q) for q in chain])
        landed("line")
        norm_ref[...] = added(norm_line, tps)
        landed("homes")

    mod_loads = [links.local(mod_w.at[k // 2, pl.ds(3 * (k % 2), 3)], mod_in) for k in range(2 * layers)]

    for level in reversed(range(layers)):
        factor = [mod_ref[level, k, 0:1, :] for k in range(6)]
        temporal = level % 2 == 1
        chunk = GROUP // (2 * frames)
        start = kinds.index((level, 2)) * tps
        x_load = bring(xm_ref.at[level], x)
        branch_load.wait()

        def open_m(span, gate=factor[5], level=level):
            value = g[span, :]
            column_sum(level, 5, value * branch[span, :])
            lhs[span, :] = (gate * value).astype(low)

        by_rows(open_m)
        branch_load = bring(bra_ref.at[level], branch)
        for i in range(tps):
            u = start + i
            if i == 0:
                pre_load = bring(pre_ref.at[level, lax.rem(t + 1, tps)], pre)
            release(u)
            for copy in loads[u]:
                copy.wait()
            fetch(u + 1)
            w, act = wbuf.at[u % 2], side.at[u % 2]
            pre_load.wait()

            def third(k, u=u, i=i, w=w, act=act):
                at = lanes(k)
                put(u, at, dot_tn(lhs[...], act[:, at]))
                d_act = dot_nn(lhs[...], w[:, at])
                dpre[i, :, at] = (d_act * gelu_slope(pre[:, at])).astype(low)

            loop(width // LANES, third)
            if i + 1 < tps:
                pre_load = bring(pre_ref.at[level, lax.rem(t + 2 + i, tps)], pre)
            stage_a(u)
            advance(u + 1)
        dacc[...] = jnp.zeros_like(dacc)
        x_load.wait()
        for i in range(tps):
            u = start + tps + i
            release(u)
            for copy in loads[u]:
                copy.wait()
            fetch(u + 1)
            w = wbuf.at[u % 2]

            def second(k, u=u, i=i, w=w):
                at = lanes(k)
                put(u, at, dot_tn(x[...], dpre[i, :, at]))
                dacc[:, at] += dot_nt(dpre[i], w[at, :])

            loop(width // LANES, second)
            stage_a(u)
            advance(u + 1)
        x_load = bring(xa_ref.at[level], x)
        base_load.wait()
        branch_load.wait()

        def turn_back(span, source, s_at, r_at, r):
            normed, rstd = normalize(source[span, :])
            d = dacc[span, :]
            column_sum(level, s_at, d)
            column_sum(level, r_at, d * normed)
            return g[span, :] + normalize_back(d * (1.0 + r), normed, rstd)

        def close_m(span, r=factor[4], gate=factor[2], level=level):
            value = turn_back(span, base, 3, 4, r)
            g[span, :] = value
            column_sum(level, 2, value * branch[span, :])
            lhs[span, :] = (gate * value).astype(low)

        by_rows(close_m)
        base_load = bring(hid_ref.at[level], base)
        if level:
            branch_load = bring(brm_ref.at[level - 1], branch)
        dacc[...] = jnp.zeros_like(dacc)
        x_load.wait()

        def weigh(i, start=start):
            u = start + 2 * tps + i
            release(u)

            def first(k):
                at = lanes(k)
                put(u, at, dot_tn(x[...], dpre[i, :, at]))

            loop(width // LANES - 1, first)
            at = slice(width - LANES, width)
            put(u, at, dot_tn(x[...], dpre[i, :, at]) + dot_tn(lhs[...], mix[i]))
            stage_a(u)

        for i in range(tps):
            u = start + 2 * tps + i
            for copy in loads[u]:
                copy.wait()
            fetch(u + 1)
            w, qkv_j, dproj = wbuf.at[u % 2], side.at[u % 2], dpre.at[i]

            def attention(k, w=w, qkv_j=qkv_j, dproj=dproj, temporal=temporal, chunk=chunk):
                span = pl.ds(pl.multiple_of(k * GROUP, GROUP), GROUP)
                scale = HD ** (-0.5)
                low_v = LANES - wide
                d_mix = dot_nn(lhs[span, :], w[:, 768 : 768 + LANES]).astype(low)
                d_mix4 = head_stack(d_mix, low_v, heads)
                query4 = head_stack(qkv_j[span, 0:LANES], 0, heads)
                key, value = qkv_j[span, LANES : 2 * LANES], qkv_j[span, 2 * LANES : 3 * LANES]
                probs = softmax_rows(dot_nt(query4, key) * scale, chunk if temporal else 0)
                d_probs = dot_nt(d_mix4, value)
                d_scores = (probs * (d_probs - jnp.sum(probs * d_probs, axis=-1, keepdims=True))).astype(low)
                d_value = pltpu.roll(dot_tn(probs.astype(low), d_mix4), LANES - 32, 1)
                d_query = head_merge(dot_nn(d_scores, key), 0, heads) * scale
                d_key = pltpu.roll(dot_tn(d_scores, query4), 32, 1) * scale
                dproj[span, 0:256] = d_query[:, 0:256].astype(low)
                dproj[span, 256:384] = (d_query[:, 256:384] + d_key[:, 0:128]).astype(low)
                dproj[span, 384:512] = d_key[:, 128:256].astype(low)
                dproj[span, 512:640] = (d_key[:, 256:384] + d_value[:, 0:128]).astype(low)
                dproj[span, 640:896] = d_value[:, 128:384].astype(low)
                dproj[span, 896:1152] = jnp.zeros((GROUP, 256), low)

            loop(tokens // GROUP, attention)
            for k in range(width // LANES):
                at = slice(k * LANES, (k + 1) * LANES)
                dacc[:, at] += dot_nt(dproj[:, 0:896], w[at, 0:896])
            if level:
                advance(start + 2 * tps, i + 1)
            else:
                weigh(i)
                advance(u + 1)
        base_load.wait()
        outgoing = side.at[1]

        def close_a(span, r=factor[1], level=level):
            value = turn_back(span, base, 0, 1, r)
            g[span, :] = value
            outgoing[span, :] = value.astype(low)

        by_rows(close_a)
        strip = home_ref.shape[1]
        part, flock = strip // 2, frames // tps
        patches = strip * tps
        if level:
            base_load = bring(mid_ref.at[level - 1], base)
            away, stay = [], []
            for k in range(part // chunk):
                for f in range(flock):
                    to = pl.ds(pl.multiple_of(f * patches + t * strip + c * part + k * chunk, 16), chunk)
                    for peer in [None, twin] + chain + crossed:
                        _, pc, pt = peer or (p, c, t)
                        row = (k * 2 * frames + (pt * 2 + pc) * flock + f) * chunk
                        piece = outgoing.at[pl.ds(pl.multiple_of(row, 16), chunk)]
                        if peer is None:
                            stay.append(links.local(piece, arrived.at[to]))
                        else:
                            away.append(links.remote(lambda s=piece, d=arrived.at[to], q=peer: (s, d, q))())
            moves, steps = away + stay, []
        else:
            for f in range(flock):
                for peer in [None] + chain:
                    pt = t if peer is None else peer[2]
                    piece = outgoing.at[pl.ds(pl.multiple_of(f * patches + pt * strip, 16), strip)]
                    goal = home_ref.at[t * flock + f]
                    if peer is None:
                        tail.append(links.local(piece, goal))
                    else:
                        tail.append(links.remote(lambda s=piece, d=goal, q=peer: (s, d, q))())
            moves, steps = tail, [cut_columns, share_clips, share_rows, rows_home]
        for copy in moves:
            copy.start()
        if level:
            for i in range(tps):
                weigh(i)
                advance(start + 2 * tps + i + 1)
        else:
            for more, step in enumerate(steps):
                step()
                advance(units, more + 1)
        if level:
            for copy in moves:
                copy.wait()
            g[...] = arrived[...].astype(jnp.float32)
    for more in range(1, 1 + LAGS[0]):
        advance(units, more)
    norm_of_all()
    for copy in remotes:
        copy.wait_send()
    for u in range(units):
        if u >= units - 2:
            to_twin[u].wait_send()
        if u >= units - 2 * tps:
            to_corner[u].wait_send()
            to_x[u].wait_send()
            to_y[u].wait_send()
            if u in along:
                along[u].wait_send()
    for n in range(mats):
        finish[n].wait_recv()
    finish[mats - 1].wait_send()
    keep[mats - 1].wait()
    for copy in tail:
        copy.wait()


def backward_pass(full, cot_rows, modulation, cond_rows, mod_w, saved, mesh_shape, frames, strip):
    tps, dps = mesh_shape["tp"], mesh_shape["dp"]
    mats, _, depth, width = full.shape
    layers, tokens = saved[0].shape[:2]
    rows = depth // dps
    half = rows // 2
    wide = mod_w.shape[-1]
    heads = wide // HD
    low, wider = jnp.bfloat16, jnp.float32
    sds = jax.ShapeDtypeStruct
    whole = pl.BlockSpec(memory_space=pl.ANY)
    near = pl.BlockSpec(memory_space=pltpu.VMEM)
    return pl.pallas_call(
        partial(backward_kernel, tps, (layers, frames, heads * HD, heads)),
        out_shape=[
            sds((mats, rows, width), low),
            sds((frames, strip, width), low),
            sds((dps, 16, wide), wider),
            sds((dps, 8, rows), wider),
            sds((8, 128), wider),
        ],
        in_specs=[whole, whole, near, near] + [whole] * 11,
        out_specs=[whole, whole, near, near, near],
        scratch_shapes=[
            pltpu.VMEM((2, tps, dps, half, width), low),
            pltpu.VMEM((2, dps, rows, width), low),
            pltpu.VMEM((2, dps, half, width), low),
            pltpu.VMEM((RING, half, width), low),
            pltpu.VMEM((RING, half, width), low),
            pltpu.VMEM((RING, half, width), low),
            pltpu.VMEM((tps - 1, half, width), low),
            pltpu.VMEM((half, width), low),
            pltpu.VMEM((tokens, width), wider),
            pltpu.VMEM((tokens, width), wider),
            pltpu.VMEM((tokens, width), low),
            pltpu.VMEM((tokens, width), low),
            pltpu.VMEM((2, depth, width), low),
            pltpu.VMEM((2, tokens, width), low),
            pltpu.VMEM((tokens, width), wider),
            pltpu.VMEM((tps, tokens, width), low),
            pltpu.VMEM((tps, tokens, LANES), low),
            pltpu.VMEM((tokens, width), wider),
            pltpu.VMEM((tokens, width), wider),
            pltpu.VMEM((tokens, width), low),
            pltpu.VMEM((layers, 6, 8, width), wider),
            pltpu.VMEM((tps, 16, wide), wider),
            pltpu.VMEM((2 * tps, 16, wide), wider),
            pltpu.VMEM((3, rows, wide), wider),
            pltpu.VMEM((tps, 8, rows), wider),
            pltpu.VMEM((8, width), wider),
            pltpu.VMEM((2 * dps, 8, 128), wider),
            pltpu.VMEM((tps, 8, 128), wider),
            pltpu.SemaphoreType.DMA((200,)),
            pltpu.SemaphoreType.DMA((200,)),
            pltpu.SemaphoreType.DMA((110,)),
            pltpu.SemaphoreType.REGULAR((2 + tps + 3 * RING,)),
        ],
        compiler_params=pltpu.CompilerParams(
            collective_id=1, has_side_effects=True, vmem_limit_bytes=VMEM_LIMIT
        ),
        name="backward_pass",
    )(full, cot_rows.reshape(tokens, width), modulation, cond_rows, mod_w, *saved)


def sum_grads(grads):
    parts = []
    for grad in grads:
        part = lax.psum_scatter(grad, "tp", scatter_dimension=0, tiled=True)[0]
        part = lax.psum_scatter(part, "dp", scatter_dimension=0, tiled=True)
        parts.append(lax.psum(part, "ctx"))
    return jnp.stack(parts)


def update_kernel(wide, red_ref, norm_ref, cond_ref, lines_ref, *refs):
    masters, firsts, seconds = refs[0:5], refs[5:10], refs[10:15]
    news, copies, moments, squares = refs[15:20], refs[20:25], refs[25:30], refs[30:35]
    level, part = pl.program_id(0), pl.program_id(1)
    coef = CLIP_MAX / jnp.maximum(jnp.sqrt(norm_ref[0:1, 0:1]), CLIP_MAX)

    def step(kind, at, grad):
        new, copy, moment, square = adam_update(masters[kind][at], firsts[kind][at], seconds[kind][at], grad, coef)
        news[kind][at] = new
        copies[kind][at] = copy
        moments[kind][at] = moment
        squares[kind][at] = square

    rows = masters[0].shape[2]
    span = pl.ds(pl.multiple_of(part * rows, 32), rows)
    first = red_ref[0, span, :].astype(jnp.float32)
    for k in range(3):
        step(0, (0, k), first[:, k * wide : (k + 1) * wide])
    step(2, 0, red_ref[1, span, :].astype(jnp.float32))
    step(3, 0, red_ref[2, span, :].astype(jnp.float32))

    @pl.when(part == 0)
    def _():
        step(1, 0, red_ref[0, :, 3 * wide :].astype(jnp.float32).T)

    for k in range(2):
        lines = lines_ref[level * 6 + part * 2 + k]
        grad = cond_ref[:, 0:1] * lines[0:1, :]
        for q in range(1, lines_ref.shape[1]):
            grad = grad + cond_ref[:, q : q + 1] * lines[q : q + 1, :]
        step(4, (0, k), grad)


def update_all(reduced, norm, cond_columns, lines, masters, firsts, seconds):
    layers, _, rows, wide = masters[0].shape
    width = reduced.shape[-1]
    parts = 3
    blocks = (
        pl.BlockSpec((1, 3, rows // parts, wide), lambda l, q: (l, 0, q, 0)),
        pl.BlockSpec((1, wide, rows), lambda l, q: (l, 0, 0)),
        pl.BlockSpec((1, rows // parts, width), lambda l, q: (l, q, 0)),
        pl.BlockSpec((1, rows // parts, width), lambda l, q: (l, q, 0)),
        pl.BlockSpec((1, 6 // parts, rows, wide), lambda l, q: (l, q, 0, 0)),
    )
    small = [pl.BlockSpec(a.shape, lambda l, q, n=a.ndim: (0,) * n) for a in (norm, cond_columns, lines)]
    shapes = [[jax.ShapeDtypeStruct(w.shape, kind) for w in masters] for kind in (jnp.float32, jnp.bfloat16, jnp.float32, jnp.float32)]
    return pl.pallas_call(
        partial(update_kernel, wide),
        grid=(layers, parts),
        out_shape=sum(shapes, []),
        in_specs=[pl.BlockSpec((MATS, rows, width), lambda l, q: (l, 0, 0))] + small + list(blocks) * 3,
        out_specs=list(blocks) * 4,
        compiler_params=pltpu.CompilerParams(vmem_limit_bytes=VMEM_LIMIT),
        name="update_all",
    )(reduced, norm, cond_columns, lines, *masters, *firsts, *seconds)


def pack(qkv, out, up, down):
    rows = qkv.shape[0]
    low = jnp.bfloat16
    first = jnp.concatenate([qkv.astype(low).reshape(rows, -1), out.astype(low).T], axis=1)
    return jnp.stack([first, up.astype(low), down.astype(low).T])


def unpack(first, second, third, like):
    rows, _, wide = like.shape
    cut = 3 * wide
    return (first[:, :cut].reshape(rows, 3, wide), first[:, cut:].T, second, third.T)


def frames_whole(rows):
    return lax.all_to_all(rows, "tp", 0, 1, tiled=True)


def frames_back(rows):
    return lax.all_to_all(rows, "tp", 1, 0, tiled=True)


def patches_whole(rows):
    return lax.all_to_all(rows, ("tp", "ctx"), 1, 0, tiled=True)


def patches_back(rows):
    return lax.all_to_all(rows, ("tp", "ctx"), 0, 1, tiled=True)


def columns_home(rows, mesh_shape):
    frames, patches, width = rows.shape
    tps, cs = mesh_shape["tp"], mesh_shape["ctx"]
    split = rows.reshape(tps, cs, frames // (tps * cs), patches, width)
    split = split.transpose(1, 0, 2, 3, 4).reshape(cs, frames // cs, patches, width)
    return lax.all_to_all(split, "ctx", 0, 2, tiled=True)[0]


def columns_away(rows, mesh_shape):
    tps, cs = mesh_shape["tp"], mesh_shape["ctx"]
    frames, patches, width = rows.shape
    split = lax.all_to_all(rows[None], "ctx", 2, 0, tiled=True)
    split = split.reshape(cs, tps, frames // tps, patches // cs, width).transpose(1, 0, 2, 3, 4)
    return split.reshape(frames * cs, patches // cs, width)


def per_device_plain(mesh_shape, inputs, conditioning, *states):
    masters, firsts, seconds, cotangent = states[:5], states[5:10], states[10:15], states[15]
    qkv_weight, out_weight, up_weight, down_weight, mod_weight = masters
    low = jnp.bfloat16
    highest = lax.Precision.HIGHEST
    layers = qkv_weight.shape[0]
    scale = HD ** (-0.5)
    dp_at, _, tp_at = place()
    tps, dps = mesh_shape["tp"], mesh_shape["dp"]
    rows = qkv_weight.shape[1]
    wide = qkv_weight.shape[3]
    heads = wide // HD
    width = inputs.shape[-1]

    shards = jnp.concatenate(
        [pack(qkv_weight[l], out_weight[l], up_weight[l], down_weight[l]) for l in range(layers)]
    )
    full = gather_weights(shards)

    cond_low = jax.nn.silu(conditioning).astype(low)
    cond_all = lax.all_gather(cond_low, "dp", axis=0, tiled=True)
    cond_mine = lax.dynamic_slice_in_dim(cond_all, dp_at * rows, rows, 1)
    mod_low = mod_weight.astype(low)
    mod_part = jnp.einsum("cd,ldke->clke", cond_mine, mod_low, preferred_element_type=jnp.float32)
    mod_part = lax.psum_scatter(mod_part, "dp", scatter_dimension=0, tiled=True)
    modulation = lax.all_gather(mod_part, "tp", axis=3, tiled=True)[0]

    hidden = frames_whole(inputs[0]).astype(jnp.float32)
    saved = []
    for level in range(layers):
        if level:
            if level % 2 == 1:
                hidden = patches_whole(hidden.astype(low)).astype(jnp.float32)
            else:
                hidden = patches_back(hidden.astype(low)).astype(jnp.float32)
        forms = SPATIAL_FORMS if level % 2 == 0 else TEMPORAL_FORMS
        first_w, up_w, down_w = full[MATS * level], full[MATS * level + 1], full[MATS * level + 2]
        factors = modulation[level]
        frames, patches = hidden.shape[:2]
        normed_a, rstd_a = normalize(hidden)
        attn_in = (normed_a * (1.0 + factors[1]) + factors[0]).astype(low)
        projected = jnp.einsum(
            "fpd,jde->fpje", attn_in, first_w[:, :, : 3 * wide], preferred_element_type=jnp.float32
        ).astype(low)
        projected = projected.reshape(frames, patches, tps, 3, heads, HD)
        query, key, value = (projected[:, :, :, s] for s in range(3))
        mixed, log_total = attend(query, key, value, forms, scale)
        mixed = mixed.reshape(frames, patches, tps, wide)
        branch_a = jnp.einsum(
            "fpje,jde->fpd", mixed, first_w[:, :, 3 * wide :], preferred_element_type=jnp.float32
        )
        middle = hidden + factors[2] * branch_a
        normed_m, rstd_m = normalize(middle)
        mlp_in = (normed_m * (1.0 + factors[4]) + factors[3]).astype(low)
        hidden_pre = jnp.einsum("fpd,jdh->fpjh", mlp_in, up_w, preferred_element_type=jnp.float32)
        hidden_act = jax.nn.gelu(hidden_pre, approximate=True).astype(low)
        branch_m = jnp.einsum("fpjh,jdh->fpd", hidden_act, down_w, preferred_element_type=jnp.float32)
        saved.append(
            (forms, first_w, up_w, down_w, factors, normed_a, rstd_a, attn_in, query, key, value,
             mixed, log_total, branch_a, normed_m, rstd_m, mlp_in, hidden_pre, hidden_act, branch_m)
        )
        hidden = middle + factors[5] * branch_m
    temporal_end = layers % 2 == 0
    output = hidden.astype(low)
    output = columns_home(output, mesh_shape) if temporal_end else frames_back(output)
    upstream = columns_away(cotangent[0], mesh_shape) if temporal_end else frames_whole(cotangent[0])
    upstream = upstream.astype(jnp.float32)

    grads = [None] * (MATS * layers)
    d_mods = [None] * layers
    for level in reversed(range(layers)):
        (forms, first_w, up_w, down_w, factors, normed_a, rstd_a, attn_in, query, key, value,
         mixed, log_total, branch_a, normed_m, rstd_m, mlp_in, hidden_pre, hidden_act, branch_m) = saved[level]
        frames, patches = upstream.shape[:2]
        d_gate_m = jnp.sum(upstream * branch_m, axis=(0, 1))
        d_branch_m = (factors[5] * upstream).astype(low)
        grads[MATS * level + 2] = jnp.einsum(
            "fpd,fpjh->jdh", d_branch_m, hidden_act, preferred_element_type=jnp.float32
        ).astype(low)
        d_act = jnp.einsum("fpd,jdh->fpjh", d_branch_m, down_w, preferred_element_type=jnp.float32)
        slope_pull = jax.vjp(partial(jax.nn.gelu, approximate=True), hidden_pre)[1]
        d_pre = slope_pull(d_act)[0].astype(low)
        grads[MATS * level + 1] = jnp.einsum(
            "fpd,fpjh->jdh", mlp_in, d_pre, preferred_element_type=jnp.float32
        ).astype(low)
        d_mlp_in = jnp.einsum("fpjh,jdh->fpd", d_pre, up_w, preferred_element_type=jnp.float32)
        d_shift_m = jnp.sum(d_mlp_in, axis=(0, 1))
        d_scale_m = jnp.sum(d_mlp_in * normed_m, axis=(0, 1))
        upstream = upstream + normalize_back(d_mlp_in * (1.0 + factors[4]), normed_m, rstd_m)
        d_gate_a = jnp.sum(upstream * branch_a, axis=(0, 1))
        d_branch_a = (factors[2] * upstream).astype(low)
        grad_out = jnp.einsum("fpd,fpje->jde", d_branch_a, mixed, preferred_element_type=jnp.float32)
        d_mixed = jnp.einsum(
            "fpd,jde->fpje", d_branch_a, first_w[:, :, 3 * wide :], preferred_element_type=jnp.float32
        ).astype(low)
        d_mixed = d_mixed.reshape(frames, patches, tps, heads, HD)
        d_parts = attend_back(query, key, value, d_mixed, log_total, forms, scale)
        d_projected = jnp.stack(d_parts, axis=3).astype(low).reshape(frames, patches, tps, 3 * wide)
        grad_qkv = jnp.einsum("fpd,fpje->jde", attn_in, d_projected, preferred_element_type=jnp.float32)
        grads[MATS * level] = jnp.concatenate([grad_qkv, grad_out], axis=2).astype(low)
        d_attn_in = jnp.einsum(
            "fpje,jde->fpd", d_projected, first_w[:, :, : 3 * wide], preferred_element_type=jnp.float32
        )
        d_shift_a = jnp.sum(d_attn_in, axis=(0, 1))
        d_scale_a = jnp.sum(d_attn_in * normed_a, axis=(0, 1))
        upstream = upstream + normalize_back(d_attn_in * (1.0 + factors[1]), normed_a, rstd_a)
        d_mods[level] = jnp.stack([d_shift_a, d_scale_a, d_gate_a, d_shift_m, d_scale_m, d_gate_m])
        if level:
            if level % 2 == 1:
                upstream = patches_back(upstream.astype(low)).astype(jnp.float32)
            else:
                upstream = patches_whole(upstream.astype(low)).astype(jnp.float32)
    input_grad = frames_back(upstream.astype(low)).astype(jnp.float32)

    reduced = sum_grads([grads[m] for m in reversed(range(MATS * layers))])
    reduced = reduced.astype(jnp.float32)

    d_mod = lax.psum(jnp.stack(d_mods)[None], ("ctx", "tp"))
    d_mod_all = lax.all_gather(d_mod, "dp", axis=0, tiled=True)
    d_mod_mine = lax.dynamic_slice_in_dim(d_mod_all, tp_at * wide, wide, 3)
    grad_mod = jnp.einsum("cd,clke->ldke", cond_mine.astype(jnp.float32), d_mod_mine, precision=highest)
    cond_part = jnp.einsum("clke,ldke->cd", d_mod_mine, mod_low.astype(jnp.float32), precision=highest)
    cond_part = lax.all_gather(lax.psum(cond_part, "tp"), "dp", axis=1, tiled=True)
    cond_total = lax.dynamic_slice_in_dim(cond_part, dp_at * conditioning.shape[0], conditioning.shape[0], 0)
    cond_grad = jax.vjp(jax.nn.silu, conditioning)[1](cond_total)[0]

    order = list(reversed(range(MATS * layers)))
    per_level = [
        unpack(*[reduced[order.index(MATS * level + kind)] for kind in range(MATS)], qkv_weight[level])
        for level in range(layers)
    ]
    stacked = [jnp.stack([per_level[level][kind] for level in range(layers)]) for kind in range(4)]
    stacked.append(grad_mod)
    squares = jnp.zeros((), jnp.float32)
    for grad in stacked:
        squares = squares + jnp.sum(grad * grad)
    grad_norm = jnp.sqrt(lax.psum(squares, ("dp", "tp")))
    coef = CLIP_MAX / jnp.maximum(grad_norm, CLIP_MAX)
    updates = [
        adam_update(masters[kind], firsts[kind], seconds[kind], stacked[kind], coef) for kind in range(5)
    ]
    return (output[None], input_grad[None], cond_grad, grad_norm) + tuple(
        updates[kind][part] for part in range(4) for kind in range(5)
    )


def in_memory(array, kind):
    return array.transpose(((0, 2, 1, 3), (0, 1, 2), (0, 1, 2), (0, 2, 1), (0, 2, 1, 3))[kind])


def per_device(mesh_shape, inputs, conditioning, *states):
    if not by_hand(mesh_shape, inputs, states[0]):
        return per_device_plain(mesh_shape, inputs, conditioning, *states)
    states, cotangent = states[:15], states[15]
    states = [in_memory(s, i % 5) for i, s in enumerate(states)]
    masters, firsts, seconds = states[:5], states[5:10], states[10:15]
    dp_at, _, _ = place()
    dps = mesh_shape["dp"]
    frames, strip, width = inputs.shape[1:]
    layers, _, rows, wide = masters[0].shape

    cond_low = jax.nn.silu(conditioning).astype(jnp.bfloat16).astype(jnp.float32)
    cond = jnp.broadcast_to(cond_low.reshape(dps, 1, rows), (dps, 8, rows))
    full, output, cot_rows, *saved, modulation, cond_rows = forward_pass(masters, cond, inputs[0], cotangent[0], mesh_shape)
    reduced, home, d_all, d_cond, norm = backward_pass(
        full, cot_rows, modulation, cond_rows, masters[4], saved, mesh_shape, frames, strip
    )
    updates = update_all(
        reduced, norm, cond_rows[:, 0, :].T, d_all[:, : 6 * layers].transpose(1, 0, 2), masters, firsts, seconds
    )
    updates = [in_memory(u, i % 5) for i, u in enumerate(updates)]
    d_cond = lax.dynamic_slice_in_dim(d_cond, dp_at, 1, 1).reshape(1, dps * rows)
    cond_grad = jax.vjp(jax.nn.silu, conditioning)[1](d_cond)[0]
    input_grad = home.astype(jnp.float32)
    output = output.reshape(1, frames, strip, width)
    return (output, input_grad[None], cond_grad, jnp.sqrt(norm[0, 0])) + tuple(updates)


def solution(mesh):
    weights = (
        P(None, "dp", None, "tp"),
        P(None, "tp", "dp"),
        P(None, "dp", "tp"),
        P(None, "tp", "dp"),
        P(None, "dp", None, "tp"),
    )
    rows = P("dp", "ctx", "tp", None)
    return jax.shard_map(
        partial(per_device, dict(mesh.shape)),
        mesh=mesh,
        in_specs=(rows, P("dp", None)) + weights * 3 + (rows,),
        out_specs=(rows, rows, P("dp", None), P()) + weights * 4,
        check_vma=False,
    )
```

```python
from functools import partial

import jax
import jax.numpy as jnp
from jax import lax
from jax.experimental import pallas as pl
from jax.experimental.pallas import tpu as pltpu
from jax.sharding import PartitionSpec as P

HD = 72
STEP = 5
EPS_NORM = 1e-06
LEARN_RATE = 0.03
DECAY_RATE = 0.1
BETA_ONE = 0.5
BETA_TWO = 0.5
ADAM_EPS = 1e-08
CLIP_MAX = 1.0
MESH = pl.DeviceIdType.MESH
MATS = 3
VMEM_LIMIT = 62 * 1024 * 1024
LANES = 384
SLOTS = 2
GROUP = 256
LAGS = (5, 1, 3)
RING = 4
SPATIAL_FORMS = ("fqjhe,fkjhe->fjhqk", "fjhqk,fkjhe->fqjhe", "fjhqk,fqjhe->fkjhe")
TEMPORAL_FORMS = ("qpjhe,kpjhe->pjhqk", "pjhqk,kpjhe->qpjhe", "pjhqk,qpjhe->kpjhe")


def normalize(rows):
    centred = rows - jnp.mean(rows, axis=-1, keepdims=True)
    rstd = lax.rsqrt(jnp.mean(centred * centred, axis=-1, keepdims=True) + EPS_NORM)
    return (centred * rstd, rstd)


def normalize_back(grad, normed, rstd):
    return rstd * (
        grad
        - jnp.mean(grad, axis=-1, keepdims=True)
        - normed * jnp.mean(grad * normed, axis=-1, keepdims=True)
    )


def attend(query, key, value, forms, scale):
    scores = jnp.einsum(forms[0], query, key, preferred_element_type=jnp.float32) * scale
    top = jnp.max(scores, axis=-1, keepdims=True)
    expo = jnp.exp(scores - top)
    total = jnp.sum(expo, axis=-1, keepdims=True)
    probs = (expo / total).astype(jnp.bfloat16)
    mixed = jnp.einsum(forms[1], probs, value, preferred_element_type=jnp.float32)
    return (mixed.astype(jnp.bfloat16), top + jnp.log(total))


def attend_back(query, key, value, d_mixed, log_total, forms, scale):
    scores = jnp.einsum(forms[0], query, key, preferred_element_type=jnp.float32) * scale
    probs = jnp.exp(scores - log_total)
    d_probs = jnp.einsum(forms[0], d_mixed, value, preferred_element_type=jnp.float32)
    d_scores = (probs * (d_probs - jnp.sum(probs * d_probs, axis=-1, keepdims=True))).astype(
        jnp.bfloat16
    )
    d_value = jnp.einsum(
        forms[2], probs.astype(jnp.bfloat16), d_mixed, preferred_element_type=jnp.float32
    )
    d_query = jnp.einsum(forms[1], d_scores, key, preferred_element_type=jnp.float32) * scale
    d_key = jnp.einsum(forms[2], d_scores, query, preferred_element_type=jnp.float32) * scale
    return (d_query, d_key, d_value)


def adam_update(master, first, second, grad, coef):
    clipped = coef * grad
    first_new = BETA_ONE * first + (1.0 - BETA_ONE) * clipped
    second_new = BETA_TWO * second + (1.0 - BETA_TWO) * clipped * clipped
    first_hat = first_new / (1.0 - BETA_ONE**STEP)
    second_hat = second_new / (1.0 - BETA_TWO**STEP)
    master_new = master - LEARN_RATE * (
        first_hat / (jnp.sqrt(second_hat) + ADAM_EPS) + DECAY_RATE * master
    )
    return (master_new, master_new.astype(jnp.bfloat16), first_new, second_new)


def place():
    return lax.axis_index("dp"), lax.axis_index("ctx"), lax.axis_index("tp")


def greet(peers):
    barrier = pltpu.get_barrier_semaphore()
    for peer in peers:
        pl.semaphore_signal(barrier, inc=1, device_id=peer, device_id_type=MESH)
    pl.semaphore_wait(barrier, len(peers))


def by_hand(mesh_shape, inputs, qkv_weight):
    tps, cs = mesh_shape["tp"], mesh_shape["ctx"]
    layers, rows, _, wide = qkv_weight.shape
    clips, frames, strip, width = inputs.shape
    return (
        mesh_shape["dp"] == 4 and cs == 2 and tps == 4 and clips == 1 and layers == 2 and rows % 32 == 0
        and wide == 4 * HD and 4 * wide == width and width % LANES == 0 and frames == 2 * tps
        and strip * tps == GROUP and frames * cs == 16 and strip == 64
    )


def gather_weights(shards):
    full = lax.all_gather(shards, "dp", axis=1, tiled=True)
    return lax.all_gather(full, "tp", axis=1, tiled=False)


class Links:
    def __init__(self, send_sem, recv_sem, local_sem):
        self.send_sem, self.recv_sem, self.local_sem = send_sem, recv_sem, local_sem
        self.used, self.used_local = 0, 0

    def remote(self, make):
        at = self.used
        self.used += 1

        def build(*args):
            src, dst, peer = make(*args)
            return pltpu.make_async_remote_copy(
                src_ref=src, dst_ref=dst, send_sem=self.send_sem.at[at], recv_sem=self.recv_sem.at[at],
                device_id=peer, device_id_type=MESH,
            )

        return build

    def local(self, src, dst):
        at = self.used_local
        self.used_local += 1
        return pltpu.make_async_copy(src, dst, self.local_sem.at[at])


def lane_mask(shape, low, high):
    lane = lax.broadcasted_iota(jnp.int32, shape, 1)
    return jnp.logical_and(lane >= low, lane < high)


def dot_nn(a, b):
    return lax.dot_general(a, b, (((1,), (0,)), ((), ())), preferred_element_type=jnp.float32)


def dot_nt(a, b):
    return lax.dot_general(a, b, (((1,), (1,)), ((), ())), preferred_element_type=jnp.float32)


def dot_tn(a, b):
    return lax.dot_general(a, b, (((0,), (0,)), ((), ())), preferred_element_type=jnp.float32)


def softmax_rows(scores, columns):
    if columns:
        rows = lax.broadcasted_iota(jnp.int32, scores.shape, 0)
        cols = lax.broadcasted_iota(jnp.int32, scores.shape, 1)
        scores = jnp.where((rows & (columns - 1)) == (cols & (columns - 1)), scores, -1e30)
    top = jnp.max(scores, axis=-1, keepdims=True)
    expo = jnp.exp(scores - top)
    return expo * (1.0 / jnp.sum(expo, axis=-1, keepdims=True))


def head_stack(rows, first, heads):
    return jnp.concatenate(
        [jnp.where(lane_mask(rows.shape, first + h * HD, first + (h + 1) * HD), rows, jnp.zeros_like(rows)) for h in range(heads)],
        axis=0,
    )


def head_merge(stacked, first, heads):
    size = stacked.shape[0] // heads
    total = jnp.zeros((size, stacked.shape[1]), stacked.dtype)
    for h in range(heads):
        part = stacked[h * size : (h + 1) * size]
        total = jnp.where(lane_mask(part.shape, first + h * HD, first + (h + 1) * HD), part, total)
    return total


def forward_kernel(tps, geometry, *refs):
    layers, frames, wide, heads = geometry
    (qkv_w, out_w, up_w, down_w, mod_w, cond_ref, rows_ref, cot_ref,
     full_ref, out_ref, cot_out, hid_out, mid_out, bra_out, brm_out, xa_out, xm_out, qkv_out, mix_out, pre_out, act_out, mod_ref, cond_in,
     hid, mid, acc_a, acc_m, x_a, x_m, wbuf, act, pre, qkv, mix, rows_in, moved, turned,
     packed, wide_in, out_in, up_in, down_in, mod_in, part, part_in, columns,
     send_sem, recv_sem, local_sem) = refs
    p, c, t = place()
    mats, rows, width = packed.shape
    tokens = hid.shape[1]
    half = rows // 2
    own_half = pl.multiple_of(c * half, 16)
    beside, above, twin = (p ^ 1, c, t), (p ^ 2, c, t), (p, 1 - c, t)
    chain = [(p, c, lax.rem(t + k, tps)) for k in range(1, tps)]
    crossed = [(p, 1 - c, lax.rem(t + k, tps)) for k in range(1, tps)]
    plane = [(p ^ k, c, t) for k in range(1, 4)]
    links = Links(send_sem, recv_sem, local_sem)
    low = jnp.bfloat16

    arrivals = {}
    for level in range(layers):
        arrivals[level] = (
            links.local(qkv_w.at[level], wide_in.at[level]), links.local(out_w.at[level], out_in.at[level]),
            links.local(up_w.at[level], up_in.at[level]), links.local(down_w.at[level], down_in.at[level]),
        )
        for copy in arrivals[level]:
            copy.start()
    mod_loads = [links.local(mod_w.at[k // 2, pl.ds(3 * (k % 2), 3)], mod_in.at[k % 2]) for k in range(2 * layers)]
    mod_loads[0].start()
    mod_loads[1].start()
    greet(chain + crossed + plane + [twin])
    cond_copies = [links.remote(lambda q=q: (cond_ref.at[q[0]], cond_in.at[p], q))() for q in plane]
    cond_own = links.local(cond_ref.at[p], cond_in.at[p])
    for copy in cond_copies + [cond_own]:
        copy.start()

    def rows_of(owner):
        return pl.ds(pl.multiple_of(owner * rows + own_half, 16), half)

    def block(m, k, owner):
        return full_ref.at[m, lax.rem(t + tps - k, tps), rows_of(owner)]

    def column(m, owner):
        return full_ref.at[m, :, rows_of(owner)]

    def own(m):
        return packed.at[m, pl.ds(own_half, half)]

    keep, along, to_x, to_y, corner, to_twin = {}, {}, {}, {}, {}, {}
    for m in range(mats):
        keep[m] = links.local(own(m), block(m, 0, p))
        for k in range(tps):
            if k:
                along[m, k] = links.remote(lambda m=m, k=k: (own(m), block(m, 0, p), chain[k - 1]))()
            source = own(m) if k == 0 else block(m, k, p)
            to_x[m, k] = links.remote(lambda m=m, k=k, s=source: (s, block(m, k, p), beside))()
            to_y[m, k] = links.remote(lambda m=m, k=k, s=source: (s, block(m, k, p), above))()
            if k % 2 == 0:
                corner[m, k] = links.remote(lambda m=m, k=k: (block(m, k, p ^ 1), block(m, k, p ^ 1), above))()
            else:
                corner[m, k] = links.remote(lambda m=m, k=k: (block(m, k, p ^ 2), block(m, k, p ^ 2), beside))()
        for which in range(4):
            owner = (p, p ^ 1, p ^ 2, p ^ 3)[which]
            to_twin[m, which] = links.remote(lambda m=m, o=owner: (column(m, o), column(m, o), twin))()

    def unit(step):
        for m in range(1, mats):
            if step == (tps - 1 if m == 1 else tps * (m - 1) + 1):
                for j in range(1, tps):
                    along[m, j].start()
        if step < mats * tps:
            m, k = divmod(step, tps)
            if k:
                along[m, k].wait_recv()
                to_x[m, k].start()
                to_y[m, k].start()
            if k == tps - 1:
                keep[m].wait()
                to_twin[m, 0].start()
        if 0 <= step - 2 < mats * tps:
            m, k = divmod(step - 2, tps)
            to_x[m, k].wait_recv()
            if k % 2 == 0:
                corner[m, k].start()
            to_y[m, k].wait_recv()
            if k % 2:
                corner[m, k].start()
            if k == tps - 1:
                to_twin[m, 1].start()
                to_twin[m, 2].start()
        if 0 <= step - 4 < mats * tps:
            m, k = divmod(step - 4, tps)
            corner[m, k].wait_recv()
            if k == tps - 1:
                to_twin[m, 3].start()

    def prepare(m):
        level, kind = divmod(m, MATS)
        if kind == 0:
            arrivals[level][0].wait()
            arrivals[level][1].wait()
            for k in range(3):
                packed[m, :, k * wide : (k + 1) * wide] = wide_in[level, k].astype(low)
            packed[m, :, 3 * wide :] = out_in[level].T.astype(low)
        elif kind == 1:
            arrivals[level][2].wait()
            packed[m] = up_in[level].astype(low)
        else:
            arrivals[level][3].wait()
            packed[m] = down_in[level].astype(low)
        keep[m].start()
        to_x[m, 0].start()
        to_y[m, 0].start()
        if m == 0:
            for j in range(1, tps):
                along[m, j].start()

    prepare(0)
    for copy in cond_copies:
        copy.wait_recv()
    cond_own.wait()
    cond_rows = cond_in[...].reshape(-1, rows).astype(low)
    for k in range(2 * layers):
        mod_loads[k].wait()
        for j in range(3):
            value = dot_nn(cond_rows, mod_in[k % 2, j].astype(low))
            part[:, 3 * k + j] = value.reshape(part.shape[0], 8, wide)
        if k + 2 < 2 * layers:
            mod_loads[k + 2].start()
    part_copies = [links.remote(lambda q=q: (part.at[q[0]], part_in.at[p], q))() for q in plane]
    for copy in part_copies:
        copy.start()
    part_in[p] = part[p]
    for m in range(1, mats):
        prepare(m)
    column_copies = [links.remote(lambda q=q: (columns.at[t], columns.at[t], q))() for q in chain]

    def add_parts():
        for copy in part_copies:
            copy.wait_recv()
        columns[t] = part_in[0] + part_in[1] + part_in[2] + part_in[3]
        for copy in column_copies:
            copy.start()

    def join_columns():
        for copy in column_copies:
            copy.wait_recv()
        for k in range(6 * layers):
            for j in range(tps):
                mod_ref[k // 6, k % 6, :, j * wide : (j + 1) * wide] = columns[j, k]

    progress = [0]

    def tick():
        if progress[0] < mats * tps + 4:
            unit(progress[0])
            progress[0] += 1

    def arrive(m):
        while progress[0] < tps * m + tps + 4:
            tick()
        for which in range(4):
            to_twin[m, which].wait_recv()

    loads = {}

    def fetch(m, j):
        if (m, j) not in loads and m < mats:
            loads[m, j] = links.local(full_ref.at[m, j], wbuf.at[(m * tps + j) % SLOTS])
            loads[m, j].start()

    flock = frames // tps
    patches = rows_in.shape[1]
    strip = patches // tps

    def strip_of(owner):
        return pl.ds(pl.multiple_of(owner * strip, 16), strip)

    spread_rows = [
        links.remote(lambda k=k: (rows_ref.at[chain[k - 1][2]], rows_in.at[:, strip_of(t)], chain[k - 1]))() for k in range(1, tps)
    ]
    keep_rows = links.local(rows_ref.at[t], rows_in.at[:, strip_of(t)])

    part = strip // 2
    chunk = turned.shape[2]
    cot_copies = []
    for g in range(part // chunk):
        there = pl.ds(pl.multiple_of((1 - c) * part + g * chunk, 16), chunk)
        here = pl.ds(pl.multiple_of(c * part + g * chunk, 16), chunk)
        cot_copies.append(links.remote(lambda g=g, s=there: (cot_ref.at[:, :, s], cot_out.at[g, :, c], twin))())
        cot_copies.append(links.local(cot_ref.at[:, :, here], cot_out.at[g, :, c]))
    for copy in cot_copies:
        copy.start()

    saves = []

    def save(src, dst):
        copy = links.local(src, dst)
        copy.start()
        return copy

    def by_rows(body, size=64):
        def one(i, carry):
            body(pl.ds(pl.multiple_of(i * size, size), size))
            return carry

        lax.fori_loop(0, tokens // size, one, 0)

    def loop(count, body):
        def one(i, carry):
            body(i)
            return carry

        lax.fori_loop(0, count, one, 0)

    pending = {}

    def settle(name):
        if name in pending:
            for copy in pending.pop(name):
                copy.wait()

    for level in range(layers):
        hidden = hid.at[level]
        middle = mid.at[level]
        temporal = level % 2 == 1
        first, second, third = MATS * level, MATS * level + 1, MATS * level + 2
        if level == 0:
            tick()
            tick()
            add_parts()
            tick()
            tick()
            for copy in spread_rows + [keep_rows]:
                copy.start()
            tick()
            join_columns()
            for copy in spread_rows:
                copy.wait_recv()
            keep_rows.wait()
            for f in range(flock):
                loop(patches // 64, lambda i, f=f: hidden.__setitem__(
                    pl.ds(pl.multiple_of(f * patches + i * 64, 64), 64),
                    rows_in[f, pl.ds(pl.multiple_of(i * 64, 64), 64), :].astype(jnp.float32)))
        settle("x_a")
        factor = [mod_ref[level, k, 0:1, :] for k in range(6)]

        def enter(span, source=hidden, to=x_a, s=factor[0], r=factor[1]):
            normed, _ = normalize(source[span, :])
            to[span, :] = (normed * (1.0 + r) + s).astype(low)

        by_rows(enter)
        pending["x_a"] = [save(x_a, xa_out.at[level])]
        saves.append(save(hidden, hid_out.at[level]))
        settle("acc_a")
        acc_a[...] = jnp.zeros_like(acc_a)
        arrive(first)
        fetch(first, 0)
        for j in range(tps):
            tick()
            fetch(first, j + 1) if j + 1 < tps else None
            loads[first, j].wait()
            w = wbuf.at[(first * tps + j) % SLOTS]
            settle(("qkv", j % 2))
            settle(("mix", j % 2))
            qkv_j, mix_j = qkv.at[j % 2], mix.at[j % 2]

            def attention(g):
                span = pl.ds(pl.multiple_of(g * GROUP, GROUP), GROUP)
                x = x_a[span, :]
                q = dot_nn(x, w[:, 0:LANES])
                q = jnp.where(lane_mask(q.shape, 0, wide), q, 0.0).astype(low)
                k = pltpu.roll(dot_nn(x, w[:, 256 : 256 + LANES]), LANES - 32, 1)
                k = jnp.where(lane_mask(k.shape, 0, wide), k, 0.0).astype(low)
                v = pltpu.roll(dot_nn(x, w[:, 512 : 512 + LANES]), 32, 1)
                v = jnp.where(lane_mask(v.shape, LANES - wide, LANES), v, 0.0).astype(low)
                qkv_j[span, 0:LANES] = q
                qkv_j[span, LANES : 2 * LANES] = k
                qkv_j[span, 2 * LANES : 3 * LANES] = v
                scores = dot_nt(head_stack(q, 0, heads), k) * (HD ** (-0.5))
                probs = softmax_rows(scores, chunk if temporal else 0).astype(low)
                mixed = head_merge(dot_nn(probs, v), LANES - wide, heads).astype(low)
                mix_j[span, :] = mixed
                for i in range(width // LANES):
                    at = slice(i * LANES, (i + 1) * LANES)
                    acc_a[span, at] += dot_nt(mixed, w[at, 768 : 768 + LANES])

            loop(tokens // GROUP, attention)
            pending["qkv", j % 2] = [save(qkv_j, qkv_out.at[level, j])]
            pending["mix", j % 2] = [save(mix_j, mix_out.at[level, j])]
        settle("x_m")

        def between(span, hidden=hidden, middle=middle, gate=factor[2], s=factor[3], r=factor[4]):
            rows_mid = hidden[span, :] + gate * acc_a[span, :]
            middle[span, :] = rows_mid
            normed, _ = normalize(rows_mid)
            x_m[span, :] = (normed * (1.0 + r) + s).astype(low)

        by_rows(between)
        pending["acc_a"] = [save(acc_a, bra_out.at[level])]
        pending["x_m"] = [save(x_m, xm_out.at[level])]
        saves.append(save(middle, mid_out.at[level]))
        arrive(second)
        fetch(second, 0)
        for j in range(tps):
            tick()
            fetch(second, j + 1) if j + 1 < tps else None
            loads[second, j].wait()
            w = wbuf.at[(second * tps + j) % SLOTS]
            settle(("pre", j % 2))
            settle(("act", j))
            pre_j, act_j = pre.at[j % 2], act.at[j]

            def raise_up(i):
                at = pl.ds(pl.multiple_of(i * LANES, LANES), LANES)
                value = dot_nn(x_m[...], w[:, at])
                pre_j[:, at] = value
                act_j[:, at] = jax.nn.gelu(value, approximate=True).astype(low)

            loop(width // LANES, raise_up)
            pending["pre", j % 2] = [save(pre_j, pre_out.at[level, j])]
            pending["act", j] = [save(act_j, act_out.at[level, j])]
        settle("acc_m")
        acc_m[...] = jnp.zeros_like(acc_m)
        arrive(third)
        fetch(third, 0)
        for j in range(tps):
            tick()
            fetch(third, j + 1) if j + 1 < tps else None
            loads[third, j].wait()
            w = wbuf.at[(third * tps + j) % SLOTS]
            act_j = act.at[j]

            def lower(i):
                at = pl.ds(pl.multiple_of(i * LANES, LANES), LANES)
                acc_m[:, at] += dot_nt(act_j[...], w[at, :])

            loop(width // LANES, lower)
        if level + 1 < layers:
            def leave(span, middle=middle, gate=factor[5]):
                moved[span, :] = (middle[span, :] + gate * acc_m[span, :]).astype(low)

            by_rows(leave)
            pending["acc_m"] = [save(acc_m, brm_out.at[level])]
            away, stay = [], []
            here = (t * 2 + c) * flock
            for g in range(part // chunk):
                for f in range(flock):
                    goal = turned.at[g, here + f]
                    for peer in [None, twin] + chain + crossed:
                        _, pc, pt = peer or (p, c, t)
                        first_row = f * patches + pt * strip + pc * part + g * chunk
                        piece = moved.at[pl.ds(pl.multiple_of(first_row, 16), chunk)]
                        if peer is None:
                            stay.append(links.local(piece, goal))
                        else:
                            away.append(links.remote(lambda s=piece, d=goal, q=peer: (s, d, q))())
            for copy in away + stay:
                copy.start()
            tick()
            for copy in away:
                copy.wait()
            for copy in stay:
                copy.wait()
            nxt = hid.at[level + 1]
            for g in range(part // chunk):
                for f in range(turned.shape[1]):
                    base = (g * turned.shape[1] + f) * chunk
                    nxt[base : base + chunk, :] = turned[g, f].astype(jnp.float32)
        else:
            for g in range(part // chunk):
                for f in range(turned.shape[1]):
                    base = (g * turned.shape[1] + f) * chunk
                    span = slice(base, base + chunk)
                    turned[g, f] = (middle[span, :] + factor[5] * acc_m[span, :]).astype(low)
            pending["acc_m"] = [save(acc_m, brm_out.at[level])]
            home_copies = []
            for g in range(part // chunk):
                for ts in range(tps):
                    for f in range(flock):
                        to = pl.ds(pl.multiple_of(c * part + g * chunk, 16), chunk)
                        theirs = turned.at[g, (ts * 2 + 1 - c) * flock + f]
                        ours = turned.at[g, (ts * 2 + c) * flock + f]
                        home_copies.append(links.remote(lambda s=theirs, d=out_ref.at[ts, f, to]: (s, d, twin))())
                        home_copies.append(links.local(ours, out_ref.at[ts, f, to]))
            for copy in home_copies:
                copy.start()
    while progress[0] < mats * tps + 4:
        tick()
    for copy in saves + cot_copies + home_copies:
        copy.wait()
    for name in list(pending):
        settle(name)
    for copy in spread_rows + cond_copies + part_copies + column_copies:
        copy.wait_send()
    for m in range(mats):
        for which in range(4):
            to_twin[m, which].wait_send()
        for k in range(tps):
            if k:
                along[m, k].wait_send()
            to_x[m, k].wait_send()
            to_y[m, k].wait_send()
            corner[m, k].wait_send()


def forward_pass(masters, cond, rows, cot, mesh_shape):
    tps, dps, cs = mesh_shape["tp"], mesh_shape["dp"], mesh_shape["ctx"]
    qkv_w, out_w, up_w, down_w, mod_w = masters
    layers, _, depth, wide = qkv_w.shape
    heads = wide // HD
    mats, width = MATS * layers, rows.shape[-1]
    frames, strip = rows.shape[:2]
    flock = frames // tps
    tokens = frames * strip
    patches = strip * tps
    chunk = GROUP // (frames * cs)
    groups = strip // cs // chunk
    low, wider = jnp.bfloat16, jnp.float32
    sds = jax.ShapeDtypeStruct
    whole = pl.BlockSpec(memory_space=pl.ANY)
    return pl.pallas_call(
        partial(forward_kernel, tps, (layers, frames, wide, heads)),
        out_shape=[
            sds((mats, tps, dps * depth, width), low),
            sds((tps, flock, strip, width), low),
            sds((groups, tps, cs, flock, chunk, width), low),
            sds((layers, tokens, width), wider),
            sds((layers, tokens, width), wider),
            sds((layers, tokens, width), wider),
            sds((layers, tokens, width), wider),
            sds((layers, tokens, width), low),
            sds((layers, tokens, width), low),
            sds((layers, tps, tokens, 3 * LANES), low),
            sds((layers, tps, tokens, LANES), low),
            sds((layers, tps, tokens, width), wider),
            sds((layers, tps, tokens, width), low),
            sds((layers, 6, 8, width), wider),
            sds((dps, 8, depth), wider),
        ],
        in_specs=[whole] * 8,
        out_specs=[whole] * 13 + [pl.BlockSpec(memory_space=pltpu.VMEM)] * 2,
        scratch_shapes=[
            pltpu.VMEM((layers, tokens, width), wider),
            pltpu.VMEM((layers, tokens, width), wider),
            pltpu.VMEM((tokens, width), wider),
            pltpu.VMEM((tokens, width), wider),
            pltpu.VMEM((tokens, width), low),
            pltpu.VMEM((tokens, width), low),
            pltpu.VMEM((SLOTS, dps * depth, width), low),
            pltpu.VMEM((tps, tokens, width), low),
            pltpu.VMEM((2, tokens, width), wider),
            pltpu.VMEM((2, tokens, 3 * LANES), low),
            pltpu.VMEM((2, tokens, LANES), low),
            pltpu.VMEM((flock, patches, width), low),
            pltpu.VMEM((tokens, width), low),
            pltpu.VMEM((groups, frames * cs, chunk, width), low),
            pltpu.VMEM((mats, depth, width), low),
            pltpu.VMEM(qkv_w.shape, wider),
            pltpu.VMEM(out_w.shape, wider),
            pltpu.VMEM(up_w.shape, wider),
            pltpu.VMEM(down_w.shape, wider),
            pltpu.VMEM((2, 3, depth, wide), wider),
            pltpu.VMEM((dps, 6 * layers, 8, wide), wider),
            pltpu.VMEM((dps, 6 * layers, 8, wide), wider),
            pltpu.VMEM((tps, 6 * layers, 8, wide), wider),
            pltpu.SemaphoreType.DMA((200,)),
            pltpu.SemaphoreType.DMA((200,)),
            pltpu.SemaphoreType.DMA((140,)),
        ],
        compiler_params=pltpu.CompilerParams(
            collective_id=0, has_side_effects=True, vmem_limit_bytes=VMEM_LIMIT
        ),
        name="forward_pass",
    )(qkv_w, out_w, up_w, down_w, mod_w, cond, rows.reshape(tps, flock, strip, width), cot.reshape(tps, flock, strip, width))


def gelu_slope(v):
    root, cubic = 0.7978845608028654, 0.044715
    square = v * v
    bend = jnp.tanh(root * v * (1.0 + cubic * square))
    return 0.5 * (1.0 + bend) + 0.5 * v * (1.0 - bend * bend) * (root * (1.0 + 3.0 * cubic * square))


def backward_kernel(tps, geometry, *refs):
    layers, frames, wide, heads = geometry
    (full_ref, cot_ref, mod_ref, cond_in, mod_w, hid_ref, mid_ref, bra_ref, brm_ref, xa_ref, xm_ref, qkv_ref, mix_ref, pre_ref, act_ref,
     red_ref, home_ref, d_all, d_cond, norm_ref,
     tot, grad, twin_in, corner_in, beside_in, above_in, chain_in, last,
     g, dacc, lhs, x, wbuf, side, pre, dpre, mix, branch, base, arrived,
     dmod_ref, d_cut, d_in, mod_in, z_in, squares, norm_in, norm_line,
     send_sem, recv_sem, local_sem, free_sem) = refs
    p, c, t = place()
    mats = full_ref.shape[0]
    half, width = last.shape
    rows = 2 * half
    depth = full_ref.shape[2]
    dps = depth // rows
    tokens = g.shape[0]
    low = jnp.bfloat16
    mine = pl.ds(pl.multiple_of(c * half, 16), half)
    theirs = pl.ds(pl.multiple_of((1 - c) * half, 16), half)
    beside, above, twin = (p ^ 1, c, t), (p ^ 2, c, t), (p, 1 - c, t)
    chain = [(p, c, lax.rem(t + k, tps)) for k in range(1, tps)]
    crossed = [(p, 1 - c, lax.rem(t + k, tps)) for k in range(1, tps)]
    plane = [(p ^ k, c, t) for k in range(1, 4)]
    across = [(p ^ k, 1 - c, t) for k in range(1, 4)]
    greet(chain + crossed + plane + across + [twin])
    links = Links(send_sem, recv_sem, local_sem)
    units = mats * tps
    kinds = [(level, kind) for level in reversed(range(layers)) for kind in (2, 1, 0)]

    TWIN, CHAIN, CORNER, BESIDE, ABOVE = 0, 2, 2 + tps, 2 + tps + RING, 2 + tps + 2 * RING

    def credit(slot, peer, u, gap):
        if u + gap < units:
            pl.semaphore_signal(free_sem.at[slot], inc=1, device_id=peer, device_id_type=MESH)

    def spend(slot, u, gap):
        if u >= gap:
            pl.semaphore_wait(free_sem.at[slot], 1)

    to_twin, to_corner, to_x, to_y, along, finish, keep = {}, {}, {}, {}, {}, {}, {}
    for u in range(units):
        n, i = divmod(u, tps)
        here = tot.at[n % 2, i]
        to_twin[u] = links.remote(lambda u=u: (grad.at[u % 2, :, theirs], twin_in.at[u % 2], twin))()
        via = beside if i % 2 == 0 else above
        to_corner[u] = links.remote(lambda h=here, u=u, v=via: (h.at[p ^ 3], corner_in.at[u % RING], v))()
        to_x[u] = links.remote(lambda h=here, u=u: (h.at[p ^ 1], beside_in.at[u % RING], beside))()
        to_y[u] = links.remote(lambda h=here, u=u: (h.at[p ^ 2], above_in.at[u % RING], above))()
        if i < tps - 1:
            along[u] = links.remote(lambda h=here, i=i: (h.at[p], chain_in.at[i], chain[i]))()
        else:
            level, kind = kinds[n]
            goal = red_ref.at[MATS * level + kind, mine]
            finish[n] = links.remote(lambda d=goal: (last, d, twin))()
            keep[n] = links.local(last, goal)

    def plus(a, b):
        return (a.astype(jnp.float32) + b.astype(jnp.float32)).astype(low)

    def release(u):
        if u >= 2:
            to_twin[u - 2].wait_send()
        n, i = divmod(u, tps)
        if n >= 2:
            old = u - 2 * tps
            to_corner[old].wait_send()
            to_x[old].wait_send()
            to_y[old].wait_send()
            if i < tps - 1:
                along[old].wait_send()

    def stage_a(u):
        spend(TWIN + u % 2, u, 2)
        to_twin[u].start()

    def stage_b(u):
        n, i = divmod(u, tps)
        to_twin[u].wait_recv()
        here = tot.at[n % 2, i]

        def one(q, carry):
            here[q] = plus(grad[u % 2, q, mine], twin_in[u % 2, q])
            return carry

        lax.fori_loop(0, dps, one, 0)
        credit(TWIN + u % 2, twin, u, 2)
        spend(CORNER + u % RING, u, RING)
        to_corner[u].start()

    def stage_c(u):
        n, i = divmod(u, tps)
        here = tot.at[n % 2, i]
        to_corner[u].wait_recv()
        if i % 2 == 0:
            here[p ^ 2] = plus(here[p ^ 2], corner_in[u % RING])
            credit(CORNER + u % RING, beside, u, RING)
        else:
            here[p ^ 1] = plus(here[p ^ 1], corner_in[u % RING])
            credit(CORNER + u % RING, above, u, RING)
        spend(ABOVE + u % RING, u, RING)
        to_y[u].start()
        spend(BESIDE + u % RING, u, RING)
        to_x[u].start()

    def stage_d(u):
        n, i = divmod(u, tps)
        here = tot.at[n % 2, i]
        to_x[u].wait_recv()
        to_y[u].wait_recv()
        own = here[p].astype(jnp.float32) + beside_in[u % RING].astype(jnp.float32) + above_in[u % RING].astype(jnp.float32)
        credit(BESIDE + u % RING, beside, u, RING)
        credit(ABOVE + u % RING, above, u, RING)
        if i < tps - 1:
            here[p] = own.astype(low)
            spend(CHAIN + i, u, tps)
            along[u].start()
            return
        for k in range(tps - 1):
            along[u - tps + 1 + k].wait_recv()
            own = own + chain_in[k].astype(jnp.float32)
            credit(CHAIN + k, (p, c, lax.rem(t + tps - 1 - k, tps)), u - tps + 1 + k, tps)
        if n:
            finish[n - 1].wait_send()
            keep[n - 1].wait()
        last[...] = own.astype(low)
        kept = last[...].astype(jnp.float32)
        squares[...] += jnp.sum((kept * kept).reshape(half // 8, 8, width), axis=0)
        finish[n].start()
        keep[n].start()

    reached = [0, 0, 0]

    def advance(done, extra=0):
        for which, (stage, lag) in enumerate(zip((stage_d, stage_b, stage_c), LAGS)):
            while reached[which] < min(units, done) and reached[which] + lag <= done + extra - 1:
                stage(reached[which])
                reached[which] += 1

    loads = {}

    def fetch(u):
        if u >= units or u in loads:
            return
        n, i = divmod(u, tps)
        level, kind = kinds[n]
        owner = lax.rem(t + 1 + i, tps)
        copies = [links.local(full_ref.at[MATS * level + kind, owner], wbuf.at[u % 2])]
        if kind == 2:
            copies.append(links.local(act_ref.at[level, owner], side.at[u % 2]))
        if kind == 0:
            copies.append(links.local(qkv_ref.at[level, owner], side.at[u % 2]))
            copies.append(links.local(mix_ref.at[level, owner], mix.at[i]))
        for copy in copies:
            copy.start()
        loads[u] = copies

    def bring(src, dst):
        copy = links.local(src, dst)
        copy.start()
        return copy

    def by_rows(body, size=64):
        def one(i, carry):
            body(pl.ds(pl.multiple_of(i * size, size), size))
            return carry

        lax.fori_loop(0, tokens // size, one, 0)

    def loop(count, body):
        def one(i, carry):
            body(i)
            return carry

        lax.fori_loop(0, count, one, 0)

    def column_sum(level, k, value):
        dmod_ref[level, k] += jnp.sum(value.reshape(value.shape[0] // 8, 8, width), axis=0)

    def lanes(i):
        return pl.ds(pl.multiple_of(i * LANES, LANES), LANES)

    def put(u, at, value):
        grad[u % 2, :, :, at] = value.astype(low).reshape(dps, rows, LANES)

    dmod_ref[...] = jnp.zeros_like(dmod_ref)
    squares[...] = jnp.zeros_like(squares)
    d_cut[...] = jnp.zeros_like(d_cut)
    top = layers - 1
    fetch(0)
    first = bring(cot_ref, arrived)
    branch_load, base_load = bring(brm_ref.at[top], branch), bring(mid_ref.at[top], base)
    first.wait()
    g[...] = arrived[...].astype(jnp.float32)
    tail, remotes = [], []

    def send_all(pairs):
        copies = [links.remote(lambda v=v: v)() for v in pairs]
        for copy in copies:
            copy.start()
        remotes.extend(copies)
        return copies

    flying = {}
    own_slot = 2 * t + c

    def landed(name):
        for copy in flying[name]:
            copy.wait_recv()

    def added(ref, count):
        total = ref[0]
        for k in range(1, count):
            total = total + ref[k]
        return total

    def cut_columns():
        mod_loads[0].start()
        for k in range(6 * layers):
            line = jnp.sum(dmod_ref[k // 6, k % 6], axis=0, keepdims=True)
            for j in range(tps):
                d_cut[j, k : k + 1, :] = line[:, j * wide : (j + 1) * wide]
        flying["cut"] = send_all([(d_cut.at[q[2]], d_in.at[own_slot], q) for q in chain + crossed + [twin]])
        d_in[own_slot] = d_cut[t]

    def share_clips():
        landed("cut")
        d_all[p] = added(d_in, 2 * tps)
        flying["clips"] = send_all([(d_all.at[p], d_all.at[p], q) for q in plane])

    def share_rows():
        landed("clips")
        share = jnp.zeros((8, rows), jnp.float32)
        for k in range(2 * layers):
            mod_loads[k].wait()
            for j in range(3):
                at = 3 * k + j
                lines = jnp.concatenate([d_all[q, at : at + 1, :] for q in range(dps)] + [jnp.zeros((8 - dps, wide), jnp.float32)], axis=0)
                coarse = lines.astype(low)
                fine = (lines - coarse.astype(jnp.float32)).astype(low)
                weight = mod_in[j].astype(low)
                share = share + dot_nt(coarse, weight) + dot_nt(fine, weight)
            if k + 1 < 2 * layers:
                mod_loads[k + 1].start()
        z_in[t] = share
        flying["shares"] = send_all([(z_in.at[t], z_in.at[t], q) for q in chain])

    def rows_home():
        landed("shares")
        d_cond[p] = added(z_in, tps)
        flying["homes"] = send_all([(d_cond.at[p], d_cond.at[p], q) for q in plane])
        conds = jnp.concatenate([cond_in[a, 0:1, :] for a in range(dps)], axis=0)
        gram = jnp.zeros((1, wide), jnp.float32)
        for b in range(dps):
            left = jnp.sum(conds * cond_in[b, 0:1, :], axis=1, keepdims=True)
            for a in range(dps):
                gram = gram + left[a : a + 1, 0:1] * jnp.sum(d_all[a] * d_all[b], axis=0, keepdims=True)
        squares[0:1, 0:wide] += 0.5 * gram

    def norm_of_all():
        line = jnp.sum(jnp.sum(squares[...], axis=0, keepdims=True), axis=1, keepdims=True)
        slot = 2 * p + c
        norm_in[slot] = jnp.broadcast_to(line, norm_ref.shape)
        flying["plane"] = send_all([(norm_in.at[slot], norm_in.at[slot], q) for q in plane + across + [twin]])
        landed("plane")
        norm_line[t] = added(norm_in, 2 * dps)
        flying["line"] = send_all([(norm_line.at[t], norm_line.at[t], q) for q in chain])
        landed("line")
        norm_ref[...] = added(norm_line, tps)
        landed("homes")

    mod_loads = [links.local(mod_w.at[k // 2, pl.ds(3 * (k % 2), 3)], mod_in) for k in range(2 * layers)]

    for level in reversed(range(layers)):
        factor = [mod_ref[level, k, 0:1, :] for k in range(6)]
        temporal = level % 2 == 1
        chunk = GROUP // (2 * frames)
        start = kinds.index((level, 2)) * tps
        x_load = bring(xm_ref.at[level], x)
        branch_load.wait()

        def open_m(span, gate=factor[5], level=level):
            value = g[span, :]
            column_sum(level, 5, value * branch[span, :])
            lhs[span, :] = (gate * value).astype(low)

        by_rows(open_m)
        branch_load = bring(bra_ref.at[level], branch)
        for i in range(tps):
            u = start + i
            if i == 0:
                pre_load = bring(pre_ref.at[level, lax.rem(t + 1, tps)], pre)
            release(u)
            for copy in loads[u]:
                copy.wait()
            fetch(u + 1)
            w, act = wbuf.at[u % 2], side.at[u % 2]
            pre_load.wait()

            def third(k, u=u, i=i, w=w, act=act):
                at = lanes(k)
                put(u, at, dot_tn(lhs[...], act[:, at]))
                d_act = dot_nn(lhs[...], w[:, at])
                dpre[i, :, at] = (d_act * gelu_slope(pre[:, at])).astype(low)

            loop(width // LANES, third)
            if i + 1 < tps:
                pre_load = bring(pre_ref.at[level, lax.rem(t + 2 + i, tps)], pre)
            stage_a(u)
            advance(u + 1)
        dacc[...] = jnp.zeros_like(dacc)
        x_load.wait()
        for i in range(tps):
            u = start + tps + i
            release(u)
            for copy in loads[u]:
                copy.wait()
            fetch(u + 1)
            w = wbuf.at[u % 2]

            def second(k, u=u, i=i, w=w):
                at = lanes(k)
                put(u, at, dot_tn(x[...], dpre[i, :, at]))
                dacc[:, at] += dot_nt(dpre[i], w[at, :])

            loop(width // LANES, second)
            stage_a(u)
            advance(u + 1)
        x_load = bring(xa_ref.at[level], x)
        base_load.wait()
        branch_load.wait()

        def turn_back(span, source, s_at, r_at, r):
            normed, rstd = normalize(source[span, :])
            d = dacc[span, :]
            column_sum(level, s_at, d)
            column_sum(level, r_at, d * normed)
            return g[span, :] + normalize_back(d * (1.0 + r), normed, rstd)

        def close_m(span, r=factor[4], gate=factor[2], level=level):
            value = turn_back(span, base, 3, 4, r)
            g[span, :] = value
            column_sum(level, 2, value * branch[span, :])
            lhs[span, :] = (gate * value).astype(low)

        by_rows(close_m)
        base_load = bring(hid_ref.at[level], base)
        if level:
            branch_load = bring(brm_ref.at[level - 1], branch)
        dacc[...] = jnp.zeros_like(dacc)
        x_load.wait()

        def weigh(i, start=start):
            u = start + 2 * tps + i
            release(u)

            def first(k):
                at = lanes(k)
                put(u, at, dot_tn(x[...], dpre[i, :, at]))

            loop(width // LANES - 1, first)
            at = slice(width - LANES, width)
            put(u, at, dot_tn(x[...], dpre[i, :, at]) + dot_tn(lhs[...], mix[i]))
            stage_a(u)

        for i in range(tps):
            u = start + 2 * tps + i
            for copy in loads[u]:
                copy.wait()
            fetch(u + 1)
            w, qkv_j, dproj = wbuf.at[u % 2], side.at[u % 2], dpre.at[i]

            def attention(k, w=w, qkv_j=qkv_j, dproj=dproj, temporal=temporal, chunk=chunk):
                span = pl.ds(pl.multiple_of(k * GROUP, GROUP), GROUP)
                scale = HD ** (-0.5)
                low_v = LANES - wide
                d_mix = dot_nn(lhs[span, :], w[:, 768 : 768 + LANES]).astype(low)
                d_mix4 = head_stack(d_mix, low_v, heads)
                query4 = head_stack(qkv_j[span, 0:LANES], 0, heads)
                key, value = qkv_j[span, LANES : 2 * LANES], qkv_j[span, 2 * LANES : 3 * LANES]
                probs = softmax_rows(dot_nt(query4, key) * scale, chunk if temporal else 0)
                d_probs = dot_nt(d_mix4, value)
                d_scores = (probs * (d_probs - jnp.sum(probs * d_probs, axis=-1, keepdims=True))).astype(low)
                d_value = pltpu.roll(dot_tn(probs.astype(low), d_mix4), LANES - 32, 1)
                d_query = head_merge(dot_nn(d_scores, key), 0, heads) * scale
                d_key = pltpu.roll(dot_tn(d_scores, query4), 32, 1) * scale
                dproj[span, 0:256] = d_query[:, 0:256].astype(low)
                dproj[span, 256:384] = (d_query[:, 256:384] + d_key[:, 0:128]).astype(low)
                dproj[span, 384:512] = d_key[:, 128:256].astype(low)
                dproj[span, 512:640] = (d_key[:, 256:384] + d_value[:, 0:128]).astype(low)
                dproj[span, 640:896] = d_value[:, 128:384].astype(low)
                dproj[span, 896:1152] = jnp.zeros((GROUP, 256), low)

            loop(tokens // GROUP, attention)
            for k in range(width // LANES):
                at = slice(k * LANES, (k + 1) * LANES)
                dacc[:, at] += dot_nt(dproj[:, 0:896], w[at, 0:896])
            if level:
                advance(start + 2 * tps, i + 1)
            else:
                weigh(i)
                advance(u + 1)
        base_load.wait()
        outgoing = side.at[1]

        def close_a(span, r=factor[1], level=level):
            value = turn_back(span, base, 0, 1, r)
            g[span, :] = value
            outgoing[span, :] = value.astype(low)

        by_rows(close_a)
        flock, patches = home_ref.shape[:2]
        strip = patches // tps
        part = strip // 2
        if level:
            base_load = bring(mid_ref.at[level - 1], base)
            away, stay = [], []
            for k in range(part // chunk):
                for f in range(flock):
                    to = pl.ds(pl.multiple_of(f * patches + t * strip + c * part + k * chunk, 16), chunk)
                    for peer in [None, twin] + chain + crossed:
                        _, pc, pt = peer or (p, c, t)
                        row = (k * 2 * frames + (pt * 2 + pc) * flock + f) * chunk
                        piece = outgoing.at[pl.ds(pl.multiple_of(row, 16), chunk)]
                        if peer is None:
                            stay.append(links.local(piece, arrived.at[to]))
                        else:
                            away.append(links.remote(lambda s=piece, d=arrived.at[to], q=peer: (s, d, q))())
            moves, steps = away + stay, []
        else:
            tail.extend(links.local(outgoing.at[pl.ds(f * patches, patches)], home_ref.at[f]) for f in range(flock))
            moves, steps = tail, [cut_columns, share_clips, share_rows, rows_home]
        for copy in moves:
            copy.start()
        if level:
            for i in range(tps):
                weigh(i)
                advance(start + 2 * tps + i + 1)
        else:
            for more, step in enumerate(steps):
                step()
                advance(units, more + 1)
        if level:
            for copy in moves:
                copy.wait()
            g[...] = arrived[...].astype(jnp.float32)
    for more in range(1, 1 + LAGS[0]):
        advance(units, more)
    norm_of_all()
    for copy in remotes:
        copy.wait_send()
    for u in range(units):
        if u >= units - 2:
            to_twin[u].wait_send()
        if u >= units - 2 * tps:
            to_corner[u].wait_send()
            to_x[u].wait_send()
            to_y[u].wait_send()
            if u in along:
                along[u].wait_send()
    for n in range(mats):
        finish[n].wait_recv()
    finish[mats - 1].wait_send()
    keep[mats - 1].wait()
    for copy in tail:
        copy.wait()


def backward_pass(full, cot_rows, modulation, cond_rows, mod_w, saved, mesh_shape, frames, strip):
    tps, dps = mesh_shape["tp"], mesh_shape["dp"]
    mats, _, depth, width = full.shape
    layers, tokens = saved[0].shape[:2]
    rows = depth // dps
    half = rows // 2
    wide = mod_w.shape[-1]
    heads = wide // HD
    low, wider = jnp.bfloat16, jnp.float32
    sds = jax.ShapeDtypeStruct
    whole = pl.BlockSpec(memory_space=pl.ANY)
    near = pl.BlockSpec(memory_space=pltpu.VMEM)
    return pl.pallas_call(
        partial(backward_kernel, tps, (layers, frames, heads * HD, heads)),
        out_shape=[
            sds((mats, rows, width), low),
            sds((frames // tps, strip * tps, width), low),
            sds((dps, 16, wide), wider),
            sds((dps, 8, rows), wider),
            sds((8, 128), wider),
        ],
        in_specs=[whole, whole, near, near] + [whole] * 11,
        out_specs=[whole, whole, near, near, near],
        scratch_shapes=[
            pltpu.VMEM((2, tps, dps, half, width), low),
            pltpu.VMEM((2, dps, rows, width), low),
            pltpu.VMEM((2, dps, half, width), low),
            pltpu.VMEM((RING, half, width), low),
            pltpu.VMEM((RING, half, width), low),
            pltpu.VMEM((RING, half, width), low),
            pltpu.VMEM((tps - 1, half, width), low),
            pltpu.VMEM((half, width), low),
            pltpu.VMEM((tokens, width), wider),
            pltpu.VMEM((tokens, width), wider),
            pltpu.VMEM((tokens, width), low),
            pltpu.VMEM((tokens, width), low),
            pltpu.VMEM((2, depth, width), low),
            pltpu.VMEM((2, tokens, width), low),
            pltpu.VMEM((tokens, width), wider),
            pltpu.VMEM((tps, tokens, width), low),
            pltpu.VMEM((tps, tokens, LANES), low),
            pltpu.VMEM((tokens, width), wider),
            pltpu.VMEM((tokens, width), wider),
            pltpu.VMEM((tokens, width), low),
            pltpu.VMEM((layers, 6, 8, width), wider),
            pltpu.VMEM((tps, 16, wide), wider),
            pltpu.VMEM((2 * tps, 16, wide), wider),
            pltpu.VMEM((3, rows, wide), wider),
            pltpu.VMEM((tps, 8, rows), wider),
            pltpu.VMEM((8, width), wider),
            pltpu.VMEM((2 * dps, 8, 128), wider),
            pltpu.VMEM((tps, 8, 128), wider),
            pltpu.SemaphoreType.DMA((200,)),
            pltpu.SemaphoreType.DMA((200,)),
            pltpu.SemaphoreType.DMA((110,)),
            pltpu.SemaphoreType.REGULAR((2 + tps + 3 * RING,)),
        ],
        compiler_params=pltpu.CompilerParams(
            collective_id=1, has_side_effects=True, vmem_limit_bytes=VMEM_LIMIT
        ),
        name="backward_pass",
    )(full, cot_rows.reshape(tokens, width), modulation, cond_rows, mod_w, *saved)


def sum_grads(grads):
    parts = []
    for grad in grads:
        part = lax.psum_scatter(grad, "tp", scatter_dimension=0, tiled=True)[0]
        part = lax.psum_scatter(part, "dp", scatter_dimension=0, tiled=True)
        parts.append(lax.psum(part, "ctx"))
    return jnp.stack(parts)


def update_kernel(wide, red_ref, norm_ref, cond_ref, lines_ref, *refs):
    masters, firsts, seconds = refs[0:5], refs[5:10], refs[10:15]
    news, copies, moments, squares = refs[15:20], refs[20:25], refs[25:30], refs[30:35]
    level, part = pl.program_id(0), pl.program_id(1)
    coef = CLIP_MAX / jnp.maximum(jnp.sqrt(norm_ref[0:1, 0:1]), CLIP_MAX)

    def step(kind, at, grad):
        new, copy, moment, square = adam_update(masters[kind][at], firsts[kind][at], seconds[kind][at], grad, coef)
        news[kind][at] = new
        copies[kind][at] = copy
        moments[kind][at] = moment
        squares[kind][at] = square

    rows = masters[0].shape[2]
    span = pl.ds(pl.multiple_of(part * rows, 32), rows)
    first = red_ref[0, span, :].astype(jnp.float32)
    for k in range(3):
        step(0, (0, k), first[:, k * wide : (k + 1) * wide])
    step(2, 0, red_ref[1, span, :].astype(jnp.float32))
    step(3, 0, red_ref[2, span, :].astype(jnp.float32))

    @pl.when(part == 0)
    def _():
        step(1, 0, red_ref[0, :, 3 * wide :].astype(jnp.float32).T)

    for k in range(2):
        lines = lines_ref[level * 6 + part * 2 + k]
        grad = cond_ref[:, 0:1] * lines[0:1, :]
        for q in range(1, lines_ref.shape[1]):
            grad = grad + cond_ref[:, q : q + 1] * lines[q : q + 1, :]
        step(4, (0, k), grad)


def update_all(reduced, norm, cond_columns, lines, masters, firsts, seconds):
    layers, _, rows, wide = masters[0].shape
    width = reduced.shape[-1]
    parts = 3
    blocks = (
        pl.BlockSpec((1, 3, rows // parts, wide), lambda l, q: (l, 0, q, 0)),
        pl.BlockSpec((1, wide, rows), lambda l, q: (l, 0, 0)),
        pl.BlockSpec((1, rows // parts, width), lambda l, q: (l, q, 0)),
        pl.BlockSpec((1, rows // parts, width), lambda l, q: (l, q, 0)),
        pl.BlockSpec((1, 6 // parts, rows, wide), lambda l, q: (l, q, 0, 0)),
    )
    small = [pl.BlockSpec(a.shape, lambda l, q, n=a.ndim: (0,) * n) for a in (norm, cond_columns, lines)]
    shapes = [[jax.ShapeDtypeStruct(w.shape, kind) for w in masters] for kind in (jnp.float32, jnp.bfloat16, jnp.float32, jnp.float32)]
    return pl.pallas_call(
        partial(update_kernel, wide),
        grid=(layers, parts),
        out_shape=sum(shapes, []),
        in_specs=[pl.BlockSpec((MATS, rows, width), lambda l, q: (l, 0, 0))] + small + list(blocks) * 3,
        out_specs=list(blocks) * 4,
        compiler_params=pltpu.CompilerParams(vmem_limit_bytes=VMEM_LIMIT),
        cost_estimate=pl.CostEstimate(
            flops=20 * sum(w.size for w in masters), bytes_accessed=26 * sum(w.size for w in masters), transcendentals=0
        ),
        name="update_all",
    )(reduced, norm, cond_columns, lines, *masters, *firsts, *seconds)


def pack(qkv, out, up, down):
    rows = qkv.shape[0]
    low = jnp.bfloat16
    first = jnp.concatenate([qkv.astype(low).reshape(rows, -1), out.astype(low).T], axis=1)
    return jnp.stack([first, up.astype(low), down.astype(low).T])


def unpack(first, second, third, like):
    rows, _, wide = like.shape
    cut = 3 * wide
    return (first[:, :cut].reshape(rows, 3, wide), first[:, cut:].T, second, third.T)


def frames_whole(rows):
    return lax.all_to_all(rows, "tp", 0, 1, tiled=True)


def frames_back(rows):
    return lax.all_to_all(rows, "tp", 1, 0, tiled=True)


def patches_whole(rows):
    return lax.all_to_all(rows, ("tp", "ctx"), 1, 0, tiled=True)


def patches_back(rows):
    return lax.all_to_all(rows, ("tp", "ctx"), 0, 1, tiled=True)


def columns_home(rows, mesh_shape):
    frames, patches, width = rows.shape
    tps, cs = mesh_shape["tp"], mesh_shape["ctx"]
    split = rows.reshape(tps, cs, frames // (tps * cs), patches, width)
    split = split.transpose(1, 0, 2, 3, 4).reshape(cs, frames // cs, patches, width)
    return lax.all_to_all(split, "ctx", 0, 2, tiled=True)[0]


def columns_away(rows, mesh_shape):
    tps, cs = mesh_shape["tp"], mesh_shape["ctx"]
    frames, patches, width = rows.shape
    split = lax.all_to_all(rows[None], "ctx", 2, 0, tiled=True)
    split = split.reshape(cs, tps, frames // tps, patches // cs, width).transpose(1, 0, 2, 3, 4)
    return split.reshape(frames * cs, patches // cs, width)


def per_device_plain(mesh_shape, inputs, conditioning, *states):
    masters, firsts, seconds, cotangent = states[:5], states[5:10], states[10:15], states[15]
    qkv_weight, out_weight, up_weight, down_weight, mod_weight = masters
    low = jnp.bfloat16
    highest = lax.Precision.HIGHEST
    layers = qkv_weight.shape[0]
    scale = HD ** (-0.5)
    dp_at, _, tp_at = place()
    tps, dps = mesh_shape["tp"], mesh_shape["dp"]
    rows = qkv_weight.shape[1]
    wide = qkv_weight.shape[3]
    heads = wide // HD
    width = inputs.shape[-1]

    shards = jnp.concatenate(
        [pack(qkv_weight[l], out_weight[l], up_weight[l], down_weight[l]) for l in range(layers)]
    )
    full = gather_weights(shards)

    cond_low = jax.nn.silu(conditioning).astype(low)
    cond_all = lax.all_gather(cond_low, "dp", axis=0, tiled=True)
    cond_mine = lax.dynamic_slice_in_dim(cond_all, dp_at * rows, rows, 1)
    mod_low = mod_weight.astype(low)
    mod_part = jnp.einsum("cd,ldke->clke", cond_mine, mod_low, preferred_element_type=jnp.float32)
    mod_part = lax.psum_scatter(mod_part, "dp", scatter_dimension=0, tiled=True)
    modulation = lax.all_gather(mod_part, "tp", axis=3, tiled=True)[0]

    hidden = frames_whole(inputs[0]).astype(jnp.float32)
    saved = []
    for level in range(layers):
        if level:
            if level % 2 == 1:
                hidden = patches_whole(hidden.astype(low)).astype(jnp.float32)
            else:
                hidden = patches_back(hidden.astype(low)).astype(jnp.float32)
        forms = SPATIAL_FORMS if level % 2 == 0 else TEMPORAL_FORMS
        first_w, up_w, down_w = full[MATS * level], full[MATS * level + 1], full[MATS * level + 2]
        factors = modulation[level]
        frames, patches = hidden.shape[:2]
        normed_a, rstd_a = normalize(hidden)
        attn_in = (normed_a * (1.0 + factors[1]) + factors[0]).astype(low)
        projected = jnp.einsum(
            "fpd,jde->fpje", attn_in, first_w[:, :, : 3 * wide], preferred_element_type=jnp.float32
        ).astype(low)
        projected = projected.reshape(frames, patches, tps, 3, heads, HD)
        query, key, value = (projected[:, :, :, s] for s in range(3))
        mixed, log_total = attend(query, key, value, forms, scale)
        mixed = mixed.reshape(frames, patches, tps, wide)
        branch_a = jnp.einsum(
            "fpje,jde->fpd", mixed, first_w[:, :, 3 * wide :], preferred_element_type=jnp.float32
        )
        middle = hidden + factors[2] * branch_a
        normed_m, rstd_m = normalize(middle)
        mlp_in = (normed_m * (1.0 + factors[4]) + factors[3]).astype(low)
        hidden_pre = jnp.einsum("fpd,jdh->fpjh", mlp_in, up_w, preferred_element_type=jnp.float32)
        hidden_act = jax.nn.gelu(hidden_pre, approximate=True).astype(low)
        branch_m = jnp.einsum("fpjh,jdh->fpd", hidden_act, down_w, preferred_element_type=jnp.float32)
        saved.append(
            (forms, first_w, up_w, down_w, factors, normed_a, rstd_a, attn_in, query, key, value,
             mixed, log_total, branch_a, normed_m, rstd_m, mlp_in, hidden_pre, hidden_act, branch_m)
        )
        hidden = middle + factors[5] * branch_m
    temporal_end = layers % 2 == 0
    output = hidden.astype(low)
    output = columns_home(output, mesh_shape) if temporal_end else frames_back(output)
    upstream = columns_away(cotangent[0], mesh_shape) if temporal_end else frames_whole(cotangent[0])
    upstream = upstream.astype(jnp.float32)

    grads = [None] * (MATS * layers)
    d_mods = [None] * layers
    for level in reversed(range(layers)):
        (forms, first_w, up_w, down_w, factors, normed_a, rstd_a, attn_in, query, key, value,
         mixed, log_total, branch_a, normed_m, rstd_m, mlp_in, hidden_pre, hidden_act, branch_m) = saved[level]
        frames, patches = upstream.shape[:2]
        d_gate_m = jnp.sum(upstream * branch_m, axis=(0, 1))
        d_branch_m = (factors[5] * upstream).astype(low)
        grads[MATS * level + 2] = jnp.einsum(
            "fpd,fpjh->jdh", d_branch_m, hidden_act, preferred_element_type=jnp.float32
        ).astype(low)
        d_act = jnp.einsum("fpd,jdh->fpjh", d_branch_m, down_w, preferred_element_type=jnp.float32)
        slope_pull = jax.vjp(partial(jax.nn.gelu, approximate=True), hidden_pre)[1]
        d_pre = slope_pull(d_act)[0].astype(low)
        grads[MATS * level + 1] = jnp.einsum(
            "fpd,fpjh->jdh", mlp_in, d_pre, preferred_element_type=jnp.float32
        ).astype(low)
        d_mlp_in = jnp.einsum("fpjh,jdh->fpd", d_pre, up_w, preferred_element_type=jnp.float32)
        d_shift_m = jnp.sum(d_mlp_in, axis=(0, 1))
        d_scale_m = jnp.sum(d_mlp_in * normed_m, axis=(0, 1))
        upstream = upstream + normalize_back(d_mlp_in * (1.0 + factors[4]), normed_m, rstd_m)
        d_gate_a = jnp.sum(upstream * branch_a, axis=(0, 1))
        d_branch_a = (factors[2] * upstream).astype(low)
        grad_out = jnp.einsum("fpd,fpje->jde", d_branch_a, mixed, preferred_element_type=jnp.float32)
        d_mixed = jnp.einsum(
            "fpd,jde->fpje", d_branch_a, first_w[:, :, 3 * wide :], preferred_element_type=jnp.float32
        ).astype(low)
        d_mixed = d_mixed.reshape(frames, patches, tps, heads, HD)
        d_parts = attend_back(query, key, value, d_mixed, log_total, forms, scale)
        d_projected = jnp.stack(d_parts, axis=3).astype(low).reshape(frames, patches, tps, 3 * wide)
        grad_qkv = jnp.einsum("fpd,fpje->jde", attn_in, d_projected, preferred_element_type=jnp.float32)
        grads[MATS * level] = jnp.concatenate([grad_qkv, grad_out], axis=2).astype(low)
        d_attn_in = jnp.einsum(
            "fpje,jde->fpd", d_projected, first_w[:, :, : 3 * wide], preferred_element_type=jnp.float32
        )
        d_shift_a = jnp.sum(d_attn_in, axis=(0, 1))
        d_scale_a = jnp.sum(d_attn_in * normed_a, axis=(0, 1))
        upstream = upstream + normalize_back(d_attn_in * (1.0 + factors[1]), normed_a, rstd_a)
        d_mods[level] = jnp.stack([d_shift_a, d_scale_a, d_gate_a, d_shift_m, d_scale_m, d_gate_m])
        if level:
            if level % 2 == 1:
                upstream = patches_back(upstream.astype(low)).astype(jnp.float32)
            else:
                upstream = patches_whole(upstream.astype(low)).astype(jnp.float32)
    input_grad = frames_back(upstream.astype(low)).astype(jnp.float32)

    reduced = sum_grads([grads[m] for m in reversed(range(MATS * layers))])
    reduced = reduced.astype(jnp.float32)

    d_mod = lax.psum(jnp.stack(d_mods)[None], ("ctx", "tp"))
    d_mod_all = lax.all_gather(d_mod, "dp", axis=0, tiled=True)
    d_mod_mine = lax.dynamic_slice_in_dim(d_mod_all, tp_at * wide, wide, 3)
    grad_mod = jnp.einsum("cd,clke->ldke", cond_mine.astype(jnp.float32), d_mod_mine, precision=highest)
    cond_part = jnp.einsum("clke,ldke->cd", d_mod_mine, mod_low.astype(jnp.float32), precision=highest)
    cond_part = lax.all_gather(lax.psum(cond_part, "tp"), "dp", axis=1, tiled=True)
    cond_total = lax.dynamic_slice_in_dim(cond_part, dp_at * conditioning.shape[0], conditioning.shape[0], 0)
    cond_grad = jax.vjp(jax.nn.silu, conditioning)[1](cond_total)[0]

    order = list(reversed(range(MATS * layers)))
    per_level = [
        unpack(*[reduced[order.index(MATS * level + kind)] for kind in range(MATS)], qkv_weight[level])
        for level in range(layers)
    ]
    stacked = [jnp.stack([per_level[level][kind] for level in range(layers)]) for kind in range(4)]
    stacked.append(grad_mod)
    squares = jnp.zeros((), jnp.float32)
    for grad in stacked:
        squares = squares + jnp.sum(grad * grad)
    grad_norm = jnp.sqrt(lax.psum(squares, ("dp", "tp")))
    coef = CLIP_MAX / jnp.maximum(grad_norm, CLIP_MAX)
    updates = [
        adam_update(masters[kind], firsts[kind], seconds[kind], stacked[kind], coef) for kind in range(5)
    ]
    return (output[None], input_grad[None], cond_grad, grad_norm) + tuple(
        updates[kind][part] for part in range(4) for kind in range(5)
    )


def in_memory(array, kind):
    return array.transpose(((0, 2, 1, 3), (0, 1, 2), (0, 1, 2), (0, 2, 1), (0, 2, 1, 3))[kind])


def per_device(mesh_shape, inputs, conditioning, *states):
    if not by_hand(mesh_shape, inputs, states[0]):
        return per_device_plain(mesh_shape, inputs, conditioning, *states)
    states, cotangent = states[:15], states[15]
    states = [in_memory(s, i % 5) for i, s in enumerate(states)]
    masters, firsts, seconds = states[:5], states[5:10], states[10:15]
    dp_at, _, _ = place()
    dps = mesh_shape["dp"]
    frames, strip, width = inputs.shape[1:]
    layers, _, rows, wide = masters[0].shape

    cond_low = jax.nn.silu(conditioning).astype(jnp.bfloat16).astype(jnp.float32)
    cond = jnp.broadcast_to(cond_low.reshape(dps, 1, rows), (dps, 8, rows))
    full, output, cot_rows, *saved, modulation, cond_rows = forward_pass(masters, cond, inputs[0], cotangent[0], mesh_shape)
    reduced, home, d_all, d_cond, norm = backward_pass(
        full, cot_rows, modulation, cond_rows, masters[4], saved, mesh_shape, frames, strip
    )
    updates = update_all(
        reduced, norm, cond_rows[:, 0, :].T, d_all[:, : 6 * layers].transpose(1, 0, 2), masters, firsts, seconds
    )
    updates = [in_memory(u, i % 5) for i, u in enumerate(updates)]
    d_cond = lax.dynamic_slice_in_dim(d_cond, dp_at, 1, 1).reshape(1, dps * rows)
    cond_grad = jax.vjp(jax.nn.silu, conditioning)[1](d_cond)[0]
    input_grad = frames_back(home).astype(jnp.float32)
    output = output.reshape(1, frames, strip, width)
    return (output, input_grad[None], cond_grad, jnp.sqrt(norm[0, 0])) + tuple(updates)


def solution(mesh):
    weights = (
        P(None, "dp", None, "tp"),
        P(None, "tp", "dp"),
        P(None, "dp", "tp"),
        P(None, "tp", "dp"),
        P(None, "dp", None, "tp"),
    )
    rows = P("dp", "ctx", "tp", None)
    return jax.shard_map(
        partial(per_device, dict(mesh.shape)),
        mesh=mesh,
        in_specs=(rows, P("dp", None)) + weights * 3 + (rows,),
        out_specs=(rows, rows, P("dp", None), P()) + weights * 4,
        check_vma=False,
    )
```
